512 devices in a mesh: dp: 8 (over z_hi, x), grid: 64 (over z_lo, y, core).
Axes of the slice: x: 4, y: 4, z: 16 (z_hi: 2, z_lo: 8; z = z_hi * 8 + z_lo), core: 2. Of those that a mesh axis runs over, the one named last changes fastest.
Arguments:
- tokens: bfloat16 [8, 128, 64, 512], P('dp', 'grid'), may hold values from -16 to 16
- grad_out: bfloat16 [8, 128, 64, 512], P('dp', 'grid'), may hold values from -6 to 6
- gain: float32 [512], replicated, may hold values from 0.1 to 1.9
- w_qkv: bfloat16 [512, 1536], P('grid'), as said below
- w_out: bfloat16 [512, 512], P('grid'), may hold values from -0.25 to 0.25
Outputs:
- grad_tokens: bfloat16 [8, 128, 64, 512], P('dp', 'grid')
- grad_qkv: float32 [512, 1536], P('grid')
- grad_wout: float32 [512, 512], P('grid')
- grad_gain: float32 [512], replicated
The draws below stay inside these ranges and needn't reach their ends.
Inputs may be any that keep to these rules, and one draw needn't show every extreme that they name: `w_qkv`: query, key and value projection columns in that order.
All inputs are finite; a program needn't handle non-finite values.
Results may differ from the reference program's by a relative error of at most 0.015.
Values may be sent and summed in bfloat16 or wider, within the bound.
No kernel may reach another device: no remote copies, remote signals or barrier semaphores. Data moves between devices by JAX's collectives and lax.ppermute only.
A program may use at most 64 MiB of HBM per device.

```python
import jax
import jax.numpy as jnp
from jax import lax

D = 512
HEADS = 8
FREQ = 128
FR_DEV = 1
FRAMES = 64
BATCH = 8


def draw_w_qkv(key, part):
    key = jax.random.fold_in(key, 5)
    base = jax.random.normal(key, (D, 3 * D), jnp.float32) * D ** (-0.5)
    return base.astype(jnp.bfloat16)


def with_spikes(values, key, source, target, shards_of, factor):
    owner, partner = [(jnp.arange(values.shape[position]) // (values.shape[position] // shards_of)).reshape([-1 if axis == position else 1 for axis in range(values.ndim)]) for position in (source, target)]
    chosen = jax.random.permutation(key, shards_of)[partner]
    strong = (owner == chosen) | (owner == (partner + shards_of // 2) % shards_of)
    return jnp.where(strong, factor * values, values)


def steps_of(key, dims, cuts, smallest, top_value):
    def one(dim, blocks):
        steps = jax.random.uniform(jax.random.fold_in(jax.random.fold_in(key, 6), dim), (blocks,), jnp.float32, smallest / len(cuts), top_value / len(cuts))
        return jnp.repeat(jnp.exp(steps), dims[dim] // blocks).reshape((-1,) + (1,) * (len(dims) - dim - 1))

    factor_of = one(*cuts[0])
    for cut in cuts[1:]:
        factor_of = factor_of * one(*cut)
    return factor_of


def scatter_about(rng, shape, spread, reach, cuts=(), kind=jnp.bfloat16):
    array = jax.random.normal(rng, shape, jnp.float32) * spread
    if len(cuts) > 0:
        array = steps_of(rng, shape, cuts, -0.22, 0.18) * array
    return jnp.clip(array, min=-reach, max=reach).astype(kind)


def heavy_noise(rng, dims, scale, reach, cuts, heavy, held_as=jnp.bfloat16):
    values = scale * jax.random.normal(rng, dims, jnp.float32)
    if cuts:
        values = values * steps_of(rng, dims, cuts, -0.22, 0.18)
    return jnp.clip(with_spikes(values, jax.random.fold_in(rng, 3), *heavy), -reach, reach).astype(held_as)


def setup_inputs(seed: int = 0) -> dict:
    splits = jax.random.split(jax.random.key(seed), 6)
    return {
        "tokens": heavy_noise(splits[0], (BATCH, FREQ, FRAMES, D), 1.0, 16.0, ((0, 8), (1, 64)), (1, 3, 64, 4.0)),
        "grad_out": scatter_about(splits[1], (BATCH, FREQ, FRAMES, D), 1.0, 6.0, ((0, 8), (1, 64))),
        "gain": jnp.clip(1.0 + 0.18 * jax.random.normal(splits[2], (D,), jnp.float32), 0.1, 1.9),
        "w_qkv": draw_w_qkv(jax.random.fold_in(splits[5], 71), 0),
        "w_out": scatter_about(splits[4], (D, D), D ** -0.5, 0.25, ((0, 64),)),
    }


EPS = 1e-06

def normalize(block_in, gain):
    values = block_in.astype(jnp.float32)
    inverse = lax.rsqrt(lax.optimization_barrier(jnp.mean(values * values, axis=-1, keepdims=True)) + EPS)
    scaled = values * inverse
    normed = (scaled * gain).astype(jnp.bfloat16)
    return (scaled, inverse, normed)

def rounded(values):
    low = lax.optimization_barrier(values.astype(jnp.bfloat16))
    return low.astype(jnp.float32)

def attend_backward(queries, keys, values, upstream, heads):
    freq, frames, width = queries.shape
    size = width // heads
    scale = size ** (-0.5)

    def split(arr):
        return arr.astype(jnp.float32).reshape(freq, frames, heads, size)
    q32, k32, v32, d32 = (split(queries), split(keys), split(values), split(upstream))
    scores = jnp.einsum('fnhd,gnhd->nhfg', q32, k32) * scale
    top = lax.optimization_barrier(jnp.max(scores, axis=-1, keepdims=True))
    expo = jnp.exp(scores - top)
    probs = expo / lax.optimization_barrier(jnp.sum(expo, axis=-1, keepdims=True))
    weights = rounded(probs)
    attended = jnp.einsum('nhfg,gnhd->fnhd', weights, v32)
    dprob = jnp.einsum('fnhd,gnhd->nhfg', d32, v32)
    dvals = jnp.einsum('nhfg,fnhd->gnhd', weights, d32)
    dscore = rounded(probs * (dprob - lax.optimization_barrier(jnp.sum(probs * dprob, axis=-1, keepdims=True))) * scale)
    dquery = jnp.einsum('nhfg,gnhd->fnhd', dscore, k32)
    dkey = jnp.einsum('nhfg,fnhd->gnhd', dscore, q32)

    def join(arr):
        return arr.reshape(freq, frames, width).astype(jnp.bfloat16)
    return (join(attended), join(dquery), join(dkey), join(dvals))

def block_backward(block_in, block_grad, gain, w_qkv, w_out):
    freq, frames, width = block_in.shape
    scaled, inverse, normed = normalize(block_in, gain)
    flat = normed.reshape(-1, width)
    qkv = jnp.dot(flat, w_qkv, preferred_element_type=jnp.float32).astype(jnp.bfloat16)
    qkv = qkv.reshape(freq, frames, 3 * width)
    grad_rows = block_grad.reshape(-1, width)
    upstream = lax.dot_general(grad_rows, w_out, (((1,), (1,)), ((), ())), preferred_element_type=jnp.float32)
    upstream = upstream.astype(jnp.bfloat16).reshape(freq, frames, width)
    attended, dquery, dkey, dvals = attend_backward(qkv[..., :width], qkv[..., width:2 * width], qkv[..., 2 * width:], upstream, HEADS)
    dqkv = jnp.concatenate([dquery, dkey, dvals], axis=-1).reshape(-1, 3 * width)
    grad_wout = lax.dot_general(attended.reshape(-1, width), grad_rows, (((0,), (0,)), ((), ())), preferred_element_type=jnp.float32)
    grad_qkv = lax.dot_general(flat, dqkv, (((0,), (0,)), ((), ())), preferred_element_type=jnp.float32)
    dnormed = lax.dot_general(dqkv, w_qkv, (((1,), (1,)), ((), ())), preferred_element_type=jnp.float32)
    scaled_rows = scaled.reshape(-1, width)
    inverse_rows = inverse.reshape(-1, 1)
    grad_gain = lax.optimization_barrier(jnp.sum(dnormed * scaled_rows, axis=0))
    dscaled = dnormed * gain
    result = grad_rows.astype(jnp.float32) + inverse_rows * (dscaled - scaled_rows * lax.optimization_barrier(jnp.mean(dscaled * scaled_rows, axis=-1, keepdims=True)))
    return (result.astype(jnp.bfloat16).reshape(freq, frames, width), grad_qkv, grad_wout, grad_gain)

def reference(tokens, grad_out, gain, w_qkv, w_out):
    batch, freq, frames, width = tokens.shape
    blocks = frames // FR_DEV

    def step(carry, index):
        which = (index // blocks).astype(jnp.int32)
        start = (index % blocks * FR_DEV).astype(jnp.int32)
        zero = jnp.int32(0)
        block_in = lax.dynamic_slice(tokens, (which, zero, start, zero), (1, freq, FR_DEV, width))[0]
        block_grad = lax.dynamic_slice(grad_out, (which, zero, start, zero), (1, freq, FR_DEV, width))[0]
        result, grad_qkv, grad_wout, grad_gain = block_backward(block_in, block_grad, gain, w_qkv, w_out)
        return ((carry[0] + grad_qkv, carry[1] + grad_wout, carry[2] + grad_gain), result)
    init = (jnp.zeros((width, 3 * width), jnp.float32), jnp.zeros((width, width), jnp.float32), jnp.zeros((width,), jnp.float32))
    sums, pieces = lax.scan(step, init, jnp.arange(batch * blocks, dtype=jnp.int32))
    grad_tokens = pieces.reshape(batch, blocks, freq, FR_DEV, width).transpose(0, 2, 1, 3, 4).reshape(batch, freq, frames, width)
    return (grad_tokens, sums[0], sums[1], sums[2])
```

```python
import jax
import jax.numpy as jnp
from jax import lax
from jax.sharding import Mesh
from jax.sharding import PartitionSpec as P

HEADS = 8
EPS = 1e-06
BF = jnp.bfloat16
F32 = jnp.float32

ZH, X, ZL, Y, C = 2, 4, 8, 4, 2
ND = ZL * Y
SWAP = [(0, 1), (1, 0)]


def share(block, axes, count):
    wide = jnp.broadcast_to(block[None], (count,) + block.shape)
    return lax.all_to_all(wide, axes, split_axis=0, concat_axis=0, tiled=True)


def gather_weights(w_qkv, w_out, core):
    halves = w_qkv.reshape(8, 3, 2, 256)
    mine = lax.dynamic_index_in_dim(halves, core, 2, keepdims=False).reshape(8, 768)
    other = lax.dynamic_index_in_dim(halves, 1 - core, 2, keepdims=False).reshape(8, 768)
    sent = jnp.concatenate([other, w_out], axis=1)
    got = lax.ppermute(sent, "c", SWAP)
    kept = jnp.concatenate([mine, w_out], axis=1)
    first = jnp.where(core == 0, kept, got)
    second = jnp.where(core == 0, got, kept)
    rows = jnp.concatenate([first, second], axis=0)
    plane = share(rows, "zl", ZL)
    out_part = lax.dynamic_slice_in_dim(plane[:, :, 768:], core * 4, 4, 0)
    out_part = out_part.reshape(4, 16, 2, 256).transpose(2, 0, 1, 3).reshape(8, 16, 256)
    block = jnp.concatenate([plane[:, :, :768], out_part], axis=2)
    full = share(block, "y", Y)
    wh = full[..., :768].transpose(1, 0, 2, 3).reshape(512, 768)
    wo = full[..., 768:].reshape(Y, 2, 4, 16, 256).transpose(2, 0, 3, 1, 4).reshape(256, 512)
    return wh, wo


def normalize(tokens, gain):
    values = tokens.astype(F32)
    inverse = lax.rsqrt(jnp.mean(values * values, axis=-1, keepdims=True) + EPS)
    scaled = values * inverse
    return scaled, inverse, (scaled * gain).astype(BF)


def attend(qkv, ups):
    q, k, v = (qkv[..., i * 256 : (i + 1) * 256].reshape(2, 128, 4, 64) for i in range(3))
    u = ups.reshape(2, 128, 4, 64)
    scale = 64 ** (-0.5)
    scores = jnp.einsum("nfhd,nghd->nhfg", q, k, preferred_element_type=F32) * scale
    top = jnp.max(scores, axis=-1, keepdims=True)
    expo = jnp.exp(scores - top)
    probs = expo / jnp.sum(expo, axis=-1, keepdims=True)
    weights = probs.astype(BF)
    att = jnp.einsum("nhfg,nghd->nfhd", weights, v, preferred_element_type=F32)
    dprob = jnp.einsum("nfhd,nghd->nhfg", u, v, preferred_element_type=F32)
    dv = jnp.einsum("nhfg,nfhd->nghd", weights, u, preferred_element_type=F32)
    ds = (probs * (dprob - jnp.sum(probs * dprob, axis=-1, keepdims=True)) * scale).astype(BF)
    dq = jnp.einsum("nhfg,nghd->nfhd", ds, k, preferred_element_type=F32)
    dk = jnp.einsum("nhfg,nfhd->nghd", ds, q, preferred_element_type=F32)

    def join(arr):
        return arr.reshape(2, 128, 256).astype(BF)

    return join(att), jnp.concatenate([join(dq), join(dk), join(dv)], axis=-1)


def on_device(tokens, grad_out, gain, w_qkv, w_out):
    core = lax.axis_index("c")
    third = lax.axis_index("x") == 3

    both = jnp.stack([tokens[0], grad_out[0]])
    both = both.reshape(2, 2, 2, ND, 512).transpose(3, 0, 2, 1, 4)
    moved = lax.all_to_all(
        both.reshape(ND, 8, 512), ("zl", "y"), split_axis=0, concat_axis=0, tiled=True
    )
    far = lax.ppermute(moved, "c", SWAP)

    def rows_of(arr):
        return arr.reshape(ND, 2, 2, 2, 512).transpose(1, 2, 0, 3, 4).reshape(2, 2, 64, 512)

    pair = jnp.concatenate([rows_of(moved), rows_of(far)], axis=2)
    x_in, g_in = pair[0], pair[1]

    wh, wo = gather_weights(w_qkv, w_out, core)

    scaled, inverse, normed = normalize(x_in, gain)
    flat = normed.reshape(256, 512)
    grows = g_in.reshape(256, 512)
    qkv = jnp.dot(flat, wh, preferred_element_type=F32).astype(BF)
    ups = lax.dot_general(grows, wo, (((1,), (1,)), ((), ())), preferred_element_type=F32)
    ups = ups.astype(BF)
    att, dqkv = attend(qkv.reshape(2, 128, 768), ups.reshape(2, 128, 256))
    att, dqkv = att.reshape(256, 256), dqkv.reshape(256, 768)

    over = (((0,), (0,)), ((), ()))
    g_wout = lax.dot_general(att, grows, over, preferred_element_type=F32).astype(BF)
    g_qkv = lax.dot_general(flat, dqkv, over, preferred_element_type=F32).astype(BF)
    dn = lax.dot_general(dqkv, wh, (((1,), (1,)), ((), ())), preferred_element_type=F32)
    dn = dn.reshape(2, 128, 512)

    q_part = g_qkv.reshape(ND, 2, 8, 3, 256).transpose(3, 1, 0, 2, 4).reshape(3, 2, 256, 256)
    o_part = g_wout.reshape(16, 2, 8, 2, 256).transpose(1, 3, 0, 2, 4).reshape(1, 2, 256, 256)
    parts = jnp.concatenate([q_part, o_part], axis=0).reshape(8, 256, 256)
    got = lax.all_to_all(parts, ("x", "c"), split_axis=0, concat_axis=0, tiled=True)
    part = jnp.sum(got.reshape(X, C, 256, 256).astype(F32), axis=0).astype(BF)
    as_cols = jnp.concatenate([part[0], part[1]], axis=1)
    as_rows = part.reshape(2, 2, 128, 256).transpose(0, 2, 1, 3).reshape(256, 512)
    part = jnp.where(third, as_rows, as_cols)

    dn_far = lax.ppermute(dn[:, 64:].astype(BF), "c", SWAP)
    dn_own = dn[:, :64] + dn_far.astype(F32)
    s_own, i_own, g_own = scaled[:, :64], inverse[:, :64], g_in[:, :64].astype(F32)
    gg = jnp.sum(dn_own * s_own, axis=(0, 1))
    dscaled = dn_own * gain
    result = g_own + i_own * (
        dscaled - s_own * jnp.mean(dscaled * s_own, axis=-1, keepdims=True)
    )
    result = result.astype(BF)
    gg = gg + lax.ppermute(gg, "c", SWAP)

    def split(vec):
        high = vec.astype(BF)
        low = (vec - high.astype(F32)).astype(BF)
        return jnp.concatenate([high, low])

    out_rows = result.reshape(2, ND, 2, 512).transpose(1, 0, 2, 3).reshape(ND, 2048)
    gain_rows = jnp.broadcast_to(split(gg)[None], (ND, 1024))
    sent = jnp.concatenate([part.reshape(ND, 4096), out_rows, gain_rows], axis=1)
    back = lax.all_to_all(
        sent.reshape(ND, 7, 1024), ("zl", "y"), split_axis=0, concat_axis=0, tiled=True
    ).reshape(ND, 7168)
    grads = jnp.sum(back[:, :4096].astype(F32), axis=0).astype(BF)
    gg = jnp.sum(back[:, 6144:].reshape(ND, 2, 512).astype(F32), axis=(0, 1))
    grad_tokens = (
        back[:, 4096:6144].reshape(ND, 2, 2, 512).transpose(2, 1, 0, 3).reshape(1, 2, 64, 512)
    )

    last = jnp.concatenate([grads, split(gg)])
    all_dp = share(last.reshape(10, 512), ("zh", "x"), ZH * X).astype(F32)
    sums = jnp.sum(all_dp[:, :8].reshape(ZH, X, 8, 512), axis=0)
    shard_qkv = jnp.concatenate([sums[0], sums[1], sums[2]], axis=1)
    shard_wout = sums[3]
    total_gain = jnp.sum(all_dp[:, 8:], axis=(0, 1))
    return grad_tokens, shard_qkv, shard_wout, total_gain


def solution(mesh):
    inner = Mesh(mesh.devices.reshape(ZH, X, ZL, Y, C), ("zh", "x", "zl", "y", "c"))
    grid = ("zl", "y", "c")
    tok = P(("zh", "x"), grid, None, None)
    return jax.shard_map(
        on_device,
        mesh=inner,
        in_specs=(tok, tok, P(), P(grid, None), P(grid, None)),
        out_specs=(tok, P(grid, None), P(grid, None), P()),
        check_vma=False,
    )
```

```python
import jax
import jax.numpy as jnp
from jax import lax
from jax.experimental import pallas as pl
from jax.experimental.pallas import tpu as pltpu
from jax.sharding import Mesh
from jax.sharding import PartitionSpec as P

EPS = 1e-06
BF = jnp.bfloat16
F32 = jnp.float32

ZH, X, ZL, Y, C = 2, 4, 8, 4, 2
ND = ZL * Y
SWAP = [(0, 1), (1, 0)]
PLANE = ("zl", "y")


def flip(arr, axis, count, bits):
    return lax.ppermute(arr, axis, [(i, i ^ bits) for i in range(count)])


def share(block, axes, count):
    wide = jnp.broadcast_to(block[None], (count,) + block.shape)
    return lax.all_to_all(wide, axes, split_axis=0, concat_axis=0, tiled=True)


def call(body, outs, *args, scratch=(), smem=0):
    specs = [pl.BlockSpec(memory_space=pltpu.SMEM)] * smem
    specs += [pl.BlockSpec(memory_space=pltpu.VMEM)] * (len(args) - smem)
    return pl.pallas_call(
        body,
        out_shape=[jax.ShapeDtypeStruct(shape, kind) for shape, kind in outs],
        in_specs=specs,
        out_specs=[pl.BlockSpec(memory_space=pltpu.VMEM)] * len(outs),
        scratch_shapes=list(scratch),
        compiler_params=pltpu.CompilerParams(vmem_limit_bytes=40 * 2**20),
    )(*args)


def dot(a, b, ca=1, cb=0):
    return lax.dot_general(a, b, (((ca,), (cb,)), ((), ())), preferred_element_type=F32)


def chooser(rows, cols, source_of):
    row = lax.broadcasted_iota(jnp.int32, (rows, cols), 0)
    col = lax.broadcasted_iota(jnp.int32, (rows, cols), 1)
    return (col == source_of(row)).astype(F32).astype(BF)


def mover(rows, cols, target_of):
    return chooser(rows, cols, target_of)


def pack_body(tok_ref, grad_ref, out_ref):
    both = jnp.concatenate([tok_ref[...], grad_ref[...]], axis=0)
    pick = chooser(
        256, 256, lambda i: (i >> 2 & 1) * 128 + (i & 1) * 64 + (i >> 1 & 1) * 32 + (i >> 3)
    )
    out_ref[...] = dot(pick, both).astype(BF)


def main_body(
    where_ref, own_ref, far_ref, blk_ref, pa_ref, pb_ref, pc_ref, pd_ref, gain_ref,
    parts_ref, send_ref, keep_ref, mine_ref, wh_ref, wo_ref,
):
    zl, y = where_ref[0], where_ref[1]

    def place(ref, jy, jz, at):
        row = pl.multiple_of(((zl ^ jz) * Y + (y ^ jy)) * 16, 16)
        wh_ref[pl.ds(row, 16), :] = ref[at : at + 16, :768]
        low = pl.multiple_of((((zl & 3) ^ (jz & 3)) * Y + (y ^ jy)) * 16, 16)
        half = (jz >> 2) * 256
        wo_ref[pl.ds(low, 16), half : half + 256] = ref[at : at + 16, 768:]

    for jz in range(8):
        place(blk_ref, 0, jz, jz * 16)
        place(pa_ref, 1, jz, jz * 16)
        place(pb_ref, 3, jz, jz * 16)
        if jz < 4:
            place(pc_ref, 2, jz, jz * 16)
        else:
            place(pd_ref, 2, jz, jz * 16 - 64)

    pick = chooser(
        256, 256, lambda i: (i >> 1 & 31) * 8 + (i >> 7) * 4 + (i >> 6 & 1) * 2 + (i & 1)
    )
    own = dot(pick, own_ref[...]).astype(BF)
    far = dot(pick, far_ref[...]).astype(BF)
    mine_ref[...] = own
    x_in = jnp.concatenate([own[0:64], far[0:64], own[64:128], far[64:128]], axis=0)
    g_in = jnp.concatenate([own[128:192], far[128:192], own[192:], far[192:]], axis=0)

    values = x_in.astype(F32)
    inverse = lax.rsqrt(jnp.mean(values * values, axis=-1, keepdims=True) + EPS)
    normed = (values * inverse * gain_ref[...]).astype(BF)
    wh = wh_ref[...]
    qkv = dot(normed, wh).astype(BF)
    ups = dot(g_in, wo_ref[...], 1, 1).astype(BF)

    lane = lax.broadcasted_iota(jnp.int32, (128, 128), 1)
    first = lane < 64
    zero = jnp.zeros((128, 128), BF)

    def stack(arr):
        return jnp.concatenate([jnp.where(first, arr, zero), jnp.where(first, zero, arr)], axis=0)

    def pile(arr):
        return jnp.concatenate([arr[:, :128], arr[:, 128:]], axis=0)

    atts, dqs, dks, dvs = [], [], [], []
    for f in range(2):
        rows = slice(f * 128, (f + 1) * 128)
        for pair in range(2):
            at = pair * 128
            q = qkv[rows, at : at + 128]
            k2 = stack(qkv[rows, 256 + at : 256 + at + 128])
            v2 = stack(qkv[rows, 512 + at : 512 + at + 128])
            u = ups[rows, at : at + 128]
            scores = dot(q, k2, 1, 1) * 0.125
            dprob = dot(u, v2, 1, 1)
            weights, dscores = [], []
            for head in range(2):
                cols = slice(head * 128, (head + 1) * 128)
                s = scores[:, cols]
                expo = jnp.exp(s - jnp.max(s, axis=-1, keepdims=True))
                probs = expo * (1.0 / jnp.sum(expo, axis=-1, keepdims=True))
                dp = dprob[:, cols]
                weights.append(probs.astype(BF))
                inner = jnp.sum(probs * dp, axis=-1, keepdims=True)
                dscores.append((probs * (dp - inner) * 0.125).astype(BF))
            weight = jnp.concatenate(weights, axis=1)
            dscore = jnp.concatenate(dscores, axis=1)
            atts.append(dot(weight, v2).astype(BF))
            dqs.append(dot(dscore, k2).astype(BF))
            dks.append(dot(pile(dscore), stack(q), 0, 0).astype(BF))
            dvs.append(dot(pile(weight), stack(u), 0, 0).astype(BF))

    def frames(items):
        return [
            jnp.concatenate([items[0], items[2]], axis=0),
            jnp.concatenate([items[1], items[3]], axis=0),
        ]

    att = jnp.concatenate(frames(atts), axis=1)
    dqkv = jnp.concatenate(frames(dqs) + frames(dks) + frames(dvs), axis=1)

    dn = dot(dqkv, wh, 1, 1)
    keep_ref[...] = jnp.concatenate([dn[0:64], dn[128:192]], axis=0)
    send_ref[...] = jnp.concatenate([dn[64:128], dn[192:]], axis=0).astype(BF)

    shuffle = mover(
        512, 512, lambda i: (i >> 1 & 3) * 128 + (i >> 3 & 1) * 64 + (i >> 4) * 2 + (i & 1)
    )
    flat = dot(normed, shuffle).astype(BF)
    g_qkv = dot(flat, dqkv, 0, 0).astype(BF)
    shuffle = mover(
        256, 256, lambda i: (i >> 1 & 3) * 64 + (i >> 3 & 1) * 32 + (i >> 4) * 2 + (i & 1)
    )
    att = dot(att, shuffle).astype(BF)
    g_out = dot(att, g_in, 0, 0).astype(BF)
    for yc in range(8):
        for part in range(3):
            parts_ref[part * 8 + yc] = g_qkv[yc * 64 : yc * 64 + 64, part * 256 : part * 256 + 256]
        block = g_out[yc * 32 : yc * 32 + 32]
        parts_ref[24 + yc] = jnp.concatenate([block[:, :256], block[:, 256:]], axis=0)


def finish_body(mine_ref, keep_ref, far_ref, gain_ref, out_ref, gg_ref):
    gain = gain_ref[...]
    values = mine_ref[0:128, :].astype(F32)
    inverse = lax.rsqrt(jnp.mean(values * values, axis=-1, keepdims=True) + EPS)
    scaled = values * inverse
    dn = keep_ref[...] + far_ref[...].astype(F32)
    gg_ref[...] = jnp.sum(dn * scaled, axis=0, keepdims=True)
    ds = dn * gain
    inner = jnp.mean(ds * scaled, axis=-1, keepdims=True)
    out_ref[...] = (mine_ref[128:256, :].astype(F32) + inverse * (ds - scaled * inner)).astype(BF)


def two_rows(vec):
    high = vec.astype(BF).astype(F32)
    return jnp.concatenate([high, vec - high, jnp.zeros((6, vec.shape[1]), F32)], axis=0)


def merge_body(where_ref, got_ref, rows_ref, gg_ref, far_ref, out_ref):
    total = got_ref[0:2].astype(F32)
    for i in range(1, 16):
        total = total + got_ref[2 * i : 2 * i + 2].astype(F32)
    low, high = total[0], total[1]
    cols = jnp.concatenate([low, high], axis=1)
    rows = jnp.concatenate(
        [
            jnp.concatenate([low[:32], low[32:]], axis=1),
            jnp.concatenate([high[:32], high[32:]], axis=1),
        ],
        axis=0,
    )
    grads = jnp.where(where_ref[2] == 3, rows, cols).astype(BF)
    gains = two_rows(gg_ref[...] + far_ref[...])
    gains = jnp.concatenate([gains, jnp.zeros((56, 512), F32)], axis=0).astype(BF)
    every = jnp.concatenate([grads, gains, rows_ref[...]], axis=0)

    def source(i):
        d, k = i >> 3, i & 7
        token = 128 + (k >> 1 & 1) * 64 + d * 2 + (k & 1)
        return jnp.where(k < 4, token, jnp.where(k < 6, d * 2 + (k & 1), 64 + (k & 1)))

    out_ref[...] = dot(chooser(256, 256, source), every).astype(BF)


def split_body(back_ref, tokens_ref, last_ref):
    back = back_ref[...]
    pick = chooser(
        128, 256, lambda i: (i & 31) * 8 + (i >> 5 & 1) * 2 + (i >> 6)
    )
    tokens_ref[...] = dot(pick, back).astype(BF)
    row = lax.broadcasted_iota(jnp.int32, (16, 256), 0)
    col = lax.broadcasted_iota(jnp.int32, (16, 256), 1)
    kind = col & 7
    grads = (row < 8) & (kind == 4 + (row & 1)) & ((col >> 3 & 3) == row >> 1)
    gains = (row == 8) & (kind >= 6)
    sums = dot((grads | gains).astype(F32).astype(BF), back)
    last_ref[...] = jnp.concatenate([sums[0:8], two_rows(sums[8:9])], axis=0).astype(BF)


def end_body(got_ref, qkv_ref, out_ref, gain_ref):
    for x in range(X):
        pair = got_ref[x].astype(F32) + got_ref[X + x].astype(F32)
        if x < 3:
            qkv_ref[:, x * 512 : x * 512 + 512] = pair[0:8]
        else:
            out_ref[...] = pair[0:8]
        gain = jnp.sum(pair[8:16], axis=0, keepdims=True)
        total = gain if x == 0 else total + gain
    gain_ref[...] = total


def gather_weights(w_qkv, w_out, core, zl):
    halves = w_qkv.reshape(8, 3, 2, 256)
    mine = lax.dynamic_index_in_dim(halves, core, 2, keepdims=False).reshape(8, 768)
    other = lax.dynamic_index_in_dim(halves, 1 - core, 2, keepdims=False).reshape(8, 768)
    got = lax.ppermute(jnp.concatenate([other, w_out], axis=1), "c", SWAP)
    kept = jnp.concatenate([mine, w_out], axis=1)
    first = jnp.where(core == 0, kept, got)
    second = jnp.where(core == 0, got, kept)
    cur = jnp.concatenate([first, second], axis=0)
    for bits in (1, 2, 4):
        cur = jnp.concatenate([cur, flip(cur, "zl", ZL, bits)], axis=0)
    side = (core ^ (zl >> 2)) * 64
    outs = lax.dynamic_slice_in_dim(cur[:, 768:], side, 64, 0)
    outs = jnp.concatenate([outs[:, :256], outs[:, 256:]], axis=0)
    block = jnp.concatenate([cur[:, :768], outs], axis=1)
    pa = flip(block, "y", Y, 1)
    pb = flip(block, "y", Y, 3)
    pc = flip(pb[:64], "y", Y, 1)
    pd = flip(pa[64:], "y", Y, 3)
    return block, pa, pb, pc, pd


def on_device(tokens, grad_out, gain, w_qkv, w_out):
    core, zl, y, x = (lax.axis_index(a) for a in ("c", "zl", "y", "x"))
    where = jnp.stack([zl, y, x, core]).astype(jnp.int32)
    row = gain.reshape(1, 512)

    [packed] = call(
        pack_body, [((256, 512), BF)], tokens.reshape(128, 512), grad_out.reshape(128, 512)
    )
    moved = lax.all_to_all(
        packed.reshape(ND, 8, 512), PLANE, split_axis=0, concat_axis=0, tiled=True
    )
    pieces = gather_weights(w_qkv, w_out, core, zl)
    moved = moved.reshape(256, 512)
    far = lax.ppermute(moved, "c", SWAP)
    parts, send, keep, mine = call(
        main_body,
        [((32, 64, 256), BF), ((128, 512), BF), ((128, 512), F32), ((256, 512), BF)],
        where, moved, far, *pieces, row,
        scratch=[pltpu.VMEM((512, 768), BF), pltpu.VMEM((256, 512), BF)],
        smem=1,
    )
    got = lax.all_to_all(parts, ("x", "y", "c"), split_axis=0, concat_axis=0, tiled=True)
    dn_far = lax.ppermute(send, "c", SWAP)
    rows, gg = call(
        finish_body, [((128, 512), BF), ((1, 512), F32)], mine, keep, dn_far, row
    )
    gg_far = lax.ppermute(gg, "c", SWAP)
    [sent] = call(merge_body, [((256, 512), BF)], where, got, rows, gg, gg_far, smem=1)
    back = lax.all_to_all(
        sent.reshape(ND, 8, 512), PLANE, split_axis=0, concat_axis=0, tiled=True
    )
    grad_tokens, last = call(
        split_body, [((128, 512), BF), ((16, 512), BF)], back.reshape(256, 512)
    )
    ends = share(last, ("zh", "x"), ZH * X)
    shard_qkv, shard_out, total = call(
        end_body, [((8, 1536), F32), ((8, 512), F32), ((1, 512), F32)], ends
    )
    return grad_tokens.reshape(1, 2, 64, 512), shard_qkv, shard_out, total.reshape(512)


def solution(mesh):
    inner = Mesh(mesh.devices.reshape(ZH, X, ZL, Y, C), ("zh", "x", "zl", "y", "c"))
    grid = ("zl", "y", "c")
    tok = P(("zh", "x"), grid, None, None)
    return jax.shard_map(
        on_device,
        mesh=inner,
        in_specs=(tok, tok, P(), P(grid, None), P(grid, None)),
        out_specs=(tok, P(grid, None), P(grid, None), P()),
        check_vma=False,
    )
```

```python
import jax
import jax.numpy as jnp
from jax import lax
from jax.experimental import pallas as pl
from jax.experimental.pallas import tpu as pltpu
from jax.sharding import Mesh
from jax.sharding import PartitionSpec as P

EPS = 1e-06
BF = jnp.bfloat16
F32 = jnp.float32

ZH, X, ZL, Y, C = 2, 4, 8, 4, 2
ND = ZL * Y
SWAP = [(0, 1), (1, 0)]
PLANE = ("zl", "y")


def exchange(arr, axes):
    return lax.all_to_all(arr, axes, split_axis=0, concat_axis=0, tiled=True)


def call(body, outs, *args, scratch=(), smem=0):
    specs = [pl.BlockSpec(memory_space=pltpu.SMEM)] * smem
    specs += [pl.BlockSpec(memory_space=pltpu.VMEM)] * (len(args) - smem)
    return pl.pallas_call(
        body,
        out_shape=[jax.ShapeDtypeStruct(shape, kind) for shape, kind in outs],
        in_specs=specs,
        out_specs=[pl.BlockSpec(memory_space=pltpu.VMEM)] * len(outs),
        scratch_shapes=list(scratch),
        compiler_params=pltpu.CompilerParams(vmem_limit_bytes=40 * 2**20),
    )(*args)


def dot(a, b, ca=1, cb=0):
    return lax.dot_general(a, b, (((ca,), (cb,)), ((), ())), preferred_element_type=F32)


def chooser(rows, cols, source_of):
    row = lax.broadcasted_iota(jnp.int32, (rows, cols), 0)
    col = lax.broadcasted_iota(jnp.int32, (rows, cols), 1)
    return (col == source_of(row)).astype(F32).astype(BF)


def mover(rows, cols, target_of):
    return chooser(rows, cols, target_of)


def pack_body(where_ref, tok_ref, grad_ref, wq_ref, wo_ref, out_ref):
    both = jnp.concatenate([tok_ref[...], grad_ref[...]], axis=0)
    pick = chooser(
        256, 256, lambda i: (i >> 2 & 1) * 128 + (i & 1) * 64 + (i >> 1 & 1) * 32 + (i >> 3)
    )
    out_ref[:, :512] = dot(pick, both).astype(BF)
    x = where_ref[0]
    part = wo_ref[...].astype(F32)
    for i in range(3):
        part = jnp.where(x == i, wq_ref[:, i * 512 : i * 512 + 512].astype(F32), part)
    blocks = jnp.concatenate([part[:, y * 128 : y * 128 + 128] for y in range(Y)], axis=0)
    out_ref[:, 512:] = jnp.concatenate([blocks] * ZL, axis=0).astype(BF)


def halves(arr):
    return arr[:, :64], arr[:, 64:]


def weights_body(where_ref, moved_ref, sent_ref, tok_ref):
    tok_ref[...] = moved_ref[:, :512]
    block = moved_ref[:, 512:].astype(F32)
    (low0, low1), (high0, high1) = halves(block[:128]), halves(block[128:])
    planes = block.reshape(4, 2, 32, 128)
    outs = x_is_last(where_ref)
    for core, cols in ((0, (low0, high0)), (1, (low1, high1))):
        mine = jnp.where(
            outs, planes[:, core].reshape(128, 128), jnp.concatenate(cols, axis=1)
        ).astype(BF)
        for xy in range(X * Y):
            sent_ref[2 * xy + core] = mine


def x_is_last(where_ref):
    return where_ref[0] == 3


def weave(first, second):
    rows, cols = first.shape
    blocks = [arr.reshape(rows // 8, 1, 8, cols) for arr in (first, second)]
    return jnp.concatenate(blocks, axis=1).reshape(2 * rows, cols)


def main_body(
    tok_ref, far_ref, w_ref, gain_ref, parts_ref, send_ref, keep_ref, mine_ref
):
    lanes = []
    for x in range(3):
        for pair in range(2):
            tops, bots = [], []
            for core in range(2):
                at = x * 8 + pair * 4 + core
                (a0, a1), (b0, b1) = (
                    halves(w_ref[at].astype(F32)),
                    halves(w_ref[at + 2].astype(F32)),
                )
                tops.append(jnp.concatenate([a0, b0], axis=1))
                bots.append(jnp.concatenate([a1, b1], axis=1))
            lanes.append(jnp.concatenate([weave(*tops), weave(*bots)], axis=0).astype(BF))
    wh = jnp.concatenate(lanes, axis=1)
    lanes = [
        weave(w_ref[24 + 2 * y].astype(F32), w_ref[25 + 2 * y].astype(F32)).astype(BF)
        for y in range(Y)
    ]
    wo = jnp.concatenate(lanes, axis=1)

    pick = chooser(
        256, 256, lambda i: (i >> 1 & 31) * 8 + (i >> 7) * 4 + (i >> 6 & 1) * 2 + (i & 1)
    )
    own = dot(pick, tok_ref[...]).astype(BF)
    far = dot(pick, far_ref[...]).astype(BF)
    mine_ref[...] = own
    x_in = jnp.concatenate([own[0:64], far[0:64], own[64:128], far[64:128]], axis=0)
    g_in = jnp.concatenate([own[128:192], far[128:192], own[192:], far[192:]], axis=0)

    values = x_in.astype(F32)
    inverse = lax.rsqrt(jnp.mean(values * values, axis=-1, keepdims=True) + EPS)
    normed = (values * inverse * gain_ref[...]).astype(BF)
    qkv = dot(normed, wh).astype(BF)
    ups = dot(g_in, wo, 1, 1).astype(BF)

    lane = lax.broadcasted_iota(jnp.int32, (128, 128), 1)
    first = lane < 64
    zero = jnp.zeros((128, 128), BF)

    def stack(arr):
        return jnp.concatenate([jnp.where(first, arr, zero), jnp.where(first, zero, arr)], axis=0)

    def pile(arr):
        return jnp.concatenate([arr[:, :128], arr[:, 128:]], axis=0)

    atts, dqs, dks, dvs = [], [], [], []
    for f in range(2):
        rows = slice(f * 128, (f + 1) * 128)
        for pair in range(2):
            at = pair * 128
            q = qkv[rows, at : at + 128]
            k2 = stack(qkv[rows, 256 + at : 256 + at + 128])
            v2 = stack(qkv[rows, 512 + at : 512 + at + 128])
            u = ups[rows, at : at + 128]
            scores = dot(q, k2, 1, 1) * 0.125
            dprob = dot(u, v2, 1, 1)
            weights, dscores = [], []
            for head in range(2):
                cols = slice(head * 128, (head + 1) * 128)
                s = scores[:, cols]
                expo = jnp.exp(s - jnp.max(s, axis=-1, keepdims=True))
                probs = expo * (1.0 / jnp.sum(expo, axis=-1, keepdims=True))
                dp = dprob[:, cols]
                weights.append(probs.astype(BF))
                inner = jnp.sum(probs * dp, axis=-1, keepdims=True)
                dscores.append((probs * (dp - inner) * 0.125).astype(BF))
            weight = jnp.concatenate(weights, axis=1)
            dscore = jnp.concatenate(dscores, axis=1)
            atts.append(dot(weight, v2).astype(BF))
            dqs.append(dot(dscore, k2).astype(BF))
            dks.append(dot(pile(dscore), stack(q), 0, 0).astype(BF))
            dvs.append(dot(pile(weight), stack(u), 0, 0).astype(BF))

    def frames(items):
        return [
            jnp.concatenate([items[0], items[2]], axis=0),
            jnp.concatenate([items[1], items[3]], axis=0),
        ]

    att = jnp.concatenate(frames(atts), axis=1)
    dqkv = jnp.concatenate(frames(dqs) + frames(dks) + frames(dvs), axis=1)

    dn = dot(dqkv, wh, 1, 1)
    keep_ref[...] = jnp.concatenate([dn[0:64], dn[128:192]], axis=0)
    send_ref[...] = jnp.concatenate([dn[64:128], dn[192:]], axis=0).astype(BF)

    shuffle = mover(
        512, 512, lambda i: (i >> 1 & 3) * 128 + (i >> 3 & 1) * 64 + (i >> 4) * 2 + (i & 1)
    )
    flat = dot(normed, shuffle).astype(BF)
    g_qkv = dot(flat, dqkv, 0, 0).astype(BF)
    shuffle = mover(
        256, 256, lambda i: (i >> 1 & 3) * 64 + (i >> 3 & 1) * 32 + (i >> 4) * 2 + (i & 1)
    )
    att = dot(att, shuffle).astype(BF)
    g_out = dot(att, g_in, 0, 0).astype(BF)
    for yc in range(8):
        for part in range(3):
            parts_ref[part * 8 + yc] = g_qkv[yc * 64 : yc * 64 + 64, part * 256 : part * 256 + 256]
        block = g_out[yc * 32 : yc * 32 + 32]
        parts_ref[24 + yc] = jnp.concatenate([block[:, :256], block[:, 256:]], axis=0)


def finish_body(mine_ref, keep_ref, far_ref, gain_ref, out_ref, gg_ref):
    gain = gain_ref[...]
    values = mine_ref[0:128, :].astype(F32)
    inverse = lax.rsqrt(jnp.mean(values * values, axis=-1, keepdims=True) + EPS)
    scaled = values * inverse
    dn = keep_ref[...] + far_ref[...].astype(F32)
    gg_ref[...] = jnp.sum(dn * scaled, axis=0, keepdims=True)
    ds = dn * gain
    inner = jnp.mean(ds * scaled, axis=-1, keepdims=True)
    out_ref[...] = (mine_ref[128:256, :].astype(F32) + inverse * (ds - scaled * inner)).astype(BF)


def two_rows(vec):
    high = vec.astype(BF).astype(F32)
    return jnp.concatenate([high, vec - high, jnp.zeros((6, vec.shape[1]), F32)], axis=0)


def merge_body(where_ref, got_ref, rows_ref, gg_ref, far_ref, out_ref):
    total = got_ref[0:2].astype(F32)
    for i in range(1, 16):
        total = total + got_ref[2 * i : 2 * i + 2].astype(F32)
    low, high = total[0], total[1]
    cols = jnp.concatenate(
        [piece[:, j * 64 : j * 64 + 64] for j in range(4) for piece in (low, high)], axis=1
    )
    rows = weave(
        jnp.concatenate([low[:32], low[32:]], axis=1),
        jnp.concatenate([high[:32], high[32:]], axis=1),
    )
    grads = jnp.where(x_is_last(where_ref), rows, cols).astype(BF)
    gains = two_rows(gg_ref[...] + far_ref[...])
    gains = jnp.concatenate([gains, jnp.zeros((56, 512), F32)], axis=0).astype(BF)
    every = jnp.concatenate([grads, gains, rows_ref[...]], axis=0)

    def source(i):
        d, k = i >> 3, i & 7
        token = 128 + (k >> 1 & 1) * 64 + d * 2 + (k & 1)
        return jnp.where(k < 4, token, jnp.where(k < 6, d * 2 + (k & 1), 64 + (k & 1)))

    out_ref[...] = dot(chooser(256, 256, source), every).astype(BF)


def split_body(back_ref, tokens_ref, last_ref):
    back = back_ref[...]
    pick = chooser(
        128, 256, lambda i: (i & 31) * 8 + (i >> 5 & 1) * 2 + (i >> 6)
    )
    tokens_ref[...] = dot(pick, back).astype(BF)
    row = lax.broadcasted_iota(jnp.int32, (16, 256), 0)
    col = lax.broadcasted_iota(jnp.int32, (16, 256), 1)
    kind = col & 7
    grads = (row < 8) & (kind == 4 + (row & 1)) & ((col >> 3 & 3) == row >> 1)
    gains = (row == 8) & (kind >= 6)
    sums = dot((grads | gains).astype(F32).astype(BF), back)
    last_ref[:, :512] = sums[0:8].astype(BF)
    gain = jnp.concatenate([sums[8:9, i * 128 : i * 128 + 128] for i in range(4)], axis=0)
    high = gain.astype(BF).astype(F32)
    last_ref[:, 512:] = jnp.concatenate([high, gain - high], axis=0).astype(BF)


def end_body(got_ref, qkv_ref, out_ref, gain_ref):
    for x in range(X):
        pair = got_ref[x].astype(F32) + got_ref[X + x].astype(F32)
        if x < 3:
            qkv_ref[:, x * 512 : x * 512 + 512] = pair[:, :512]
        else:
            out_ref[...] = pair[:, :512]
        gain = pair[0:4, 512:] + pair[4:8, 512:]
        total = gain if x == 0 else total + gain
    gain_ref[...] = total


def on_device(tokens, grad_out, gain, w_qkv, w_out):
    where = lax.axis_index("x").astype(jnp.int32).reshape(1)
    row = gain.reshape(1, 512)

    [packed] = call(
        pack_body,
        [((256, 640), BF)],
        where, tokens.reshape(128, 512), grad_out.reshape(128, 512), w_qkv, w_out,
        smem=1,
    )
    moved = exchange(packed.reshape(ND, 8, 640), PLANE).reshape(256, 640)
    sent, tok = call(
        weights_body, [((32, 128, 128), BF), ((256, 512), BF)], where, moved, smem=1
    )
    weights = exchange(sent, ("x", "y", "c"))
    far = lax.ppermute(tok, "c", SWAP)
    parts, send, keep, mine = call(
        main_body,
        [((32, 64, 256), BF), ((128, 512), BF), ((128, 512), F32), ((256, 512), BF)],
        tok, far, weights, row,
    )
    got = exchange(parts, ("x", "y", "c"))
    dn_far = lax.ppermute(send, "c", SWAP)
    rows, gg = call(
        finish_body, [((128, 512), BF), ((1, 512), F32)], mine, keep, dn_far, row
    )
    gg_far = lax.ppermute(gg, "c", SWAP)
    [sent] = call(merge_body, [((256, 512), BF)], where, got, rows, gg, gg_far, smem=1)
    back = exchange(sent.reshape(ND, 8, 512), PLANE).reshape(256, 512)
    grad_tokens, last = call(split_body, [((128, 512), BF), ((8, 640), BF)], back)
    ends = exchange(jnp.broadcast_to(last[None], (ZH * X, 8, 640)), ("zh", "x"))
    shard_qkv, shard_out, total = call(
        end_body, [((8, 1536), F32), ((8, 512), F32), ((4, 128), F32)], ends
    )
    return grad_tokens.reshape(1, 2, 64, 512), shard_qkv, shard_out, total.reshape(512)


def solution(mesh):
    inner = Mesh(mesh.devices.reshape(ZH, X, ZL, Y, C), ("zh", "x", "zl", "y", "c"))
    grid = ("zl", "y", "c")
    tok = P(("zh", "x"), grid, None, None)
    return jax.shard_map(
        on_device,
        mesh=inner,
        in_specs=(tok, tok, P(), P(grid, None), P(grid, None)),
        out_specs=(tok, P(grid, None), P(grid, None), P()),
        check_vma=False,
    )
```

```python
import jax
import jax.numpy as jnp
from jax import lax
from jax.experimental import pallas as pl
from jax.experimental.pallas import tpu as pltpu
from jax.sharding import Mesh
from jax.sharding import PartitionSpec as P

EPS = 1e-06
BF = jnp.bfloat16
F32 = jnp.float32

ZH, X, ZL, Y, C = 2, 4, 8, 4, 2
SWAP = [(0, 1), (1, 0)]


def exchange(arr, axes):
    return lax.all_to_all(arr, axes, split_axis=0, concat_axis=0, tiled=True)


def over_y(blocks):
    moved = [lax.ppermute(blocks[k], "y", [(i, i ^ k) for i in range(Y)]) for k in range(1, Y)]
    return [blocks[0]] + moved


def call(body, outs, *args, scratch=(), smem=0):
    specs = [pl.BlockSpec(memory_space=pltpu.SMEM)] * smem
    specs += [pl.BlockSpec(memory_space=pltpu.VMEM)] * (len(args) - smem)
    return pl.pallas_call(
        body,
        out_shape=[jax.ShapeDtypeStruct(shape, kind) for shape, kind in outs],
        in_specs=specs,
        out_specs=[pl.BlockSpec(memory_space=pltpu.VMEM)] * len(outs),
        scratch_shapes=list(scratch),
        compiler_params=pltpu.CompilerParams(vmem_limit_bytes=40 * 2**20),
    )(*args)


def dot(a, b, ca=1, cb=0):
    return lax.dot_general(a, b, (((ca,), (cb,)), ((), ())), preferred_element_type=F32)


def chooser(rows, cols, source_of):
    row = lax.broadcasted_iota(jnp.int32, (rows, cols), 0)
    col = lax.broadcasted_iota(jnp.int32, (rows, cols), 1)
    return (col == source_of(row)).astype(F32).astype(BF)


def pack_body(where_ref, tok_ref, grad_ref, wq_ref, wo_ref, out_ref):
    both = jnp.concatenate([tok_ref[...], grad_ref[...]], axis=0)
    pick = chooser(
        256, 256, lambda i: (i >> 2 & 1) * 128 + (i & 1) * 64 + (i >> 1 & 1) * 32 + (i >> 3)
    )
    out_ref[:, :512] = dot(pick, both).astype(BF)
    x = where_ref[0]
    part = wo_ref[...].astype(F32)
    for i in range(3):
        part = jnp.where(x == i, wq_ref[:, i * 512 : i * 512 + 512].astype(F32), part)
    blocks = jnp.concatenate([part[:, y * 128 : y * 128 + 128] for y in range(Y)], axis=0)
    out_ref[:, 512:] = jnp.concatenate([blocks] * ZL, axis=0).astype(BF)


def weights_body(where_ref, moved_ref, sent_ref, hop_ref):
    y = where_ref[1]
    pick = chooser(
        256,
        256,
        lambda i: (i >> 1 & 7) * 32 + ((i >> 6) ^ y) * 8 + (i >> 4 & 3) * 2 + (i & 1),
    )
    tokens = dot(pick, moved_ref[:, :512]).astype(BF)
    for k in range(Y):
        hop_ref[k] = tokens[k * 64 : k * 64 + 64]
    block = moved_ref[:, 512:].astype(F32).reshape(ZL, 4, 8, 128)
    cols = [block[:, lb].reshape(64, 128) for lb in range(4)]
    full = jnp.concatenate(cols, axis=1)
    planes = full.reshape(4, 2, 8, 512)
    outs = x_is_last(where_ref)
    for core in range(2):
        own = planes[:, core].reshape(32, 512)
        own = jnp.concatenate([own[:, :256], own[:, 256:]], axis=0)
        heads = jnp.concatenate([col[:, core * 64 : core * 64 + 64] for col in cols], axis=1)
        mine = jnp.where(outs, own, heads).astype(BF)
        for xy in range(X * Y):
            sent_ref[2 * xy + core] = mine


def gather_body(b0_ref, b1_ref, b2_ref, b3_ref, out_ref):
    for tf in range(4):
        for k, ref in enumerate((b0_ref, b1_ref, b2_ref, b3_ref)):
            out_ref[tf * 64 + k * 16 : tf * 64 + k * 16 + 16] = ref[tf * 16 : tf * 16 + 16]


def x_is_last(where_ref):
    return where_ref[0] == 3


def weave(first, second):
    rows, cols = first.shape
    blocks = [arr.reshape(rows // 8, 1, 8, cols) for arr in (first, second)]
    return jnp.concatenate(blocks, axis=1).reshape(2 * rows, cols)


def main_body(
    own_ref, far_ref, w_ref, gain_ref, parts_ref, send_ref, keep_ref
):
    def gathered(part, count, width, piece):
        blocks = [piece(w_ref[part * 8 + yc].astype(F32)) for yc in range(8)]
        blocks = [block.reshape(count, 1, 8, width) for block in blocks]
        return jnp.concatenate(blocks, axis=1).reshape(count * 64, width).astype(BF)

    wh = jnp.concatenate([gathered(x, 8, 256, lambda arr: arr) for x in range(3)], axis=1)
    wo = gathered(3, 4, 512, lambda arr: jnp.concatenate([arr[:32], arr[32:]], axis=1))

    own, far = own_ref[...], far_ref[...]
    x_in = jnp.concatenate([own[0:64], far[0:64], own[64:128], far[64:128]], axis=0)
    g_in = jnp.concatenate([own[128:192], far[128:192], own[192:], far[192:]], axis=0)

    values = x_in.astype(F32)
    inverse = lax.rsqrt(jnp.mean(values * values, axis=-1, keepdims=True) + EPS)
    scaled = values * inverse
    normed = (scaled * gain_ref[...]).astype(BF)
    qkv = dot(normed, wh).astype(BF)
    ups = dot(g_in, wo, 1, 1).astype(BF)

    lane = lax.broadcasted_iota(jnp.int32, (128, 128), 1)
    first = lane < 64
    zero = jnp.zeros((128, 128), BF)

    def stack(arr):
        return jnp.concatenate([jnp.where(first, arr, zero), jnp.where(first, zero, arr)], axis=0)

    def pile(arr):
        return jnp.concatenate([arr[:, :128], arr[:, 128:]], axis=0)

    atts, dqs, dks, dvs = [], [], [], []
    for f in range(2):
        rows = slice(f * 128, (f + 1) * 128)
        for pair in range(2):
            at = pair * 128
            q = qkv[rows, at : at + 128]
            k2 = stack(qkv[rows, 256 + at : 256 + at + 128])
            v2 = stack(qkv[rows, 512 + at : 512 + at + 128])
            u = ups[rows, at : at + 128]
            scores = dot(q, k2, 1, 1) * 0.125
            dprob = dot(u, v2, 1, 1)
            weights, dscores = [], []
            for head in range(2):
                cols = slice(head * 128, (head + 1) * 128)
                s = scores[:, cols]
                expo = jnp.exp(s - jnp.max(s, axis=-1, keepdims=True))
                probs = expo * (1.0 / jnp.sum(expo, axis=-1, keepdims=True))
                dp = dprob[:, cols]
                weights.append(probs.astype(BF))
                inner = jnp.sum(probs * dp, axis=-1, keepdims=True)
                dscores.append((probs * (dp - inner) * 0.125).astype(BF))
            weight = jnp.concatenate(weights, axis=1)
            dscore = jnp.concatenate(dscores, axis=1)
            atts.append(dot(weight, v2).astype(BF))
            dqs.append(dot(dscore, k2).astype(BF))
            dks.append(dot(pile(dscore), stack(q), 0, 0).astype(BF))
            dvs.append(dot(pile(weight), stack(u), 0, 0).astype(BF))

    def frames(items):
        return [
            jnp.concatenate([items[0], items[2]], axis=0),
            jnp.concatenate([items[1], items[3]], axis=0),
        ]

    att = jnp.concatenate(frames(atts), axis=1)
    dqkv = jnp.concatenate(frames(dqs) + frames(dks) + frames(dvs), axis=1)

    dn = dot(dqkv, wh, 1, 1)
    keep_ref[...] = jnp.concatenate([dn[0:64], dn[128:192]], axis=0)
    send_ref[...] = jnp.concatenate([dn[64:128], dn[192:]], axis=0).astype(BF)

    gg = two_rows(jnp.sum(dn * scaled, axis=0, keepdims=True))
    gg = jnp.concatenate([gg[0:2, i * 128 : i * 128 + 128] for i in range(4)], axis=0)

    g_qkv = dot(normed, dqkv, 0, 0).reshape(ZL, Y, 2, 8, 768)
    g_out = dot(att, g_in, 0, 0).reshape(4, Y, 2, 8, 512)
    for yc in range(8):
        block = g_qkv[:, yc // 2, yc % 2].reshape(64, 768)
        for part in range(3):
            at = part * 256
            pieces = [block[:, at : at + 128], block[:, at + 128 : at + 256], gg]
            parts_ref[part * 8 + yc] = jnp.concatenate(pieces, axis=0).astype(BF)
        block = g_out[:, yc // 2, yc % 2].reshape(32, 512)
        pieces = [block[:, i * 128 : i * 128 + 128] for i in range(4)] + [gg]
        parts_ref[24 + yc] = jnp.concatenate(pieces, axis=0).astype(BF)


def finish_body(own_ref, keep_ref, far_ref, gain_ref, out_ref):
    gain = gain_ref[...]
    values = own_ref[0:128, :].astype(F32)
    inverse = lax.rsqrt(jnp.mean(values * values, axis=-1, keepdims=True) + EPS)
    scaled = values * inverse
    ds = (keep_ref[...] + far_ref[...].astype(F32)) * gain
    inner = jnp.mean(ds * scaled, axis=-1, keepdims=True)
    result = (own_ref[128:256, :].astype(F32) + inverse * (ds - scaled * inner)).astype(BF)
    for k in range(Y):
        out_ref[k] = jnp.concatenate(
            [result[k * 16 : k * 16 + 16], result[64 + k * 16 : 64 + k * 16 + 16]], axis=0
        )


def two_rows(vec):
    high = vec.astype(BF).astype(F32)
    return jnp.concatenate([high, vec - high, jnp.zeros((6, vec.shape[1]), F32)], axis=0)


def two_blocks(rows):
    high = rows.astype(BF).astype(F32)
    return jnp.concatenate([high, rows - high], axis=0)


def merge_body(where_ref, got_ref, b0_ref, b1_ref, b2_ref, b3_ref, out_ref):
    total = got_ref[0:2].astype(F32)
    for i in range(1, 16):
        total = total + got_ref[2 * i : 2 * i + 2].astype(F32)
    low, high = total[0, :128], total[1, :128]
    wide_low = jnp.concatenate([low[:64], low[64:]], axis=1)
    wide_high = jnp.concatenate([high[:64], high[64:]], axis=1)
    cols = jnp.concatenate(
        [piece[:, j * 64 : j * 64 + 64] for j in range(4) for piece in (wide_low, wide_high)],
        axis=1,
    )
    rows = weave(
        jnp.concatenate([low[i * 32 : i * 32 + 32] for i in range(4)], axis=1),
        jnp.concatenate([high[i * 32 : i * 32 + 32] for i in range(4)], axis=1),
    )
    out_ref[:, :512] = jnp.where(x_is_last(where_ref), rows, cols).astype(BF)
    pick = chooser(64, 64, lambda i: (i >> 1 & 3) * 16 + (i >> 3) * 2 + (i & 1))
    for f in range(2):
        blocks = [ref[f * 16 : f * 16 + 16] for ref in (b0_ref, b1_ref, b2_ref, b3_ref)]
        rows = dot(pick, jnp.concatenate(blocks, axis=0)).astype(BF)
        out_ref[:, 512 + f * 512 : 1024 + f * 512] = rows
    gains = total[0, 128:] + total[1, 128:]
    gains = two_blocks(unpair(gains))
    out_ref[:, 1536:] = jnp.concatenate([gains] * ZL, axis=0).astype(BF)


def unpair(rows):
    return jnp.concatenate(
        [rows[2 * i : 2 * i + 1] + rows[2 * i + 1 : 2 * i + 2] for i in range(4)], axis=0
    )


def split_body(where_ref, back_ref, tokens_ref, last_ref):
    y = where_ref[1]
    pick = chooser(64, 64, lambda i: (i >> 2 & 7) * 8 + ((i & 3) ^ y) * 2 + (i >> 5))
    for f in range(2):
        rows = dot(pick, back_ref[:, 512 + f * 512 : 1024 + f * 512]).astype(BF)
        for b in range(2):
            tokens_ref[b * 64 + f * 32 : b * 64 + f * 32 + 32] = rows[b * 32 : b * 32 + 32]
    sums = jnp.sum(back_ref[:, :512].astype(F32).reshape(ZL, 8, 512), axis=0)
    last_ref[:, :512] = sums.astype(BF)
    gains = jnp.sum(back_ref[:, 1536:].astype(F32).reshape(ZL, 8, 128), axis=0)
    last_ref[:, 512:] = two_blocks(gains[0:4] + gains[4:8]).astype(BF)


def end_body(got_ref, qkv_ref, out_ref, gain_ref):
    for x in range(X):
        pair = got_ref[x].astype(F32) + got_ref[X + x].astype(F32)
        if x < 3:
            qkv_ref[:, x * 512 : x * 512 + 512] = pair[:, :512]
        else:
            out_ref[...] = pair[:, :512]
        if x == 0:
            gain_ref[...] = pair[0:4, 512:] + pair[4:8, 512:]


def on_device(tokens, grad_out, gain, w_qkv, w_out):
    where = jnp.stack([lax.axis_index("x"), lax.axis_index("y")]).astype(jnp.int32)
    row = gain.reshape(1, 512)
    plane = ("x", "y", "c")

    [packed] = call(
        pack_body,
        [((256, 640), BF)],
        where, tokens.reshape(128, 512), grad_out.reshape(128, 512), w_qkv, w_out,
        smem=1,
    )
    moved = exchange(packed.reshape(ZL, 32, 640), "zl").reshape(256, 640)
    sent, hop = call(
        weights_body, [((32, 64, 256), BF), ((Y, 64, 512), BF)], where, moved, smem=1
    )
    weights = exchange(sent, plane)
    [own] = call(gather_body, [((256, 512), BF)], *over_y(hop))
    far = lax.ppermute(own, "c", SWAP)
    parts, send, keep = call(
        main_body,
        [((32, 136, 128), BF), ((128, 512), BF), ((128, 512), F32)],
        own, far, weights, row,
    )
    got = exchange(parts, plane)
    dn_far = lax.ppermute(send, "c", SWAP)
    [result] = call(finish_body, [((Y, 32, 512), BF)], own, keep, dn_far, row)
    [sent] = call(merge_body, [((64, 1664), BF)], where, got, *over_y(result), smem=1)
    back = exchange(sent.reshape(ZL, 8, 1664), "zl").reshape(64, 1664)
    grad_tokens, last = call(
        split_body, [((128, 512), BF), ((8, 640), BF)], where, back, smem=1
    )
    ends = exchange(jnp.broadcast_to(last[None], (ZH * X, 8, 640)), ("zh", "x"))
    shard_qkv, shard_out, total = call(
        end_body, [((8, 1536), F32), ((8, 512), F32), ((4, 128), F32)], ends
    )
    return grad_tokens.reshape(1, 2, 64, 512), shard_qkv, shard_out, total.reshape(512)


def solution(mesh):
    inner = Mesh(mesh.devices.reshape(ZH, X, ZL, Y, C), ("zh", "x", "zl", "y", "c"))
    grid = ("zl", "y", "c")
    tok = P(("zh", "x"), grid, None, None)
    return jax.shard_map(
        on_device,
        mesh=inner,
        in_specs=(tok, tok, P(), P(grid, None), P(grid, None)),
        out_specs=(tok, P(grid, None), P(grid, None), P()),
        check_vma=False,
    )
```

```python
import jax
import jax.numpy as jnp
from jax import lax
from jax.experimental import pallas as pl
from jax.experimental.pallas import tpu as pltpu
from jax.sharding import Mesh
from jax.sharding import PartitionSpec as P

EPS = 1e-06
BF = jnp.bfloat16
F32 = jnp.float32

ZH, X, ZL, Y, C = 2, 4, 8, 4, 2
SWAP = [(0, 1), (1, 0)]


def exchange(arr, axes):
    return lax.all_to_all(arr, axes, split_axis=0, concat_axis=0, tiled=True)


def over_y(blocks):
    moved = [lax.ppermute(blocks[k], "y", [(i, i ^ k) for i in range(Y)]) for k in range(1, Y)]
    return [blocks[0]] + moved


def call(body, outs, *args, scratch=(), smem=0):
    specs = [pl.BlockSpec(memory_space=pltpu.SMEM)] * smem
    specs += [pl.BlockSpec(memory_space=pltpu.VMEM)] * (len(args) - smem)
    return pl.pallas_call(
        body,
        out_shape=[jax.ShapeDtypeStruct(shape, kind) for shape, kind in outs],
        in_specs=specs,
        out_specs=[pl.BlockSpec(memory_space=pltpu.VMEM)] * len(outs),
        scratch_shapes=list(scratch),
        compiler_params=pltpu.CompilerParams(vmem_limit_bytes=40 * 2**20),
    )(*args)


def dot(a, b, ca=1, cb=0):
    return lax.dot_general(a, b, (((ca,), (cb,)), ((), ())), preferred_element_type=F32)


def chooser(rows, cols, source_of):
    row = lax.broadcasted_iota(jnp.int32, (rows, cols), 0)
    col = lax.broadcasted_iota(jnp.int32, (rows, cols), 1)
    return (col == source_of(row)).astype(F32).astype(BF)


def pack_body(
    where_ref, tok_ref, grad_ref, wq_ref, wo_ref, out_ref, both_vm, wq_vm, wo_vm, sems
):
    copies = [
        pltpu.make_async_copy(src, dst, sems.at[i])
        for i, (src, dst) in enumerate(
            [
                (tok_ref, both_vm.at[0:128]),
                (grad_ref, both_vm.at[128:256]),
                (wq_ref, wq_vm),
                (wo_ref, wo_vm),
            ]
        )
    ]
    for copy in copies:
        copy.start()
    pick = chooser(
        256, 256, lambda i: (i >> 2 & 1) * 128 + (i & 1) * 64 + (i >> 1 & 1) * 32 + (i >> 3)
    )
    for copy in copies:
        copy.wait()
    out_ref[:, :512] = dot(pick, both_vm[...]).astype(BF)
    x = where_ref[0]
    part = wo_vm[...].astype(F32)
    for i in range(3):
        part = jnp.where(x == i, wq_vm[:, i * 512 : i * 512 + 512].astype(F32), part)
    blocks = jnp.concatenate([part[:, y * 128 : y * 128 + 128] for y in range(Y)], axis=0)
    out_ref[:, 512:] = jnp.concatenate([blocks] * ZL, axis=0).astype(BF)


def halves(arr):
    return arr[:, :64], arr[:, 64:]


def weights_body(where_ref, moved_ref, sent_ref, own_ref):
    pick = chooser(
        256, 256, lambda i: (i >> 1 & 31) * 8 + (i >> 7) * 4 + (i >> 6 & 1) * 2 + (i & 1)
    )
    own_ref[...] = dot(pick, moved_ref[:, :512]).astype(BF)
    block = moved_ref[:, 512:].astype(F32)
    (low0, low1), (high0, high1) = halves(block[:128]), halves(block[128:])
    planes = block.reshape(4, 2, 32, 128)
    outs = x_is_last(where_ref)
    for core, cols in ((0, (low0, high0)), (1, (low1, high1))):
        mine = jnp.where(
            outs, planes[:, core].reshape(128, 128), jnp.concatenate(cols, axis=1)
        ).astype(BF)
        for xy in range(X * Y):
            sent_ref[2 * xy + core] = mine


def x_is_last(where_ref):
    return where_ref[0] == 3


def weave(first, second):
    rows, cols = first.shape
    blocks = [arr.reshape(rows // 8, 1, 8, cols) for arr in (first, second)]
    return jnp.concatenate(blocks, axis=1).reshape(2 * rows, cols)


def main_body(
    own_ref, far_ref, w_ref, gain_ref, parts_ref, send_ref, keep_ref
):
    lanes = []
    for x in range(3):
        for pair in range(2):
            tops, bots = [], []
            for core in range(2):
                at = x * 8 + pair * 4 + core
                (a0, a1), (b0, b1) = (
                    halves(w_ref[at].astype(F32)),
                    halves(w_ref[at + 2].astype(F32)),
                )
                tops.append(jnp.concatenate([a0, b0], axis=1))
                bots.append(jnp.concatenate([a1, b1], axis=1))
            lanes.append(jnp.concatenate([weave(*tops), weave(*bots)], axis=0).astype(BF))
    wh = jnp.concatenate(lanes, axis=1)
    lanes = [
        weave(w_ref[24 + 2 * y].astype(F32), w_ref[25 + 2 * y].astype(F32)).astype(BF)
        for y in range(Y)
    ]
    wo = jnp.concatenate(lanes, axis=1)

    own, far = own_ref[...], far_ref[...]
    x_in = jnp.concatenate([own[0:64], far[0:64], own[64:128], far[64:128]], axis=0)
    g_in = jnp.concatenate([own[128:192], far[128:192], own[192:], far[192:]], axis=0)

    values = x_in.astype(F32)
    inverse = lax.rsqrt(jnp.mean(values * values, axis=-1, keepdims=True) + EPS)
    scaled = values * inverse
    normed = (scaled * gain_ref[...]).astype(BF)
    qkv = dot(normed, wh).astype(BF)
    ups = dot(g_in, wo, 1, 1).astype(BF)

    lane = lax.broadcasted_iota(jnp.int32, (128, 128), 1)
    first = lane < 64
    zero = jnp.zeros((128, 128), BF)

    def stack(arr):
        return jnp.concatenate([jnp.where(first, arr, zero), jnp.where(first, zero, arr)], axis=0)

    def pile(arr):
        return jnp.concatenate([arr[:, :128], arr[:, 128:]], axis=0)

    atts, dqs, dks, dvs = [], [], [], []
    for f in range(2):
        rows = slice(f * 128, (f + 1) * 128)
        for pair in range(2):
            at = pair * 128
            q = qkv[rows, at : at + 128]
            k2 = stack(qkv[rows, 256 + at : 256 + at + 128])
            v2 = stack(qkv[rows, 512 + at : 512 + at + 128])
            u = ups[rows, at : at + 128]
            scores = dot(q, k2, 1, 1) * 0.125
            dprob = dot(u, v2, 1, 1)
            weights, dscores = [], []
            for head in range(2):
                cols = slice(head * 128, (head + 1) * 128)
                s = scores[:, cols]
                expo = jnp.exp(s - jnp.max(s, axis=-1, keepdims=True))
                probs = expo * (1.0 / jnp.sum(expo, axis=-1, keepdims=True))
                dp = dprob[:, cols]
                weights.append(probs.astype(BF))
                inner = jnp.sum(probs * dp, axis=-1, keepdims=True)
                dscores.append((probs * (dp - inner) * 0.125).astype(BF))
            weight = jnp.concatenate(weights, axis=1)
            dscore = jnp.concatenate(dscores, axis=1)
            atts.append(dot(weight, v2).astype(BF))
            dqs.append(dot(dscore, k2).astype(BF))
            dks.append(dot(pile(dscore), stack(q), 0, 0).astype(BF))
            dvs.append(dot(pile(weight), stack(u), 0, 0).astype(BF))

    def frames(items):
        return [
            jnp.concatenate([items[0], items[2]], axis=0),
            jnp.concatenate([items[1], items[3]], axis=0),
        ]

    att = jnp.concatenate(frames(atts), axis=1)
    dqkv = jnp.concatenate(frames(dqs) + frames(dks) + frames(dvs), axis=1)

    dn = dot(dqkv, wh, 1, 1)
    keep_ref[...] = jnp.concatenate([dn[0:64], dn[128:192]], axis=0)
    send_ref[...] = jnp.concatenate([dn[64:128], dn[192:]], axis=0).astype(BF)

    gg = two_rows(jnp.sum(dn * scaled, axis=0, keepdims=True))
    gg = jnp.concatenate([gg[0:2, i * 128 : i * 128 + 128] for i in range(4)], axis=0)

    g_qkv = dot(normed, dqkv, 0, 0).reshape(ZL, Y, 2, 8, 768)
    g_out = dot(att, g_in, 0, 0).reshape(4, Y, 2, 8, 512)
    for yc in range(8):
        block = g_qkv[:, yc // 2, yc % 2].reshape(64, 768)
        for part in range(3):
            at = part * 256
            pieces = [block[:, at : at + 128], block[:, at + 128 : at + 256], gg]
            parts_ref[part * 8 + yc] = jnp.concatenate(pieces, axis=0).astype(BF)
        block = g_out[:, yc // 2, yc % 2].reshape(32, 512)
        pieces = [block[:, i * 128 : i * 128 + 128] for i in range(4)] + [gg]
        parts_ref[24 + yc] = jnp.concatenate(pieces, axis=0).astype(BF)


def finish_body(own_ref, keep_ref, far_ref, gain_ref, out_ref):
    gain = gain_ref[...]
    values = own_ref[0:128, :].astype(F32)
    inverse = lax.rsqrt(jnp.mean(values * values, axis=-1, keepdims=True) + EPS)
    scaled = values * inverse
    ds = (keep_ref[...] + far_ref[...].astype(F32)) * gain
    inner = jnp.mean(ds * scaled, axis=-1, keepdims=True)
    out_ref[...] = (own_ref[128:256, :].astype(F32) + inverse * (ds - scaled * inner)).astype(BF)


def two_rows(vec):
    high = vec.astype(BF).astype(F32)
    return jnp.concatenate([high, vec - high, jnp.zeros((6, vec.shape[1]), F32)], axis=0)


def two_blocks(rows):
    high = rows.astype(BF).astype(F32)
    return jnp.concatenate([high, rows - high], axis=0)


def merge_body(where_ref, got_ref, rows_ref, out_ref):
    total = got_ref[0:2].astype(F32)
    for i in range(1, 16):
        total = total + got_ref[2 * i : 2 * i + 2].astype(F32)
    low, high = total[0, :128], total[1, :128]
    wide_low = jnp.concatenate([low[:64], low[64:]], axis=1)
    wide_high = jnp.concatenate([high[:64], high[64:]], axis=1)
    cols = jnp.concatenate(
        [piece[:, j * 64 : j * 64 + 64] for j in range(4) for piece in (wide_low, wide_high)],
        axis=1,
    )
    rows = weave(
        jnp.concatenate([low[i * 32 : i * 32 + 32] for i in range(4)], axis=1),
        jnp.concatenate([high[i * 32 : i * 32 + 32] for i in range(4)], axis=1),
    )
    out_ref[:, :512] = jnp.where(x_is_last(where_ref), rows, cols).astype(BF)
    for f in range(2):
        out_ref[:, 512 + f * 512 : 1024 + f * 512] = rows_ref[f * 64 : f * 64 + 64]
    gains = total[0, 128:] + total[1, 128:]
    gains = two_blocks(unpair(gains))
    out_ref[:, 1536:] = jnp.concatenate([gains] * ZL, axis=0).astype(BF)


def unpair(rows):
    return jnp.concatenate(
        [rows[2 * i : 2 * i + 1] + rows[2 * i + 1 : 2 * i + 2] for i in range(4)], axis=0
    )


def split_body(where_ref, back_ref, hop_ref, last_ref):
    y = where_ref[1]
    pick = chooser(64, 64, lambda i: (i >> 1 & 7) * 8 + ((i >> 4) ^ y) * 2 + (i & 1))
    for f in range(2):
        rows = dot(pick, back_ref[:, 512 + f * 512 : 1024 + f * 512]).astype(BF)
        for k in range(Y):
            hop_ref[k, f * 16 : f * 16 + 16] = rows[k * 16 : k * 16 + 16]
    sums = jnp.sum(back_ref[:, :512].astype(F32).reshape(ZL, 8, 512), axis=0)
    last_ref[:, :512] = sums.astype(BF)
    gains = jnp.sum(back_ref[:, 1536:].astype(F32).reshape(ZL, 8, 128), axis=0)
    last_ref[:, 512:] = two_blocks(gains[0:4] + gains[4:8]).astype(BF)


def tokens_body(where_ref, b0_ref, b1_ref, b2_ref, b3_ref, out_ref):
    y = where_ref[1]
    blocks = jnp.concatenate([ref[...] for ref in (b0_ref, b1_ref, b2_ref, b3_ref)], axis=0)

    def source(i):
        return ((i & 3) ^ y) * 32 + (i >> 5 & 1) * 16 + (i >> 2 & 7) * 2 + (i >> 6)

    out_ref[...] = dot(chooser(128, 128, source), blocks).astype(BF)


def end_body(got_ref, qkv_ref, out_ref, gain_ref):
    for x in range(X):
        pair = got_ref[x].astype(F32) + got_ref[X + x].astype(F32)
        if x < 3:
            qkv_ref[:, x * 512 : x * 512 + 512] = pair[:, :512]
        else:
            out_ref[...] = pair[:, :512]
        if x == 0:
            gain_ref[...] = pair[0:4, 512:] + pair[4:8, 512:]


def on_device(tokens, grad_out, gain, w_qkv, w_out):
    where = jnp.stack([lax.axis_index("x"), lax.axis_index("y")]).astype(jnp.int32)
    row = gain.reshape(1, 512)
    plane = ("x", "y", "c")

    hbm = pl.BlockSpec(memory_space=pl.ANY)
    packed = pl.pallas_call(
        pack_body,
        out_shape=jax.ShapeDtypeStruct((256, 640), BF),
        in_specs=[pl.BlockSpec(memory_space=pltpu.SMEM)] + [hbm] * 4,
        out_specs=pl.BlockSpec(memory_space=pltpu.VMEM),
        scratch_shapes=[
            pltpu.VMEM((256, 512), BF),
            pltpu.VMEM((8, 1536), BF),
            pltpu.VMEM((8, 512), BF),
            pltpu.SemaphoreType.DMA((4,)),
        ],
        compiler_params=pltpu.CompilerParams(vmem_limit_bytes=60 * 2**20),
    )(where, tokens.reshape(128, 512), grad_out.reshape(128, 512), w_qkv, w_out)
    moved = exchange(packed.reshape(ZL * Y, 8, 640), ("zl", "y")).reshape(256, 640)
    sent, own = call(
        weights_body, [((32, 128, 128), BF), ((256, 512), BF)], where, moved, smem=1
    )
    weights = exchange(sent, plane)
    far = lax.ppermute(own, "c", SWAP)
    parts, send, keep = call(
        main_body,
        [((32, 136, 128), BF), ((128, 512), BF), ((128, 512), F32)],
        own, far, weights, row,
    )
    got = exchange(parts, plane)
    dn_far = lax.ppermute(send, "c", SWAP)
    [result] = call(finish_body, [((128, 512), BF)], own, keep, dn_far, row)
    [sent] = call(merge_body, [((64, 1664), BF)], where, got, result, smem=1)
    back = exchange(sent.reshape(ZL, 8, 1664), "zl").reshape(64, 1664)
    hop, last = call(
        split_body, [((Y, 32, 512), BF), ((8, 640), BF)], where, back, smem=1
    )
    ends = exchange(jnp.broadcast_to(last[None], (ZH * X, 8, 640)), ("zh", "x"))
    [grad_tokens] = call(tokens_body, [((128, 512), BF)], where, *over_y(hop), smem=1)
    shard_qkv, shard_out, total = call(
        end_body, [((8, 1536), F32), ((8, 512), F32), ((4, 128), F32)], ends
    )
    return grad_tokens.reshape(1, 2, 64, 512), shard_qkv, shard_out, total.reshape(512)


def solution(mesh):
    inner = Mesh(mesh.devices.reshape(ZH, X, ZL, Y, C), ("zh", "x", "zl", "y", "c"))
    grid = ("zl", "y", "c")
    tok = P(("zh", "x"), grid, None, None)
    return jax.shard_map(
        on_device,
        mesh=inner,
        in_specs=(tok, tok, P(), P(grid, None), P(grid, None)),
        out_specs=(tok, P(grid, None), P(grid, None), P()),
        check_vma=False,
    )
```

```python
import jax
import jax.numpy as jnp
from jax import lax
from jax.experimental import pallas as pl
from jax.experimental.pallas import tpu as pltpu
from jax.sharding import Mesh
from jax.sharding import PartitionSpec as P

EPS = 1e-06
BF = jnp.bfloat16
F32 = jnp.float32

ZH, X, ZL, Y, C = 2, 4, 8, 4, 2
SWAP = [(0, 1), (1, 0)]


def exchange(arr, axes):
    return lax.all_to_all(arr, axes, split_axis=0, concat_axis=0, tiled=True)


def to_y(block, k):
    return lax.ppermute(block, "y", [(i, i ^ k) for i in range(Y)])


def call(body, outs, *args):
    vmem = pl.BlockSpec(memory_space=pltpu.VMEM)
    return pl.pallas_call(
        body,
        out_shape=[jax.ShapeDtypeStruct(shape, kind) for shape, kind in outs],
        in_specs=[vmem] * len(args),
        out_specs=[vmem] * len(outs),
        compiler_params=pltpu.CompilerParams(vmem_limit_bytes=40 * 2**20),
    )(*args)


def dot(a, b, ca=1, cb=0):
    return lax.dot_general(a, b, (((ca,), (cb,)), ((), ())), preferred_element_type=F32)


def chooser(rows, cols, source_of):
    row = lax.broadcasted_iota(jnp.int32, (rows, cols), 0)
    col = lax.broadcasted_iota(jnp.int32, (rows, cols), 1)
    return (col == source_of(row)).astype(F32).astype(BF)


def pack_body(
    tok_ref, grad_ref, wq_ref, wo_ref, out_ref, both_vm, wq_vm, wo_vm, sems
):
    copies = [
        pltpu.make_async_copy(src, dst, sems.at[i])
        for i, (src, dst) in enumerate(
            [
                (tok_ref, both_vm.at[0:128]),
                (grad_ref, both_vm.at[128:256]),
                (wq_ref, wq_vm),
                (wo_ref, wo_vm),
            ]
        )
    ]
    for copy in copies:
        copy.start()
    pick = chooser(
        256, 256, lambda i: (i >> 2 & 1) * 128 + (i & 1) * 64 + (i >> 1 & 1) * 32 + (i >> 3)
    )
    for copy in copies:
        copy.wait()
    out_ref[:, :512] = dot(pick, both_vm[...]).astype(BF)
    x = lax.axis_index("x")
    part = wo_vm[...].astype(F32)
    for i in range(3):
        part = jnp.where(x == i, wq_vm[:, i * 512 : i * 512 + 512].astype(F32), part)
    blocks = jnp.concatenate([part[:, y * 128 : y * 128 + 128] for y in range(Y)], axis=0)
    out_ref[:, 512:] = jnp.concatenate([blocks] * ZL, axis=0).astype(BF)


def halves(arr):
    return arr[:, :64], arr[:, 64:]


def weights_body(moved_ref, sent_ref):
    block = moved_ref[:, 512:].astype(F32)
    (low0, low1), (high0, high1) = halves(block[:128]), halves(block[128:])
    planes = block.reshape(4, 2, 32, 128)
    outs = x_is_last()
    for core, cols in ((0, (low0, high0)), (1, (low1, high1))):
        mine = jnp.where(
            outs, planes[:, core].reshape(128, 128), jnp.concatenate(cols, axis=1)
        ).astype(BF)
        for xy in range(X * Y):
            sent_ref[2 * xy + core] = mine


def rows_body(moved_ref, own_ref):
    pick = chooser(
        256, 256, lambda i: (i >> 1 & 31) * 8 + (i >> 7) * 4 + (i >> 6 & 1) * 2 + (i & 1)
    )
    own_ref[...] = dot(pick, moved_ref[:, :512]).astype(BF)


def norm_body(own_ref, far_ref, gain_ref, scaled_ref, normed_ref, grad_ref):
    own, far = own_ref[...], far_ref[...]
    x_in = jnp.concatenate([own[0:64], far[0:64], own[64:128], far[64:128]], axis=0)
    grad_ref[...] = jnp.concatenate([own[128:192], far[128:192], own[192:], far[192:]], axis=0)
    values = x_in.astype(F32)
    inverse = lax.rsqrt(jnp.mean(values * values, axis=-1, keepdims=True) + EPS)
    scaled = values * inverse
    scaled_ref[...] = scaled
    normed_ref[...] = (scaled * gain_ref[...]).astype(BF)


def x_is_last():
    return lax.axis_index("x") == 3


def weave(first, second):
    rows, cols = first.shape
    blocks = [arr.reshape(rows // 8, 1, 8, cols) for arr in (first, second)]
    return jnp.concatenate(blocks, axis=1).reshape(2 * rows, cols)


def main_body(
    scaled_ref, normed_ref, grad_ref, w_ref, parts_ref, send_ref, keep_ref
):
    lanes = []
    for x in range(3):
        for pair in range(2):
            tops, bots = [], []
            for core in range(2):
                at = x * 8 + pair * 4 + core
                (a0, a1), (b0, b1) = (
                    halves(w_ref[at].astype(F32)),
                    halves(w_ref[at + 2].astype(F32)),
                )
                tops.append(jnp.concatenate([a0, b0], axis=1))
                bots.append(jnp.concatenate([a1, b1], axis=1))
            lanes.append(jnp.concatenate([weave(*tops), weave(*bots)], axis=0).astype(BF))
    wh = jnp.concatenate(lanes, axis=1)
    lanes = [
        weave(w_ref[24 + 2 * y].astype(F32), w_ref[25 + 2 * y].astype(F32)).astype(BF)
        for y in range(Y)
    ]
    wo = jnp.concatenate(lanes, axis=1)

    normed, g_in = normed_ref[...], grad_ref[...]
    qkv = dot(normed, wh).astype(BF)
    ups = dot(g_in, wo, 1, 1).astype(BF)

    lane = lax.broadcasted_iota(jnp.int32, (128, 128), 1)
    first = lane < 64
    zero = jnp.zeros((128, 128), BF)

    def stack(arr):
        return jnp.concatenate([jnp.where(first, arr, zero), jnp.where(first, zero, arr)], axis=0)

    def pile(arr):
        return jnp.concatenate([arr[:, :128], arr[:, 128:]], axis=0)

    atts, dqs, dks, dvs = [], [], [], []
    for f in range(2):
        rows = slice(f * 128, (f + 1) * 128)
        for pair in range(2):
            at = pair * 128
            q = qkv[rows, at : at + 128]
            k2 = stack(qkv[rows, 256 + at : 256 + at + 128])
            v2 = stack(qkv[rows, 512 + at : 512 + at + 128])
            u = ups[rows, at : at + 128]
            scores = dot(q, k2, 1, 1) * 0.125
            dprob = dot(u, v2, 1, 1)
            weights, dscores = [], []
            for head in range(2):
                cols = slice(head * 128, (head + 1) * 128)
                s = scores[:, cols]
                expo = jnp.exp(s - jnp.max(s, axis=-1, keepdims=True))
                probs = expo * (1.0 / jnp.sum(expo, axis=-1, keepdims=True))
                dp = dprob[:, cols]
                weights.append(probs.astype(BF))
                inner = jnp.sum(probs * dp, axis=-1, keepdims=True)
                dscores.append((probs * (dp - inner) * 0.125).astype(BF))
            weight = jnp.concatenate(weights, axis=1)
            dscore = jnp.concatenate(dscores, axis=1)
            atts.append(dot(weight, v2).astype(BF))
            dqs.append(dot(dscore, k2).astype(BF))
            dks.append(dot(pile(dscore), stack(q), 0, 0).astype(BF))
            dvs.append(dot(pile(weight), stack(u), 0, 0).astype(BF))

    def frames(items):
        return [
            jnp.concatenate([items[0], items[2]], axis=0),
            jnp.concatenate([items[1], items[3]], axis=0),
        ]

    att = jnp.concatenate(frames(atts), axis=1)
    dqkv = jnp.concatenate(frames(dqs) + frames(dks) + frames(dvs), axis=1)

    dn = dot(dqkv, wh, 1, 1)
    keep_ref[...] = jnp.concatenate([dn[0:64], dn[128:192]], axis=0)
    send_ref[...] = jnp.concatenate([dn[64:128], dn[192:]], axis=0).astype(BF)

    gg = two_rows(jnp.sum(dn * scaled_ref[...], axis=0, keepdims=True))
    gg = jnp.concatenate([gg[0:2, i * 128 : i * 128 + 128] for i in range(4)], axis=0)

    g_qkv = dot(normed, dqkv, 0, 0).reshape(ZL, Y, 2, 8, 768)
    g_out = dot(att, g_in, 0, 0).reshape(4, Y, 2, 8, 512)
    for yc in range(8):
        block = g_qkv[:, yc // 2, yc % 2].reshape(64, 768)
        for part in range(3):
            at = part * 256
            pieces = [block[:, at : at + 128], block[:, at + 128 : at + 256], gg]
            parts_ref[part * 8 + yc] = jnp.concatenate(pieces, axis=0).astype(BF)
        block = g_out[:, yc // 2, yc % 2].reshape(32, 512)
        pieces = [block[:, i * 128 : i * 128 + 128] for i in range(4)] + [gg]
        parts_ref[24 + yc] = jnp.concatenate(pieces, axis=0).astype(BF)


def finish_body(own_ref, keep_ref, far_ref, gain_ref, out_ref):
    gain = gain_ref[...]
    values = own_ref[0:128, :].astype(F32)
    inverse = lax.rsqrt(jnp.mean(values * values, axis=-1, keepdims=True) + EPS)
    scaled = values * inverse
    ds = (keep_ref[...] + far_ref[...].astype(F32)) * gain
    inner = jnp.mean(ds * scaled, axis=-1, keepdims=True)
    result = (own_ref[128:256, :].astype(F32) + inverse * (ds - scaled * inner)).astype(BF)
    y = lax.axis_index("y")

    def source(i):
        return (i >> 4 & 1) * 64 + (i >> 1 & 7) * 8 + ((i >> 5) ^ y) * 2 + (i & 1)

    result = dot(chooser(128, 128, source), result).astype(BF)
    for k in range(Y):
        out_ref[k] = result[k * 32 : k * 32 + 32]


def two_rows(vec):
    high = vec.astype(BF).astype(F32)
    return jnp.concatenate([high, vec - high, jnp.zeros((6, vec.shape[1]), F32)], axis=0)


def two_blocks(rows):
    high = rows.astype(BF).astype(F32)
    return jnp.concatenate([high, rows - high], axis=0)


def merge_body(got_ref, hop_ref, b1_ref, b3_ref, out_ref):
    total = got_ref[0:2].astype(F32)
    for i in range(1, 16):
        total = total + got_ref[2 * i : 2 * i + 2].astype(F32)
    low, high = total[0, :128], total[1, :128]
    wide_low = jnp.concatenate([low[:64], low[64:]], axis=1)
    wide_high = jnp.concatenate([high[:64], high[64:]], axis=1)
    cols = jnp.concatenate(
        [piece[:, j * 64 : j * 64 + 64] for j in range(4) for piece in (wide_low, wide_high)],
        axis=1,
    )
    rows = weave(
        jnp.concatenate([low[i * 32 : i * 32 + 32] for i in range(4)], axis=1),
        jnp.concatenate([high[i * 32 : i * 32 + 32] for i in range(4)], axis=1),
    )
    out_ref[:, :512] = jnp.where(x_is_last(), rows, cols).astype(BF)
    pick = chooser(64, 64, lambda i: (i >> 1 & 3) * 16 + (i >> 3) * 2 + (i & 1))
    blocks = [hop_ref[0], b1_ref[...], hop_ref[2], b3_ref[...]]
    for f in range(2):
        rows = jnp.concatenate([block[f * 16 : f * 16 + 16] for block in blocks], axis=0)
        out_ref[:, 512 + f * 512 : 1024 + f * 512] = dot(pick, rows).astype(BF)
    gains = total[0, 128:] + total[1, 128:]
    gains = two_blocks(unpair(gains))
    out_ref[:, 1536:] = jnp.concatenate([gains] * ZL, axis=0).astype(BF)


def unpair(rows):
    return jnp.concatenate(
        [rows[2 * i : 2 * i + 1] + rows[2 * i + 1 : 2 * i + 2] for i in range(4)], axis=0
    )


def split_body(back_ref, hop_ref, rest_ref, last_ref):
    pick = chooser(64, 64, lambda i: (i >> 1 & 7) * 8 + (i >> 4) * 2 + (i & 1))
    for f in range(2):
        rows = dot(pick, back_ref[:, 512 + f * 512 : 1024 + f * 512]).astype(BF)
        hop_ref[f * 16 : f * 16 + 16] = rows[32:48]
        for at, k in enumerate((0, 1, 3)):
            row = at * 32 + f * 16
            rest_ref[row : row + 16] = rows[k * 16 : k * 16 + 16]
    sums = jnp.sum(back_ref[:, :512].astype(F32).reshape(ZL, 8, 512), axis=0)
    grads = sums.astype(BF)
    gains = jnp.sum(back_ref[:, 1536:].astype(F32).reshape(ZL, 8, 128), axis=0)
    gains = two_blocks(gains[0:4] + gains[4:8]).astype(BF)
    for i in range(ZH * X):
        last_ref[i, :, :512] = grads
        last_ref[i, :, 512:] = gains


def tokens_body(rest_ref, two_ref, out_ref):
    y = lax.axis_index("y")
    blocks = jnp.concatenate([rest_ref[0:64], two_ref[...], rest_ref[64:96]], axis=0)

    def source(i):
        return ((i & 3) ^ y) * 32 + (i >> 5 & 1) * 16 + (i >> 2 & 7) * 2 + (i >> 6)

    out_ref[...] = dot(chooser(128, 128, source), blocks).astype(BF)


def end_body(got_ref, qkv_ref, out_ref, gain_ref):
    for x in range(X):
        pair = got_ref[x].astype(F32) + got_ref[X + x].astype(F32)
        if x < 3:
            qkv_ref[:, x * 512 : x * 512 + 512] = pair[:, :512]
        else:
            out_ref[...] = pair[:, :512]
        if x == 0:
            gain_ref[...] = pair[0:4, 512:] + pair[4:8, 512:]


def on_device(tokens, grad_out, gain, w_qkv, w_out):
    row = gain.reshape(1, 512)
    plane = ("x", "y", "c")

    hbm = pl.BlockSpec(memory_space=pltpu.HBM)
    packed = pl.pallas_call(
        pack_body,
        out_shape=jax.ShapeDtypeStruct((256, 640), BF),
        in_specs=[hbm] * 4,
        out_specs=pl.BlockSpec(memory_space=pltpu.VMEM),
        scratch_shapes=[
            pltpu.VMEM((256, 512), BF),
            pltpu.VMEM((8, 1536), BF),
            pltpu.VMEM((8, 512), BF),
            pltpu.SemaphoreType.DMA((4,)),
        ],
        compiler_params=pltpu.CompilerParams(vmem_limit_bytes=40 * 2**20),
    )(tokens.reshape(128, 512), grad_out.reshape(128, 512), w_qkv, w_out)
    moved = exchange(packed.reshape(ZL * Y, 8, 640), ("zl", "y")).reshape(256, 640)
    [sent] = call(weights_body, [((32, 128, 128), BF)], moved)
    weights = exchange(sent, plane)
    [own] = call(rows_body, [((256, 512), BF)], moved)
    far = lax.ppermute(own, "c", SWAP)
    scaled, normed, grads = call(
        norm_body, [((256, 512), F32), ((256, 512), BF), ((256, 512), BF)], own, far, row
    )
    parts, send, keep = call(
        main_body,
        [((32, 136, 128), BF), ((128, 512), BF), ((128, 512), F32)],
        scaled, normed, grads, weights,
    )
    got = exchange(parts, plane)
    dn_far = lax.ppermute(send, "c", SWAP)
    [hop] = call(finish_body, [((Y, 32, 512), BF)], own, keep, dn_far, row)
    [sent] = call(merge_body, [((64, 1664), BF)], got, hop, to_y(hop[1], 1), to_y(hop[3], 3))
    back = exchange(sent.reshape(ZL, 8, 1664), "zl").reshape(64, 1664)
    hop, rest, last = call(
        split_body, [((32, 512), BF), ((96, 512), BF), ((ZH * X, 8, 640), BF)], back
    )
    ends = exchange(last, ("zh", "x"))
    [grad_tokens] = call(tokens_body, [((128, 512), BF)], rest, to_y(hop, 2))
    shard_qkv, shard_out, total = call(
        end_body, [((8, 1536), F32), ((8, 512), F32), ((4, 128), F32)], ends
    )
    return grad_tokens.reshape(1, 2, 64, 512), shard_qkv, shard_out, total.reshape(512)


def solution(mesh):
    inner = Mesh(mesh.devices.reshape(ZH, X, ZL, Y, C), ("zh", "x", "zl", "y", "c"))
    grid = ("zl", "y", "c")
    tok = P(("zh", "x"), grid, None, None)
    return jax.shard_map(
        on_device,
        mesh=inner,
        in_specs=(tok, tok, P(), P(grid, None), P(grid, None)),
        out_specs=(tok, P(grid, None), P(grid, None), P()),
        check_vma=False,
    )
```

```python
import jax
import jax.numpy as jnp
from jax import lax
from jax.experimental import pallas as pl
from jax.experimental.pallas import tpu as pltpu
from jax.sharding import Mesh
from jax.sharding import PartitionSpec as P

EPS = 1e-06
BF = jnp.bfloat16
F32 = jnp.float32

ZH, X, ZL, Y, C = 2, 4, 8, 4, 2
SWAP = [(0, 1), (1, 0)]


def exchange(arr, axes):
    return lax.all_to_all(arr, axes, split_axis=0, concat_axis=0, tiled=True)


def to_y(block, k):
    return lax.ppermute(block, "y", [(i, i ^ k) for i in range(Y)])


def call(body, outs, *args):
    vmem = pl.BlockSpec(memory_space=pltpu.VMEM)
    return pl.pallas_call(
        body,
        out_shape=[jax.ShapeDtypeStruct(shape, kind) for shape, kind in outs],
        in_specs=[vmem] * len(args),
        out_specs=[vmem] * len(outs),
        compiler_params=pltpu.CompilerParams(vmem_limit_bytes=40 * 2**20),
    )(*args)


def dot(a, b, ca=1, cb=0):
    return lax.dot_general(a, b, (((ca,), (cb,)), ((), ())), preferred_element_type=F32)


def chooser(rows, cols, source_of):
    row = lax.broadcasted_iota(jnp.int32, (rows, cols), 0)
    col = lax.broadcasted_iota(jnp.int32, (rows, cols), 1)
    return (col == source_of(row)).astype(F32).astype(BF)


def pack_body(
    tok_ref, grad_ref, wq_ref, wo_ref, out_ref, both_vm, wq_vm, wo_vm, sems
):
    copies = [
        pltpu.make_async_copy(src, dst, sems.at[i])
        for i, (src, dst) in enumerate(
            [
                (tok_ref, both_vm.at[0:128]),
                (grad_ref, both_vm.at[128:256]),
                (wq_ref, wq_vm),
                (wo_ref, wo_vm),
            ]
        )
    ]
    for copy in copies:
        copy.start()
    pick = chooser(
        256, 256, lambda i: (i >> 2 & 1) * 128 + (i & 1) * 64 + (i >> 1 & 1) * 32 + (i >> 3)
    )
    for copy in copies:
        copy.wait()
    out_ref[:, :512] = dot(pick, both_vm[...]).astype(BF)
    x = lax.axis_index("x")
    part = wo_vm[...].astype(F32)
    for i in range(3):
        part = jnp.where(x == i, wq_vm[:, i * 512 : i * 512 + 512].astype(F32), part)
    blocks = jnp.concatenate([part[:, y * 128 : y * 128 + 128] for y in range(Y)], axis=0)
    out_ref[:, 512:] = jnp.concatenate([blocks] * ZL, axis=0).astype(BF)


def halves(arr):
    return arr[:, :64], arr[:, 64:]


def weights_body(moved_ref, sent_ref):
    block = moved_ref[:, 512:].astype(F32)
    (low0, low1), (high0, high1) = halves(block[:128]), halves(block[128:])
    planes = block.reshape(4, 2, 32, 128)
    outs = x_is_last()
    for core, cols in ((0, (low0, high0)), (1, (low1, high1))):
        mine = jnp.where(
            outs, planes[:, core].reshape(128, 128), jnp.concatenate(cols, axis=1)
        ).astype(BF)
        for xy in range(X * Y):
            sent_ref[2 * xy + core] = mine


def rows_body(moved_ref, own_ref):
    pick = chooser(
        256, 256, lambda i: (i >> 1 & 31) * 8 + (i >> 7) * 4 + (i >> 6 & 1) * 2 + (i & 1)
    )
    own_ref[...] = dot(pick, moved_ref[:, :512]).astype(BF)


def norm_body(own_ref, far_ref, gain_ref, scaled_ref, normed_ref, grad_ref):
    own, far = own_ref[...], far_ref[...]
    x_in = jnp.concatenate([own[0:64], far[0:64], own[64:128], far[64:128]], axis=0)
    grad_ref[...] = jnp.concatenate([own[128:192], far[128:192], own[192:], far[192:]], axis=0)
    values = x_in.astype(F32)
    inverse = lax.rsqrt(jnp.mean(values * values, axis=-1, keepdims=True) + EPS)
    scaled = values * inverse
    scaled_ref[...] = scaled
    normed_ref[...] = (scaled * gain_ref[...]).astype(BF)


def x_is_last():
    return lax.axis_index("x") == 3


def weave(first, second):
    rows, cols = first.shape
    blocks = [arr.reshape(rows // 8, 1, 8, cols) for arr in (first, second)]
    return jnp.concatenate(blocks, axis=1).reshape(2 * rows, cols)


def main_body(
    scaled_ref, normed_ref, grad_ref, w_ref, parts_ref, send_ref, keep_ref
):
    lanes = []
    for x in range(3):
        for pair in range(2):
            tops, bots = [], []
            for core in range(2):
                at = x * 8 + pair * 4 + core
                (a0, a1), (b0, b1) = (
                    halves(w_ref[at].astype(F32)),
                    halves(w_ref[at + 2].astype(F32)),
                )
                tops.append(jnp.concatenate([a0, b0], axis=1))
                bots.append(jnp.concatenate([a1, b1], axis=1))
            lanes.append(jnp.concatenate([weave(*tops), weave(*bots)], axis=0).astype(BF))
    wh = jnp.concatenate(lanes, axis=1)
    lanes = [
        weave(w_ref[24 + 2 * y].astype(F32), w_ref[25 + 2 * y].astype(F32)).astype(BF)
        for y in range(Y)
    ]
    wo = jnp.concatenate(lanes, axis=1)

    normed, g_in = normed_ref[...], grad_ref[...]
    qkv = dot(normed, wh).astype(BF)
    ups = dot(g_in, wo, 1, 1).astype(BF)

    lane = lax.broadcasted_iota(jnp.int32, (128, 128), 1)
    first = lane < 64
    zero = jnp.zeros((128, 128), BF)

    def stack(arr):
        return jnp.concatenate([jnp.where(first, arr, zero), jnp.where(first, zero, arr)], axis=0)

    def pile(arr):
        return jnp.concatenate([arr[:, :128], arr[:, 128:]], axis=0)

    atts, dqs, dks, dvs = [], [], [], []
    for f in range(2):
        rows = slice(f * 128, (f + 1) * 128)
        for pair in range(2):
            at = pair * 128
            q = qkv[rows, at : at + 128]
            k2 = stack(qkv[rows, 256 + at : 256 + at + 128])
            v2 = stack(qkv[rows, 512 + at : 512 + at + 128])
            u = ups[rows, at : at + 128]
            scores = dot(q, k2, 1, 1) * 0.125
            dprob = dot(u, v2, 1, 1)
            weights, dscores = [], []
            for head in range(2):
                cols = slice(head * 128, (head + 1) * 128)
                s = scores[:, cols]
                expo = jnp.exp(s - jnp.max(s, axis=-1, keepdims=True))
                probs = expo * (1.0 / jnp.sum(expo, axis=-1, keepdims=True))
                dp = dprob[:, cols]
                weights.append(probs.astype(BF))
                inner = jnp.sum(probs * dp, axis=-1, keepdims=True)
                dscores.append((probs * (dp - inner) * 0.125).astype(BF))
            weight = jnp.concatenate(weights, axis=1)
            dscore = jnp.concatenate(dscores, axis=1)
            atts.append(dot(weight, v2).astype(BF))
            dqs.append(dot(dscore, k2).astype(BF))
            dks.append(dot(pile(dscore), stack(q), 0, 0).astype(BF))
            dvs.append(dot(pile(weight), stack(u), 0, 0).astype(BF))

    def frames(items):
        return [
            jnp.concatenate([items[0], items[2]], axis=0),
            jnp.concatenate([items[1], items[3]], axis=0),
        ]

    att = jnp.concatenate(frames(atts), axis=1)
    dqkv = jnp.concatenate(frames(dqs) + frames(dks) + frames(dvs), axis=1)

    dn = dot(dqkv, wh, 1, 1)
    keep_ref[...] = jnp.concatenate([dn[0:64], dn[128:192]], axis=0)
    send_ref[...] = jnp.concatenate([dn[64:128], dn[192:]], axis=0).astype(BF)

    gg = two_rows(jnp.sum(dn * scaled_ref[...], axis=0, keepdims=True))
    gg = jnp.concatenate([gg[0:2, i * 128 : i * 128 + 128] for i in range(4)], axis=0)

    g_qkv = dot(normed, dqkv, 0, 0).reshape(ZL, Y, 2, 8, 768)
    g_out = dot(att, g_in, 0, 0).reshape(4, Y, 2, 8, 512)
    for yc in range(8):
        block = g_qkv[:, yc // 2, yc % 2].reshape(64, 768)
        for part in range(3):
            at = part * 256
            pieces = [block[:, at : at + 128], block[:, at + 128 : at + 256], gg]
            parts_ref[part * 8 + yc] = jnp.concatenate(pieces, axis=0).astype(BF)
        block = g_out[:, yc // 2, yc % 2].reshape(32, 512)
        pieces = [block[:, i * 128 : i * 128 + 128] for i in range(4)] + [gg]
        parts_ref[24 + yc] = jnp.concatenate(pieces, axis=0).astype(BF)


def finish_body(own_ref, keep_ref, far_ref, gain_ref, out_ref):
    gain = gain_ref[...]
    values = own_ref[0:128, :].astype(F32)
    inverse = lax.rsqrt(jnp.mean(values * values, axis=-1, keepdims=True) + EPS)
    scaled = values * inverse
    ds = (keep_ref[...] + far_ref[...].astype(F32)) * gain
    inner = jnp.mean(ds * scaled, axis=-1, keepdims=True)
    result = (own_ref[128:256, :].astype(F32) + inverse * (ds - scaled * inner)).astype(BF)
    y = lax.axis_index("y")

    def source(i):
        return (i >> 4 & 1) * 64 + (i >> 1 & 7) * 8 + ((i >> 5) ^ y) * 2 + (i & 1)

    result = dot(chooser(128, 128, source), result).astype(BF)
    for k in range(Y):
        out_ref[k] = result[k * 32 : k * 32 + 32]


def two_rows(vec):
    high = vec.astype(BF).astype(F32)
    return jnp.concatenate([high, vec - high, jnp.zeros((6, vec.shape[1]), F32)], axis=0)


def two_blocks(rows):
    high = rows.astype(BF).astype(F32)
    return jnp.concatenate([high, rows - high], axis=0)


def merge_body(got_ref, hop_ref, b1_ref, b3_ref, out_ref):
    total = got_ref[0:2].astype(F32)
    for i in range(1, 16):
        total = total + got_ref[2 * i : 2 * i + 2].astype(F32)
    low, high = total[0, :128], total[1, :128]
    wide_low = jnp.concatenate([low[:64], low[64:]], axis=1)
    wide_high = jnp.concatenate([high[:64], high[64:]], axis=1)
    cols = jnp.concatenate(
        [piece[:, j * 64 : j * 64 + 64] for j in range(4) for piece in (wide_low, wide_high)],
        axis=1,
    )
    rows = weave(
        jnp.concatenate([low[i * 32 : i * 32 + 32] for i in range(4)], axis=1),
        jnp.concatenate([high[i * 32 : i * 32 + 32] for i in range(4)], axis=1),
    )
    out_ref[:, :512] = jnp.where(x_is_last(), rows, cols).astype(BF)
    pick = chooser(64, 64, lambda i: (i >> 1 & 3) * 16 + (i >> 3) * 2 + (i & 1))
    blocks = [hop_ref[0], b1_ref[...], hop_ref[2], b3_ref[...]]
    for f in range(2):
        rows = jnp.concatenate([block[f * 16 : f * 16 + 16] for block in blocks], axis=0)
        out_ref[:, 512 + f * 512 : 1024 + f * 512] = dot(pick, rows).astype(BF)
    gains = total[0, 128:] + total[1, 128:]
    gains = two_blocks(unpair(gains))
    out_ref[:, 1536:] = jnp.concatenate([gains] * ZL, axis=0).astype(BF)


def unpair(rows):
    return jnp.concatenate(
        [rows[2 * i : 2 * i + 1] + rows[2 * i + 1 : 2 * i + 2] for i in range(4)], axis=0
    )


def split_body(back_ref, hop_ref, rest_ref, last_ref):
    pick = chooser(64, 64, lambda i: (i >> 1 & 7) * 8 + (i >> 4) * 2 + (i & 1))
    for f in range(2):
        rows = dot(pick, back_ref[:, 512 + f * 512 : 1024 + f * 512]).astype(BF)
        hop_ref[f * 16 : f * 16 + 16] = rows[32:48]
        for at, k in enumerate((0, 1, 3)):
            row = at * 32 + f * 16
            rest_ref[row : row + 16] = rows[k * 16 : k * 16 + 16]
    sums = jnp.sum(back_ref[:, :512].astype(F32).reshape(ZL, 8, 512), axis=0)
    last_ref[:, :512] = sums.astype(BF)
    gains = jnp.sum(back_ref[:, 1536:].astype(F32).reshape(ZL, 8, 128), axis=0)
    last_ref[:, 512:] = two_blocks(gains[0:4] + gains[4:8]).astype(BF)


def pair_body(last_ref, far_ref, sent_ref, gain_ref):
    total = last_ref[...].astype(F32) + far_ref[...].astype(F32)
    grads = total[:, :512].astype(BF)
    for x in range(X):
        sent_ref[x] = grads
    gain_ref[...] = total[0:4, 512:] + total[4:8, 512:]


def tokens_body(rest_ref, two_ref, out_ref):
    y = lax.axis_index("y")
    blocks = jnp.concatenate([rest_ref[0:64], two_ref[...], rest_ref[64:96]], axis=0)

    def source(i):
        return ((i & 3) ^ y) * 32 + (i >> 5 & 1) * 16 + (i >> 2 & 7) * 2 + (i >> 6)

    out_ref[...] = dot(chooser(128, 128, source), blocks).astype(BF)


def end_body(got_ref, qkv_ref, out_ref):
    for x in range(3):
        qkv_ref[:, x * 512 : x * 512 + 512] = got_ref[x].astype(F32)
    out_ref[...] = got_ref[3].astype(F32)


def on_device(tokens, grad_out, gain, w_qkv, w_out):
    row = gain.reshape(1, 512)
    plane = ("x", "y", "c")

    hbm = pl.BlockSpec(memory_space=pl.ANY)
    packed = pl.pallas_call(
        pack_body,
        out_shape=jax.ShapeDtypeStruct((256, 640), BF),
        in_specs=[hbm] * 4,
        out_specs=pl.BlockSpec(memory_space=pltpu.VMEM),
        scratch_shapes=[
            pltpu.VMEM((256, 512), BF),
            pltpu.VMEM((8, 1536), BF),
            pltpu.VMEM((8, 512), BF),
            pltpu.SemaphoreType.DMA((4,)),
        ],
        compiler_params=pltpu.CompilerParams(vmem_limit_bytes=60 * 2**20),
    )(tokens.reshape(128, 512), grad_out.reshape(128, 512), w_qkv, w_out)
    moved = exchange(packed.reshape(ZL * Y, 8, 640), ("zl", "y")).reshape(256, 640)
    [sent] = call(weights_body, [((32, 128, 128), BF)], moved)
    weights = exchange(sent, plane)
    [own] = call(rows_body, [((256, 512), BF)], moved)
    far = lax.ppermute(own, "c", SWAP)
    scaled, normed, grads = call(
        norm_body, [((256, 512), F32), ((256, 512), BF), ((256, 512), BF)], own, far, row
    )
    parts, send, keep = call(
        main_body,
        [((32, 136, 128), BF), ((128, 512), BF), ((128, 512), F32)],
        scaled, normed, grads, weights,
    )
    got = exchange(parts, plane)
    dn_far = lax.ppermute(send, "c", SWAP)
    [hop] = call(finish_body, [((Y, 32, 512), BF)], own, keep, dn_far, row)
    [sent] = call(merge_body, [((64, 1664), BF)], got, hop, to_y(hop[1], 1), to_y(hop[3], 3))
    back = exchange(sent.reshape(ZL, 8, 1664), "zl").reshape(64, 1664)
    hop, rest, last = call(
        split_body, [((32, 512), BF), ((96, 512), BF), ((8, 640), BF)], back
    )
    last_far = lax.ppermute(last, "zh", SWAP)
    [grad_tokens] = call(tokens_body, [((128, 512), BF)], rest, to_y(hop, 2))
    sent, total = call(pair_body, [((X, 8, 512), BF), ((4, 128), F32)], last, last_far)
    ends = exchange(sent, "x")
    shard_qkv, shard_out = call(end_body, [((8, 1536), F32), ((8, 512), F32)], ends)
    return grad_tokens.reshape(1, 2, 64, 512), shard_qkv, shard_out, total.reshape(512)


def solution(mesh):
    inner = Mesh(mesh.devices.reshape(ZH, X, ZL, Y, C), ("zh", "x", "zl", "y", "c"))
    grid = ("zl", "y", "c")
    tok = P(("zh", "x"), grid, None, None)
    return jax.shard_map(
        on_device,
        mesh=inner,
        in_specs=(tok, tok, P(), P(grid, None), P(grid, None)),
        out_specs=(tok, P(grid, None), P(grid, None), P()),
        check_vma=False,
    )
```

```python
import jax
import jax.numpy as jnp
from jax import lax
from jax.experimental import pallas as pl
from jax.experimental.pallas import tpu as pltpu
from jax.sharding import Mesh
from jax.sharding import PartitionSpec as P

EPS = 1e-06
BF = jnp.bfloat16
F32 = jnp.float32

ZH, X, ZL, Y, C = 2, 4, 8, 4, 2
SWAP = [(0, 1), (1, 0)]


def exchange(arr, axes):
    return lax.all_to_all(arr, axes, split_axis=0, concat_axis=0, tiled=True)


def flip(block, axis, count, bits):
    return lax.ppermute(block, axis, [(i, i ^ bits) for i in range(count)])


def call(body, outs, *args):
    vmem = pl.BlockSpec(memory_space=pltpu.VMEM)
    return pl.pallas_call(
        body,
        out_shape=[jax.ShapeDtypeStruct(shape, kind) for shape, kind in outs],
        in_specs=[vmem] * len(args),
        out_specs=[vmem] * len(outs),
        compiler_params=pltpu.CompilerParams(vmem_limit_bytes=40 * 2**20),
    )(*args)


def dot(a, b, ca=1, cb=0):
    return lax.dot_general(a, b, (((ca,), (cb,)), ((), ())), preferred_element_type=F32)


def chooser(rows, cols, source_of):
    row = lax.broadcasted_iota(jnp.int32, (rows, cols), 0)
    col = lax.broadcasted_iota(jnp.int32, (rows, cols), 1)
    return (col == source_of(row)).astype(F32).astype(BF)


def pack_body(
    tok_ref, grad_ref, wq_ref, wo_ref, out_ref, both_vm, wq_vm, wo_vm, sems
):
    copies = [
        pltpu.make_async_copy(src, dst, sems.at[i])
        for i, (src, dst) in enumerate(
            [
                (tok_ref, both_vm.at[0:128]),
                (grad_ref, both_vm.at[128:256]),
                (wq_ref, wq_vm),
                (wo_ref, wo_vm),
            ]
        )
    ]
    for copy in copies:
        copy.start()
    pick = chooser(
        256, 256, lambda i: (i >> 2 & 1) * 128 + (i & 1) * 64 + (i >> 1 & 1) * 32 + (i >> 3)
    )
    for copy in copies:
        copy.wait()
    out_ref[:, :512] = dot(pick, both_vm[...]).astype(BF)
    x = lax.axis_index("x")
    part = wo_vm[...].astype(F32)
    for i in range(3):
        part = jnp.where(x == i, wq_vm[:, i * 512 : i * 512 + 512].astype(F32), part)
    blocks = jnp.concatenate([part[:, y * 128 : y * 128 + 128] for y in range(Y)], axis=0)
    out_ref[:, 512:] = jnp.concatenate([blocks] * ZL, axis=0).astype(BF)


def halves(arr):
    return arr[:, :64], arr[:, 64:]


def weights_body(moved_ref, sent_ref):
    block = moved_ref[:, 512:].astype(F32)
    (low0, low1), (high0, high1) = halves(block[:128]), halves(block[128:])
    planes = block.reshape(4, 2, 32, 128)
    outs = x_is_last()
    for core, cols in ((0, (low0, high0)), (1, (low1, high1))):
        mine = jnp.where(
            outs, planes[:, core].reshape(128, 128), jnp.concatenate(cols, axis=1)
        ).astype(BF)
        for xy in range(X * Y):
            sent_ref[2 * xy + core] = mine


def rows_body(moved_ref, own_ref):
    pick = chooser(
        256, 256, lambda i: (i >> 1 & 31) * 8 + (i >> 7) * 4 + (i >> 6 & 1) * 2 + (i & 1)
    )
    own_ref[...] = dot(pick, moved_ref[:, :512]).astype(BF)


def norm_body(own_ref, far_ref, gain_ref, scaled_ref, normed_ref, grad_ref):
    own, far = own_ref[...], far_ref[...]
    x_in = jnp.concatenate([own[0:64], far[0:64], own[64:128], far[64:128]], axis=0)
    grad_ref[...] = jnp.concatenate([own[128:192], far[128:192], own[192:], far[192:]], axis=0)
    values = x_in.astype(F32)
    inverse = lax.rsqrt(jnp.mean(values * values, axis=-1, keepdims=True) + EPS)
    scaled = values * inverse
    scaled_ref[...] = scaled
    normed_ref[...] = (scaled * gain_ref[...]).astype(BF)


def x_is_last():
    return lax.axis_index("x") == 3


def weave(first, second):
    rows, cols = first.shape
    blocks = [arr.reshape(rows // 8, 1, 8, cols) for arr in (first, second)]
    return jnp.concatenate(blocks, axis=1).reshape(2 * rows, cols)


def main_body(
    scaled_ref, normed_ref, grad_ref, w_ref, parts_ref, send_ref, keep_ref
):
    lanes = []
    for x in range(3):
        for pair in range(2):
            tops, bots = [], []
            for core in range(2):
                at = x * 8 + pair * 4 + core
                (a0, a1), (b0, b1) = (
                    halves(w_ref[at].astype(F32)),
                    halves(w_ref[at + 2].astype(F32)),
                )
                tops.append(jnp.concatenate([a0, b0], axis=1))
                bots.append(jnp.concatenate([a1, b1], axis=1))
            lanes.append(jnp.concatenate([weave(*tops), weave(*bots)], axis=0).astype(BF))
    wh = jnp.concatenate(lanes, axis=1)
    lanes = [
        weave(w_ref[24 + 2 * y].astype(F32), w_ref[25 + 2 * y].astype(F32)).astype(BF)
        for y in range(Y)
    ]
    wo = jnp.concatenate(lanes, axis=1)

    normed, g_in = normed_ref[...], grad_ref[...]
    qkv = dot(normed, wh).astype(BF)
    ups = dot(g_in, wo, 1, 1).astype(BF)

    lane = lax.broadcasted_iota(jnp.int32, (128, 128), 1)
    first = lane < 64
    zero = jnp.zeros((128, 128), BF)

    def stack(arr):
        return jnp.concatenate([jnp.where(first, arr, zero), jnp.where(first, zero, arr)], axis=0)

    def pile(arr):
        return jnp.concatenate([arr[:, :128], arr[:, 128:]], axis=0)

    atts, dqs, dks, dvs = [], [], [], []
    for f in range(2):
        rows = slice(f * 128, (f + 1) * 128)
        for pair in range(2):
            at = pair * 128
            q = qkv[rows, at : at + 128]
            k2 = stack(qkv[rows, 256 + at : 256 + at + 128])
            v2 = stack(qkv[rows, 512 + at : 512 + at + 128])
            u = ups[rows, at : at + 128]
            scores = dot(q, k2, 1, 1) * 0.125
            dprob = dot(u, v2, 1, 1)
            weights, dscores = [], []
            for head in range(2):
                cols = slice(head * 128, (head + 1) * 128)
                s = scores[:, cols]
                expo = jnp.exp(s - jnp.max(s, axis=-1, keepdims=True))
                probs = expo * (1.0 / jnp.sum(expo, axis=-1, keepdims=True))
                dp = dprob[:, cols]
                weights.append(probs.astype(BF))
                inner = jnp.sum(probs * dp, axis=-1, keepdims=True)
                dscores.append((probs * (dp - inner) * 0.125).astype(BF))
            weight = jnp.concatenate(weights, axis=1)
            dscore = jnp.concatenate(dscores, axis=1)
            atts.append(dot(weight, v2).astype(BF))
            dqs.append(dot(dscore, k2).astype(BF))
            dks.append(dot(pile(dscore), stack(q), 0, 0).astype(BF))
            dvs.append(dot(pile(weight), stack(u), 0, 0).astype(BF))

    def frames(items):
        return [
            jnp.concatenate([items[0], items[2]], axis=0),
            jnp.concatenate([items[1], items[3]], axis=0),
        ]

    att = jnp.concatenate(frames(atts), axis=1)
    dqkv = jnp.concatenate(frames(dqs) + frames(dks) + frames(dvs), axis=1)

    dn = dot(dqkv, wh, 1, 1)
    keep_ref[...] = jnp.concatenate([dn[0:64], dn[128:192]], axis=0)
    send_ref[...] = jnp.concatenate([dn[64:128], dn[192:]], axis=0).astype(BF)

    gg = two_rows(jnp.sum(dn * scaled_ref[...], axis=0, keepdims=True))
    gg = jnp.concatenate([gg[0:2, i * 128 : i * 128 + 128] for i in range(4)], axis=0)

    g_qkv = dot(normed, dqkv, 0, 0).reshape(ZL, Y, 2, 8, 768)
    g_out = dot(att, g_in, 0, 0).reshape(4, Y, 2, 8, 512)
    for yc in range(8):
        block = g_qkv[:, yc // 2, yc % 2].reshape(64, 768)
        for part in range(3):
            at = part * 256
            pieces = [block[:, at : at + 128], block[:, at + 128 : at + 256], gg]
            parts_ref[part * 8 + yc] = jnp.concatenate(pieces, axis=0).astype(BF)
        block = g_out[:, yc // 2, yc % 2].reshape(32, 512)
        pieces = [block[:, i * 128 : i * 128 + 128] for i in range(4)] + [gg]
        parts_ref[24 + yc] = jnp.concatenate(pieces, axis=0).astype(BF)


def finish_body(own_ref, keep_ref, far_ref, gain_ref, out_ref):
    gain = gain_ref[...]
    values = own_ref[0:128, :].astype(F32)
    inverse = lax.rsqrt(jnp.mean(values * values, axis=-1, keepdims=True) + EPS)
    scaled = values * inverse
    ds = (keep_ref[...] + far_ref[...].astype(F32)) * gain
    inner = jnp.mean(ds * scaled, axis=-1, keepdims=True)
    result = (own_ref[128:256, :].astype(F32) + inverse * (ds - scaled * inner)).astype(BF)
    out = None
    for half in range(2):

        def source(i, half=half):
            row = (i >> 2 & 1) * 64 + (i >> 3) * 2 + (i >> 1 & 1)
            return jnp.where((i & 1) == half, row, -1)

        part = dot(chooser(256, 128, source), result[:, half * 256 : half * 256 + 256])
        out = part if out is None else out + part
    out_ref[...] = out.astype(BF)


def two_rows(vec):
    high = vec.astype(BF).astype(F32)
    return jnp.concatenate([high, vec - high, jnp.zeros((6, vec.shape[1]), F32)], axis=0)


def two_blocks(rows):
    high = rows.astype(BF).astype(F32)
    return jnp.concatenate([high, rows - high], axis=0)


def merge_body(got_ref, out_ref):
    total = got_ref[0:2].astype(F32)
    for i in range(1, 16):
        total = total + got_ref[2 * i : 2 * i + 2].astype(F32)
    low, high = total[0, :128], total[1, :128]
    wide_low = jnp.concatenate([low[:64], low[64:]], axis=1)
    wide_high = jnp.concatenate([high[:64], high[64:]], axis=1)
    cols = jnp.concatenate(
        [piece[:, j * 64 : j * 64 + 64] for j in range(4) for piece in (wide_low, wide_high)],
        axis=1,
    )
    rows = weave(
        jnp.concatenate([low[i * 32 : i * 32 + 32] for i in range(4)], axis=1),
        jnp.concatenate([high[i * 32 : i * 32 + 32] for i in range(4)], axis=1),
    )
    gains = two_blocks(unpair(total[0, 128:] + total[1, 128:]))
    grads = jnp.where(x_is_last(), rows, cols).astype(BF)
    gains = jnp.concatenate([gains] * ZL, axis=0).astype(BF)
    for zh in range(ZH):
        out_ref[zh * 64 : zh * 64 + 64, :512] = grads
        out_ref[zh * 64 : zh * 64 + 64, 512:] = gains


def unpair(rows):
    return jnp.concatenate(
        [rows[2 * i : 2 * i + 1] + rows[2 * i + 1 : 2 * i + 2] for i in range(4)], axis=0
    )


def split_body(back_ref, last_ref, gain_ref):
    sums = jnp.sum(back_ref[...].astype(F32).reshape(ZH * ZL, 8, 640), axis=0)
    last_ref[...] = sums[:, :512].astype(BF)
    gain_ref[...] = sums[0:4, 512:] + sums[4:8, 512:]


def tokens_body(back_ref, out_ref):
    for half in range(2):

        def source(i, half=half):
            return (i & 31) * 8 + (i >> 5 & 1) * 4 + (i >> 6) * 2 + half

        rows = dot(chooser(128, 256, source), back_ref[...])
        out_ref[:, half * 256 : half * 256 + 256] = rows.astype(BF)


def both_body(one_ref, two_ref, out_ref):
    out_ref[:, :512] = one_ref[...]
    out_ref[:, 512:] = two_ref[...]


def end_body(near_ref, far_ref, qkv_ref, out_ref):
    x = lax.axis_index("x")
    near, far = near_ref[...].astype(F32), far_ref[...].astype(F32)
    parts = [near[:, :512], near[:, 512:], far[:, 512:], far[:, :512]]
    for part in range(X):
        total = parts[3]
        for k in range(3):
            total = jnp.where((x ^ k) == part, parts[k], total)
        if part < 3:
            qkv_ref[:, part * 512 : part * 512 + 512] = total
        else:
            out_ref[...] = total


def on_device(tokens, grad_out, gain, w_qkv, w_out):
    row = gain.reshape(1, 512)
    plane = ("x", "y", "c")

    hbm = pl.BlockSpec(memory_space=pl.ANY)
    packed = pl.pallas_call(
        pack_body,
        out_shape=jax.ShapeDtypeStruct((256, 640), BF),
        in_specs=[hbm] * 4,
        out_specs=pl.BlockSpec(memory_space=pltpu.VMEM),
        scratch_shapes=[
            pltpu.VMEM((256, 512), BF),
            pltpu.VMEM((8, 1536), BF),
            pltpu.VMEM((8, 512), BF),
            pltpu.SemaphoreType.DMA((4,)),
        ],
        compiler_params=pltpu.CompilerParams(vmem_limit_bytes=60 * 2**20),
    )(tokens.reshape(128, 512), grad_out.reshape(128, 512), w_qkv, w_out)
    moved = exchange(packed.reshape(ZL * Y, 8, 640), ("zl", "y")).reshape(256, 640)
    [sent] = call(weights_body, [((32, 128, 128), BF)], moved)
    weights = exchange(sent, plane)
    [own] = call(rows_body, [((256, 512), BF)], moved)
    far = lax.ppermute(own, "c", SWAP)
    scaled, normed, grads = call(
        norm_body, [((256, 512), F32), ((256, 512), BF), ((256, 512), BF)], own, far, row
    )
    parts, send, keep = call(
        main_body,
        [((32, 136, 128), BF), ((128, 512), BF), ((128, 512), F32)],
        scaled, normed, grads, weights,
    )
    got = exchange(parts, plane)
    dn_far = lax.ppermute(send, "c", SWAP)
    [result] = call(finish_body, [((256, 256), BF)], own, keep, dn_far, row)
    [sent] = call(merge_body, [((128, 640), BF)], got)
    back = exchange(sent.reshape(ZH * ZL, 8, 640), ("zh", "zl"))
    back, result = lax.optimization_barrier((back, result))
    result = exchange(result.reshape(ZL * Y, 8, 256), ("zl", "y")).reshape(256, 256)
    last, total = call(split_body, [((8, 512), BF), ((4, 128), F32)], back.reshape(128, 640))
    [near] = call(both_body, [((8, 1024), BF)], last, flip(last, "x", X, 1))
    shard_qkv, shard_out = call(
        end_body, [((8, 1536), F32), ((8, 512), F32)], near, flip(near, "x", X, 3)
    )
    [grad_tokens] = call(tokens_body, [((128, 512), BF)], result)
    return grad_tokens.reshape(1, 2, 64, 512), shard_qkv, shard_out, total.reshape(512)


def solution(mesh):
    inner = Mesh(mesh.devices.reshape(ZH, X, ZL, Y, C), ("zh", "x", "zl", "y", "c"))
    grid = ("zl", "y", "c")
    tok = P(("zh", "x"), grid, None, None)
    return jax.shard_map(
        on_device,
        mesh=inner,
        in_specs=(tok, tok, P(), P(grid, None), P(grid, None)),
        out_specs=(tok, P(grid, None), P(grid, None), P()),
        check_vma=False,
    )
```

```python
import jax
import jax.numpy as jnp
from jax import lax
from jax.experimental import pallas as pl
from jax.experimental.pallas import tpu as pltpu
from jax.sharding import Mesh
from jax.sharding import PartitionSpec as P

EPS = 1e-06
BF = jnp.bfloat16
F32 = jnp.float32

ZH, X, ZL, Y, C = 2, 4, 8, 4, 2
SWAP = [(0, 1), (1, 0)]


def exchange(arr, axes):
    return lax.all_to_all(arr, axes, split_axis=0, concat_axis=0, tiled=True)


def to_y(block, k):
    return lax.ppermute(block, "y", [(i, i ^ k) for i in range(Y)])


def call(body, outs, *args, first_in_hbm=False, scratch=()):
    vmem = pl.BlockSpec(memory_space=pltpu.VMEM)
    out_specs = [vmem] * len(outs)
    if first_in_hbm:
        out_specs[0] = pl.BlockSpec(memory_space=pl.ANY)
    return pl.pallas_call(
        body,
        out_shape=[jax.ShapeDtypeStruct(shape, kind) for shape, kind in outs],
        in_specs=[vmem] * len(args),
        out_specs=out_specs,
        scratch_shapes=list(scratch),
        compiler_params=pltpu.CompilerParams(vmem_limit_bytes=40 * 2**20),
    )(*args)


def dot(a, b, ca=1, cb=0):
    return lax.dot_general(a, b, (((ca,), (cb,)), ((), ())), preferred_element_type=F32)


def chooser(rows, cols, source_of):
    row = lax.broadcasted_iota(jnp.int32, (rows, cols), 0)
    col = lax.broadcasted_iota(jnp.int32, (rows, cols), 1)
    return (col == source_of(row)).astype(F32).astype(BF)


def pack_body(
    tok_ref, grad_ref, wq_ref, wo_ref, out_ref, both_vm, wq_vm, wo_vm, sems
):
    copies = [
        pltpu.make_async_copy(src, dst, sems.at[i])
        for i, (src, dst) in enumerate(
            [
                (tok_ref, both_vm.at[0:128]),
                (grad_ref, both_vm.at[128:256]),
                (wq_ref, wq_vm),
                (wo_ref, wo_vm),
            ]
        )
    ]
    for copy in copies:
        copy.start()
    pick = chooser(
        256, 256, lambda i: (i >> 2 & 1) * 128 + (i & 1) * 64 + (i >> 1 & 1) * 32 + (i >> 3)
    )
    for copy in copies:
        copy.wait()
    out_ref[:, :512] = dot(pick, both_vm[...]).astype(BF)
    x = lax.axis_index("x")
    part = wo_vm[...].astype(F32)
    for i in range(3):
        part = jnp.where(x == i, wq_vm[:, i * 512 : i * 512 + 512].astype(F32), part)
    blocks = jnp.concatenate([part[:, y * 128 : y * 128 + 128] for y in range(Y)], axis=0)
    out_ref[:, 512:] = jnp.concatenate([blocks] * ZL, axis=0).astype(BF)


def halves(arr):
    return arr[:, :64], arr[:, 64:]


def weights_body(moved_ref, sent_ref, pair_vm, sems):
    block = moved_ref[:, 512:].astype(F32)
    (low0, low1), (high0, high1) = halves(block[:128]), halves(block[128:])
    planes = block.reshape(4, 2, 32, 128)
    outs = x_is_last()
    for core, cols in ((0, (low0, high0)), (1, (low1, high1))):
        mine = jnp.where(
            outs, planes[:, core].reshape(128, 128), jnp.concatenate(cols, axis=1)
        ).astype(BF)
        pair_vm[core] = mine
    copies = [
        pltpu.make_async_copy(pair_vm, sent_ref.at[2 * xy : 2 * xy + 2], sems.at[xy])
        for xy in range(X * Y)
    ]
    for copy in copies:
        copy.start()
    for copy in copies:
        copy.wait()


def rows_body(moved_ref, own_ref):
    pick = chooser(
        256, 256, lambda i: (i >> 1 & 31) * 8 + (i >> 7) * 4 + (i >> 6 & 1) * 2 + (i & 1)
    )
    own_ref[...] = dot(pick, moved_ref[:, :512]).astype(BF)


def norm_body(own_ref, far_ref, gain_ref, scaled_ref, normed_ref, flipped_ref, grad_ref):
    own, far = own_ref[...], far_ref[...]
    x_in = jnp.concatenate([own[0:64], far[0:64], own[64:128], far[64:128]], axis=0)
    grad_ref[...] = jnp.concatenate([own[128:192], far[128:192], own[192:], far[192:]], axis=0)
    values = x_in.astype(F32)
    inverse = lax.rsqrt(jnp.mean(values * values, axis=-1, keepdims=True) + EPS)
    scaled = values * inverse
    scaled_ref[...] = scaled
    normed = scaled * gain_ref[...]
    normed_ref[...] = normed.astype(BF)
    flipped_ref[...] = normed.T.astype(BF)


def x_is_last():
    return lax.axis_index("x") == 3


def weave(first, second):
    rows, cols = first.shape
    blocks = [arr.reshape(rows // 8, 1, 8, cols) for arr in (first, second)]
    return jnp.concatenate(blocks, axis=1).reshape(2 * rows, cols)


def main_body(
    scaled_ref, normed_ref, flipped_ref, grad_ref, w_ref,
    parts_ref, send_ref, keep_ref, parts_vm, sems,
):
    lanes = []
    for x in range(3):
        for pair in range(2):
            tops, bots = [], []
            for core in range(2):
                at = x * 8 + pair * 4 + core
                (a0, a1), (b0, b1) = (
                    halves(w_ref[at].astype(F32)),
                    halves(w_ref[at + 2].astype(F32)),
                )
                tops.append(jnp.concatenate([a0, b0], axis=1))
                bots.append(jnp.concatenate([a1, b1], axis=1))
            lanes.append(jnp.concatenate([weave(*tops), weave(*bots)], axis=0).astype(BF))
    wh = jnp.concatenate(lanes, axis=1)
    lanes = [
        weave(w_ref[24 + 2 * y].astype(F32), w_ref[25 + 2 * y].astype(F32)).astype(BF)
        for y in range(Y)
    ]
    wo = jnp.concatenate(lanes, axis=1)

    normed, g_in = normed_ref[...], grad_ref[...]
    qkv = dot(normed, wh).astype(BF)
    ups = dot(g_in, wo, 1, 1).astype(BF)

    lane = lax.broadcasted_iota(jnp.int32, (128, 128), 1)
    first = lane < 64
    zero = jnp.zeros((128, 128), BF)

    def stack(arr):
        return jnp.concatenate([jnp.where(first, arr, zero), jnp.where(first, zero, arr)], axis=0)

    def pile(arr):
        return jnp.concatenate([arr[:, :128], arr[:, 128:]], axis=0)

    atts, dqs, dks, dvs = [], [], [], []
    for f in range(2):
        rows = slice(f * 128, (f + 1) * 128)
        for pair in range(2):
            at = pair * 128
            q = qkv[rows, at : at + 128]
            k2 = stack(qkv[rows, 256 + at : 256 + at + 128])
            v2 = stack(qkv[rows, 512 + at : 512 + at + 128])
            u = ups[rows, at : at + 128]
            scores = dot(q, k2, 1, 1) * 0.125
            dprob = dot(u, v2, 1, 1)
            weights, dscores = [], []
            for head in range(2):
                cols = slice(head * 128, (head + 1) * 128)
                s = scores[:, cols]
                expo = jnp.exp(s - jnp.max(s, axis=-1, keepdims=True))
                probs = expo * (1.0 / jnp.sum(expo, axis=-1, keepdims=True))
                dp = dprob[:, cols]
                weights.append(probs.astype(BF))
                inner = jnp.sum(probs * dp, axis=-1, keepdims=True)
                dscores.append((probs * (dp - inner) * 0.125).astype(BF))
            weight = jnp.concatenate(weights, axis=1)
            dscore = jnp.concatenate(dscores, axis=1)
            atts.append(dot(weight, v2).astype(BF))
            dqs.append(dot(dscore, k2).astype(BF))
            dks.append(dot(pile(dscore), stack(q), 0, 0).astype(BF))
            dvs.append(dot(pile(weight), stack(u), 0, 0).astype(BF))

    def frames(items):
        return [
            jnp.concatenate([items[0], items[2]], axis=0),
            jnp.concatenate([items[1], items[3]], axis=0),
        ]

    att = jnp.concatenate(frames(atts), axis=1)
    dqkv = jnp.concatenate(frames(dqs) + frames(dks) + frames(dvs), axis=1)

    dn = dot(dqkv, wh, 1, 1)
    keep_ref[...] = jnp.concatenate([dn[0:64], dn[128:192]], axis=0)
    send_ref[...] = jnp.concatenate([dn[64:128], dn[192:]], axis=0).astype(BF)

    gg = two_rows(jnp.sum(dn * scaled_ref[...], axis=0, keepdims=True))
    gg = jnp.concatenate([gg[0:2, i * 128 : i * 128 + 128] for i in range(4)], axis=0)

    copies = []

    def leave(part):
        at = slice(part * 8, part * 8 + 8)
        copy = pltpu.make_async_copy(parts_vm.at[at], parts_ref.at[at], sems.at[part])
        copy.start()
        copies.append(copy)

    g_out = dot(att, g_in, 0, 0).reshape(4, Y, 2, 8, 512)
    for yc in range(8):
        block = g_out[:, yc // 2, yc % 2].reshape(32, 512)
        pieces = [block[:, i * 128 : i * 128 + 128] for i in range(4)] + [gg]
        parts_vm[24 + yc] = jnp.concatenate(pieces, axis=0).astype(BF)
    leave(3)
    flipped = flipped_ref[...]
    for part in (2, 1, 0):
        g_part = dot(flipped, dqkv[:, part * 256 : part * 256 + 256])
        g_part = g_part.reshape(ZL, Y, 2, 8, 256)
        for yc in range(8):
            block = g_part[:, yc // 2, yc % 2].reshape(64, 256)
            pieces = [block[:, :128], block[:, 128:], gg]
            parts_vm[part * 8 + yc] = jnp.concatenate(pieces, axis=0).astype(BF)
        leave(part)
    for copy in copies:
        copy.wait()


def finish_body(own_ref, keep_ref, far_ref, gain_ref, out_ref):
    gain = gain_ref[...]
    values = own_ref[0:128, :].astype(F32)
    inverse = lax.rsqrt(jnp.mean(values * values, axis=-1, keepdims=True) + EPS)
    scaled = values * inverse
    ds = (keep_ref[...] + far_ref[...].astype(F32)) * gain
    inner = jnp.mean(ds * scaled, axis=-1, keepdims=True)
    result = (own_ref[128:256, :].astype(F32) + inverse * (ds - scaled * inner)).astype(BF)
    y = lax.axis_index("y")

    def source(i):
        return (i >> 4 & 1) * 64 + (i >> 1 & 7) * 8 + ((i >> 5) ^ y) * 2 + (i & 1)

    result = dot(chooser(128, 128, source), result).astype(BF)
    for k in range(Y):
        out_ref[k] = result[k * 32 : k * 32 + 32]


def two_rows(vec):
    high = vec.astype(BF).astype(F32)
    return jnp.concatenate([high, vec - high, jnp.zeros((6, vec.shape[1]), F32)], axis=0)


def two_blocks(rows):
    high = rows.astype(BF).astype(F32)
    return jnp.concatenate([high, rows - high], axis=0)


def merge_body(got_ref, hop_ref, b1_ref, b3_ref, out_ref):
    total = got_ref[0:2].astype(F32)
    for i in range(1, 16):
        total = total + got_ref[2 * i : 2 * i + 2].astype(F32)
    low, high = total[0, :128], total[1, :128]
    wide_low = jnp.concatenate([low[:64], low[64:]], axis=1)
    wide_high = jnp.concatenate([high[:64], high[64:]], axis=1)
    cols = jnp.concatenate(
        [piece[:, j * 64 : j * 64 + 64] for j in range(4) for piece in (wide_low, wide_high)],
        axis=1,
    )
    rows = weave(
        jnp.concatenate([low[i * 32 : i * 32 + 32] for i in range(4)], axis=1),
        jnp.concatenate([high[i * 32 : i * 32 + 32] for i in range(4)], axis=1),
    )
    out_ref[:, :512] = jnp.where(x_is_last(), rows, cols).astype(BF)
    pick = chooser(64, 64, lambda i: (i >> 1 & 3) * 16 + (i >> 3) * 2 + (i & 1))
    blocks = [hop_ref[0], b1_ref[...], hop_ref[2], b3_ref[...]]
    for f in range(2):
        rows = jnp.concatenate([block[f * 16 : f * 16 + 16] for block in blocks], axis=0)
        out_ref[:, 512 + f * 512 : 1024 + f * 512] = dot(pick, rows).astype(BF)
    gains = total[0, 128:] + total[1, 128:]
    gains = two_blocks(unpair(gains))
    out_ref[:, 1536:] = jnp.concatenate([gains] * ZL, axis=0).astype(BF)


def unpair(rows):
    return jnp.concatenate(
        [rows[2 * i : 2 * i + 1] + rows[2 * i + 1 : 2 * i + 2] for i in range(4)], axis=0
    )


def split_body(back_ref, hop_ref, rest_ref, last_ref):
    pick = chooser(64, 64, lambda i: (i >> 1 & 7) * 8 + (i >> 4) * 2 + (i & 1))
    for f in range(2):
        rows = dot(pick, back_ref[:, 512 + f * 512 : 1024 + f * 512]).astype(BF)
        hop_ref[f * 16 : f * 16 + 16] = rows[32:48]
        for at, k in enumerate((0, 1, 3)):
            row = at * 32 + f * 16
            rest_ref[row : row + 16] = rows[k * 16 : k * 16 + 16]
    sums = jnp.sum(back_ref[:, :512].astype(F32).reshape(ZL, 8, 512), axis=0)
    last_ref[:, :512] = sums.astype(BF)
    gains = jnp.sum(back_ref[:, 1536:].astype(F32).reshape(ZL, 8, 128), axis=0)
    last_ref[:, 512:] = two_blocks(gains[0:4] + gains[4:8]).astype(BF)


def pair_body(last_ref, far_ref, sent_ref, gain_ref):
    total = last_ref[...].astype(F32) + far_ref[...].astype(F32)
    grads = total[:, :512].astype(BF)
    for x in range(X):
        sent_ref[x] = grads
    gain_ref[...] = total[0:4, 512:] + total[4:8, 512:]


def tokens_body(rest_ref, two_ref, out_ref):
    y = lax.axis_index("y")
    blocks = jnp.concatenate([rest_ref[0:64], two_ref[...], rest_ref[64:96]], axis=0)

    def source(i):
        return ((i & 3) ^ y) * 32 + (i >> 5 & 1) * 16 + (i >> 2 & 7) * 2 + (i >> 6)

    out_ref[...] = dot(chooser(128, 128, source), blocks).astype(BF)


def end_body(got_ref, qkv_ref, out_ref):
    for x in range(3):
        qkv_ref[:, x * 512 : x * 512 + 512] = got_ref[x].astype(F32)
    out_ref[...] = got_ref[3].astype(F32)


def on_device(tokens, grad_out, gain, w_qkv, w_out):
    row = gain.reshape(1, 512)
    plane = ("x", "y", "c")

    hbm = pl.BlockSpec(memory_space=pl.ANY)
    packed = pl.pallas_call(
        pack_body,
        out_shape=jax.ShapeDtypeStruct((256, 640), BF),
        in_specs=[hbm] * 4,
        out_specs=pl.BlockSpec(memory_space=pltpu.VMEM),
        scratch_shapes=[
            pltpu.VMEM((256, 512), BF),
            pltpu.VMEM((8, 1536), BF),
            pltpu.VMEM((8, 512), BF),
            pltpu.SemaphoreType.DMA((4,)),
        ],
        compiler_params=pltpu.CompilerParams(vmem_limit_bytes=60 * 2**20),
    )(tokens.reshape(128, 512), grad_out.reshape(128, 512), w_qkv, w_out)
    moved = exchange(packed.reshape(ZL * Y, 8, 640), ("zl", "y")).reshape(256, 640)
    [sent] = call(
        weights_body,
        [((32, 128, 128), BF)],
        moved,
        first_in_hbm=True,
        scratch=[pltpu.VMEM((2, 128, 128), BF), pltpu.SemaphoreType.DMA((X * Y,))],
    )
    weights = exchange(sent, plane)
    [own] = call(rows_body, [((256, 512), BF)], moved)
    far = lax.ppermute(own, "c", SWAP)
    scaled, normed, flipped, grads = call(
        norm_body,
        [((256, 512), F32), ((256, 512), BF), ((512, 256), BF), ((256, 512), BF)],
        own, far, row,
    )
    parts, send, keep = call(
        main_body,
        [((32, 136, 128), BF), ((128, 512), BF), ((128, 512), F32)],
        scaled, normed, flipped, grads, weights,
        first_in_hbm=True,
        scratch=[pltpu.VMEM((32, 136, 128), BF), pltpu.SemaphoreType.DMA((4,))],
    )
    got = exchange(parts, plane)
    dn_far = lax.ppermute(send, "c", SWAP)
    [hop] = call(finish_body, [((Y, 32, 512), BF)], own, keep, dn_far, row)
    [sent] = call(merge_body, [((64, 1664), BF)], got, hop, to_y(hop[1], 1), to_y(hop[3], 3))
    back = exchange(sent.reshape(ZL, 8, 1664), "zl").reshape(64, 1664)
    hop, rest, last = call(
        split_body, [((32, 512), BF), ((96, 512), BF), ((8, 640), BF)], back
    )
    last_far = lax.ppermute(last, "zh", SWAP)
    [grad_tokens] = call(tokens_body, [((128, 512), BF)], rest, to_y(hop, 2))
    sent, total = call(pair_body, [((X, 8, 512), BF), ((4, 128), F32)], last, last_far)
    ends = exchange(sent, "x")
    shard_qkv, shard_out = call(end_body, [((8, 1536), F32), ((8, 512), F32)], ends)
    return grad_tokens.reshape(1, 2, 64, 512), shard_qkv, shard_out, total.reshape(512)


def solution(mesh):
    inner = Mesh(mesh.devices.reshape(ZH, X, ZL, Y, C), ("zh", "x", "zl", "y", "c"))
    grid = ("zl", "y", "c")
    tok = P(("zh", "x"), grid, None, None)
    return jax.shard_map(
        on_device,
        mesh=inner,
        in_specs=(tok, tok, P(), P(grid, None), P(grid, None)),
        out_specs=(tok, P(grid, None), P(grid, None), P()),
        check_vma=False,
    )
```

```python
import jax
import jax.numpy as jnp
from jax import lax
from jax.experimental import pallas as pl
from jax.experimental.pallas import tpu as pltpu
from jax.sharding import Mesh
from jax.sharding import PartitionSpec as P

EPS = 1e-06
BF = jnp.bfloat16
F32 = jnp.float32

ZH, X, ZL, Y, C = 2, 4, 8, 4, 2
SWAP = [(0, 1), (1, 0)]


def exchange(arr, axes):
    return lax.all_to_all(arr, axes, split_axis=0, concat_axis=0, tiled=True)


def to_y(block, k):
    return lax.ppermute(block, ("yh", "yl"), [(i, i ^ k) for i in range(Y)])


def y_index():
    return lax.axis_index("yh") * 2 + lax.axis_index("yl")


def call(body, outs, *args, first_in_hbm=False, scratch=()):
    vmem = pl.BlockSpec(memory_space=pltpu.VMEM)
    out_specs = [vmem] * len(outs)
    if first_in_hbm:
        out_specs[0] = pl.BlockSpec(memory_space=pl.ANY)
    return pl.pallas_call(
        body,
        out_shape=[jax.ShapeDtypeStruct(shape, kind) for shape, kind in outs],
        in_specs=[vmem] * len(args),
        out_specs=out_specs,
        scratch_shapes=list(scratch),
        compiler_params=pltpu.CompilerParams(vmem_limit_bytes=40 * 2**20),
    )(*args)


def dot(a, b, ca=1, cb=0):
    return lax.dot_general(a, b, (((ca,), (cb,)), ((), ())), preferred_element_type=F32)


def chooser(rows, cols, source_of):
    row = lax.broadcasted_iota(jnp.int32, (rows, cols), 0)
    col = lax.broadcasted_iota(jnp.int32, (rows, cols), 1)
    return (col == source_of(row)).astype(F32).astype(BF)


def pack_body(
    tok_ref, grad_ref, wq_ref, wo_ref, out_ref, both_vm, wq_vm, wo_vm, sems
):
    copies = [
        pltpu.make_async_copy(src, dst, sems.at[i])
        for i, (src, dst) in enumerate(
            [
                (tok_ref, both_vm.at[0:128]),
                (grad_ref, both_vm.at[128:256]),
                (wq_ref, wq_vm),
                (wo_ref, wo_vm),
            ]
        )
    ]
    for copy in copies:
        copy.start()
    yh = lax.axis_index("yh")

    def source(i):
        side = i >> 3 & 1
        chip = (i >> 5) * 4 + (yh ^ side) * 2 + ((i >> 4 & 1) ^ side)
        return (i >> 2 & 1) * 128 + (i & 1) * 64 + (i >> 1 & 1) * 32 + chip

    pick = chooser(256, 256, source)
    for copy in copies:
        copy.wait()
    out_ref[:, :512] = dot(pick, both_vm[...]).astype(BF)
    x = lax.axis_index("x")
    part = wo_vm[...].astype(F32)
    for i in range(3):
        part = jnp.where(x == i, wq_vm[:, i * 512 : i * 512 + 512].astype(F32), part)
    blocks = jnp.concatenate([part[:, y * 128 : y * 128 + 128] for y in range(Y)], axis=0)
    out_ref[:, 512:] = jnp.concatenate([blocks] * ZL, axis=0).astype(BF)


def halves(arr):
    return arr[:, :64], arr[:, 64:]


def weights_body(moved_ref, sent_ref, pair_vm, sems):
    block = moved_ref[:, 512:].astype(F32).reshape(16, 2, 8, 128)
    sides = [block[:, i].reshape(128, 128) for i in range(2)]
    outs = x_is_last()
    for core in range(2):
        heads = jnp.concatenate([side[:, core * 64 : core * 64 + 64] for side in sides], axis=1)
        planes = [side.reshape(4, 2, 16, 128)[:, core].reshape(64, 128) for side in sides]
        mine = jnp.where(outs, jnp.concatenate(planes, axis=0), heads).astype(BF)
        pair_vm[core] = mine
    copies = [
        pltpu.make_async_copy(pair_vm, sent_ref.at[2 * xy : 2 * xy + 2], sems.at[xy])
        for xy in range(X * Y)
    ]
    for copy in copies:
        copy.start()
    for copy in copies:
        copy.wait()


def hop_body(moved_ref, hop_ref):
    pick = chooser(128, 256, lambda i: (i >> 3) * 16 + 8 + (i & 7))
    hop_ref[...] = dot(pick, moved_ref[:, :512]).astype(BF)


def rows_body(moved_ref, other_ref, own_ref):
    yh = lax.axis_index("yh")

    def source(i):
        origin = (i >> 3 & 7) * 2 + (i >> 1 & 1)
        row = (i >> 7) * 4 + (i >> 6 & 1) * 2 + (i & 1)
        return jnp.where((i >> 2 & 1) == yh, origin * 16 + row, 256 + origin * 8 + row)

    both = jnp.concatenate([moved_ref[:, :512], other_ref[...]], axis=0)
    own_ref[...] = dot(chooser(256, 384, source), both).astype(BF)


def norm_body(own_ref, far_ref, gain_ref, scaled_ref, normed_ref, flipped_ref, grad_ref):
    own, far = own_ref[...], far_ref[...]
    x_in = jnp.concatenate([own[0:64], far[0:64], own[64:128], far[64:128]], axis=0)
    grad_ref[...] = jnp.concatenate([own[128:192], far[128:192], own[192:], far[192:]], axis=0)
    values = x_in.astype(F32)
    inverse = lax.rsqrt(jnp.mean(values * values, axis=-1, keepdims=True) + EPS)
    scaled = values * inverse
    scaled_ref[...] = scaled
    normed = scaled * gain_ref[...]
    normed_ref[...] = normed.astype(BF)
    flipped_ref[...] = normed.T.astype(BF)


def x_is_last():
    return lax.axis_index("x") == 3


def weave(first, second):
    rows, cols = first.shape
    blocks = [arr.reshape(rows // 8, 1, 8, cols) for arr in (first, second)]
    return jnp.concatenate(blocks, axis=1).reshape(2 * rows, cols)


def main_body(
    scaled_ref, normed_ref, flipped_ref, grad_ref, w_ref,
    parts_ref, send_ref, keep_ref, parts_vm, sems,
):
    def gathered(part, yl, count, piece):
        sides = []
        for yh in range(2):
            blocks = []
            for core in range(2):
                block = piece(w_ref[part * 8 + yh * 4 + yl * 2 + core].astype(F32))
                blocks.append(block.reshape(count, 1, 2, 1, 8, block.shape[1]))
            sides.append(jnp.concatenate(blocks, axis=3))
        full = jnp.concatenate(sides, axis=1)
        return full.reshape(count * 64, full.shape[-1]).astype(BF)

    wh = jnp.concatenate(
        [gathered(x, yl, 8, lambda arr: arr) for x in range(3) for yl in range(2)], axis=1
    )

    def wide(arr):
        return jnp.concatenate([arr[:64], arr[64:]], axis=1)

    wo = jnp.concatenate([gathered(3, yl, 4, wide) for yl in range(2)], axis=1)
    normed, g_in = normed_ref[...], grad_ref[...]
    qkv = dot(normed, wh).astype(BF)
    ups = dot(g_in, wo, 1, 1).astype(BF)

    lane = lax.broadcasted_iota(jnp.int32, (128, 128), 1)
    first = lane < 64
    zero = jnp.zeros((128, 128), BF)

    def stack(arr):
        return jnp.concatenate([jnp.where(first, arr, zero), jnp.where(first, zero, arr)], axis=0)

    def pile(arr):
        return jnp.concatenate([arr[:, :128], arr[:, 128:]], axis=0)

    atts, dqs, dks, dvs = [], [], [], []
    for f in range(2):
        rows = slice(f * 128, (f + 1) * 128)
        for pair in range(2):
            at = pair * 128
            q = qkv[rows, at : at + 128]
            k2 = stack(qkv[rows, 256 + at : 256 + at + 128])
            v2 = stack(qkv[rows, 512 + at : 512 + at + 128])
            u = ups[rows, at : at + 128]
            scores = dot(q, k2, 1, 1) * 0.125
            dprob = dot(u, v2, 1, 1)
            weights, dscores = [], []
            for head in range(2):
                cols = slice(head * 128, (head + 1) * 128)
                s = scores[:, cols]
                expo = jnp.exp(s - jnp.max(s, axis=-1, keepdims=True))
                probs = expo * (1.0 / jnp.sum(expo, axis=-1, keepdims=True))
                dp = dprob[:, cols]
                weights.append(probs.astype(BF))
                inner = jnp.sum(probs * dp, axis=-1, keepdims=True)
                dscores.append((probs * (dp - inner) * 0.125).astype(BF))
            weight = jnp.concatenate(weights, axis=1)
            dscore = jnp.concatenate(dscores, axis=1)
            atts.append(dot(weight, v2).astype(BF))
            dqs.append(dot(dscore, k2).astype(BF))
            dks.append(dot(pile(dscore), stack(q), 0, 0).astype(BF))
            dvs.append(dot(pile(weight), stack(u), 0, 0).astype(BF))

    def frames(items):
        return [
            jnp.concatenate([items[0], items[2]], axis=0),
            jnp.concatenate([items[1], items[3]], axis=0),
        ]

    att = jnp.concatenate(frames(atts), axis=1)
    dqkv = jnp.concatenate(frames(dqs) + frames(dks) + frames(dvs), axis=1)

    dn = dot(dqkv, wh, 1, 1)
    keep_ref[...] = jnp.concatenate([dn[0:64], dn[128:192]], axis=0)
    send_ref[...] = jnp.concatenate([dn[64:128], dn[192:]], axis=0).astype(BF)

    gg = two_rows(jnp.sum(dn * scaled_ref[...], axis=0, keepdims=True))
    gg = jnp.concatenate([gg[0:2, i * 128 : i * 128 + 128] for i in range(4)], axis=0)

    copies = []

    def leave(part):
        at = slice(part * 8, part * 8 + 8)
        copy = pltpu.make_async_copy(parts_vm.at[at], parts_ref.at[at], sems.at[part])
        copy.start()
        copies.append(copy)

    g_out = dot(att, g_in, 0, 0).reshape(4, Y, 2, 8, 512)
    for yc in range(8):
        block = g_out[:, yc // 2, yc % 2].reshape(32, 512)
        pieces = [block[:, i * 128 : i * 128 + 128] for i in range(4)] + [gg]
        parts_vm[24 + yc] = jnp.concatenate(pieces, axis=0).astype(BF)
    leave(3)
    flipped = flipped_ref[...]
    for part in (2, 1, 0):
        g_part = dot(flipped, dqkv[:, part * 256 : part * 256 + 256])
        g_part = g_part.reshape(ZL, Y, 2, 8, 256)
        for yc in range(8):
            block = g_part[:, yc // 2, yc % 2].reshape(64, 256)
            pieces = [block[:, :128], block[:, 128:], gg]
            parts_vm[part * 8 + yc] = jnp.concatenate(pieces, axis=0).astype(BF)
        leave(part)
    for copy in copies:
        copy.wait()


def finish_body(own_ref, keep_ref, far_ref, gain_ref, out_ref):
    gain = gain_ref[...]
    values = own_ref[0:128, :].astype(F32)
    inverse = lax.rsqrt(jnp.mean(values * values, axis=-1, keepdims=True) + EPS)
    scaled = values * inverse
    ds = (keep_ref[...] + far_ref[...].astype(F32)) * gain
    inner = jnp.mean(ds * scaled, axis=-1, keepdims=True)
    result = (own_ref[128:256, :].astype(F32) + inverse * (ds - scaled * inner)).astype(BF)
    y = y_index()

    def source(i):
        return (i >> 4 & 1) * 64 + (i >> 1 & 7) * 8 + ((i >> 5) ^ y) * 2 + (i & 1)

    result = dot(chooser(128, 128, source), result).astype(BF)
    for k in range(Y):
        out_ref[k] = result[k * 32 : k * 32 + 32]


def two_rows(vec):
    high = vec.astype(BF).astype(F32)
    return jnp.concatenate([high, vec - high, jnp.zeros((6, vec.shape[1]), F32)], axis=0)


def two_blocks(rows):
    high = rows.astype(BF).astype(F32)
    return jnp.concatenate([high, rows - high], axis=0)


def merge_body(got_ref, hop_ref, b1_ref, b3_ref, out_ref):
    total = got_ref[0:2].astype(F32)
    for i in range(1, 16):
        total = total + got_ref[2 * i : 2 * i + 2].astype(F32)
    low, high = total[0, :128], total[1, :128]
    wide_low = jnp.concatenate([low[:64], low[64:]], axis=1)
    wide_high = jnp.concatenate([high[:64], high[64:]], axis=1)
    cols = jnp.concatenate(
        [piece[:, j * 64 : j * 64 + 64] for j in range(4) for piece in (wide_low, wide_high)],
        axis=1,
    )
    rows = weave(
        jnp.concatenate([low[i * 32 : i * 32 + 32] for i in range(4)], axis=1),
        jnp.concatenate([high[i * 32 : i * 32 + 32] for i in range(4)], axis=1),
    )
    out_ref[:, :512] = jnp.where(x_is_last(), rows, cols).astype(BF)
    pick = chooser(64, 64, lambda i: (i >> 1 & 3) * 16 + (i >> 3) * 2 + (i & 1))
    blocks = [hop_ref[0], b1_ref[...], hop_ref[2], b3_ref[...]]
    for f in range(2):
        rows = jnp.concatenate([block[f * 16 : f * 16 + 16] for block in blocks], axis=0)
        out_ref[:, 512 + f * 512 : 1024 + f * 512] = dot(pick, rows).astype(BF)
    gains = total[0, 128:] + total[1, 128:]
    gains = two_blocks(unpair(gains))
    out_ref[:, 1536:] = jnp.concatenate([gains] * ZL, axis=0).astype(BF)


def unpair(rows):
    return jnp.concatenate(
        [rows[2 * i : 2 * i + 1] + rows[2 * i + 1 : 2 * i + 2] for i in range(4)], axis=0
    )


def split_body(back_ref, hop_ref, rest_ref, last_ref):
    pick = chooser(64, 64, lambda i: (i >> 1 & 7) * 8 + (i >> 4) * 2 + (i & 1))
    for f in range(2):
        rows = dot(pick, back_ref[:, 512 + f * 512 : 1024 + f * 512]).astype(BF)
        hop_ref[f * 16 : f * 16 + 16] = rows[32:48]
        for at, k in enumerate((0, 1, 3)):
            row = at * 32 + f * 16
            rest_ref[row : row + 16] = rows[k * 16 : k * 16 + 16]
    sums = jnp.sum(back_ref[:, :512].astype(F32).reshape(ZL, 8, 512), axis=0)
    last_ref[:, :512] = sums.astype(BF)
    gains = jnp.sum(back_ref[:, 1536:].astype(F32).reshape(ZL, 8, 128), axis=0)
    last_ref[:, 512:] = two_blocks(gains[0:4] + gains[4:8]).astype(BF)


def pair_body(last_ref, far_ref, sent_ref, gain_ref):
    total = last_ref[...].astype(F32) + far_ref[...].astype(F32)
    grads = total[:, :512].astype(BF)
    for x in range(X):
        sent_ref[x] = grads
    gain_ref[...] = total[0:4, 512:] + total[4:8, 512:]


def tokens_body(rest_ref, two_ref, out_ref):
    y = y_index()
    blocks = jnp.concatenate([rest_ref[0:64], two_ref[...], rest_ref[64:96]], axis=0)

    def source(i):
        return ((i & 3) ^ y) * 32 + (i >> 5 & 1) * 16 + (i >> 2 & 7) * 2 + (i >> 6)

    out_ref[...] = dot(chooser(128, 128, source), blocks).astype(BF)


def end_body(got_ref, qkv_ref, out_ref):
    for x in range(3):
        qkv_ref[:, x * 512 : x * 512 + 512] = got_ref[x].astype(F32)
    out_ref[...] = got_ref[3].astype(F32)


def on_device(tokens, grad_out, gain, w_qkv, w_out):
    row = gain.reshape(1, 512)
    plane = ("x", "yh", "yl", "c")

    hbm = pl.BlockSpec(memory_space=pl.ANY)
    packed = pl.pallas_call(
        pack_body,
        out_shape=jax.ShapeDtypeStruct((256, 640), BF),
        in_specs=[hbm] * 4,
        out_specs=pl.BlockSpec(memory_space=pltpu.VMEM),
        scratch_shapes=[
            pltpu.VMEM((256, 512), BF),
            pltpu.VMEM((8, 1536), BF),
            pltpu.VMEM((8, 512), BF),
            pltpu.SemaphoreType.DMA((4,)),
        ],
        compiler_params=pltpu.CompilerParams(vmem_limit_bytes=60 * 2**20),
    )(tokens.reshape(128, 512), grad_out.reshape(128, 512), w_qkv, w_out)
    moved = exchange(packed.reshape(ZL * 2, 16, 640), ("zl", "yl")).reshape(256, 640)
    [sent] = call(
        weights_body,
        [((32, 128, 128), BF)],
        moved,
        first_in_hbm=True,
        scratch=[pltpu.VMEM((2, 128, 128), BF), pltpu.SemaphoreType.DMA((X * Y,))],
    )
    weights = exchange(sent, plane)
    [hop] = call(hop_body, [((128, 512), BF)], moved)
    [own] = call(rows_body, [((256, 512), BF)], moved, to_y(hop, 3))
    far = lax.ppermute(own, "c", SWAP)
    scaled, normed, flipped, grads = call(
        norm_body,
        [((256, 512), F32), ((256, 512), BF), ((512, 256), BF), ((256, 512), BF)],
        own, far, row,
    )
    parts, send, keep = call(
        main_body,
        [((32, 136, 128), BF), ((128, 512), BF), ((128, 512), F32)],
        scaled, normed, flipped, grads, weights,
        first_in_hbm=True,
        scratch=[pltpu.VMEM((32, 136, 128), BF), pltpu.SemaphoreType.DMA((4,))],
    )
    got = exchange(parts, plane)
    dn_far = lax.ppermute(send, "c", SWAP)
    [hop] = call(finish_body, [((Y, 32, 512), BF)], own, keep, dn_far, row)
    [sent] = call(merge_body, [((64, 1664), BF)], got, hop, to_y(hop[1], 1), to_y(hop[3], 3))
    back = exchange(sent.reshape(ZL, 8, 1664), "zl").reshape(64, 1664)
    hop, rest, last = call(
        split_body, [((32, 512), BF), ((96, 512), BF), ((8, 640), BF)], back
    )
    last_far = lax.ppermute(last, "zh", SWAP)
    [grad_tokens] = call(tokens_body, [((128, 512), BF)], rest, to_y(hop, 2))
    sent, total = call(pair_body, [((X, 8, 512), BF), ((4, 128), F32)], last, last_far)
    ends = exchange(sent, "x")
    shard_qkv, shard_out = call(end_body, [((8, 1536), F32), ((8, 512), F32)], ends)
    return grad_tokens.reshape(1, 2, 64, 512), shard_qkv, shard_out, total.reshape(512)


def solution(mesh):
    names = ("zh", "x", "zl", "yh", "yl", "c")
    inner = Mesh(mesh.devices.reshape(ZH, X, ZL, 2, 2, C), names)
    grid = names[2:]
    tok = P(("zh", "x"), grid, None, None)
    return jax.shard_map(
        on_device,
        mesh=inner,
        in_specs=(tok, tok, P(), P(grid, None), P(grid, None)),
        out_specs=(tok, P(grid, None), P(grid, None), P()),
        check_vma=False,
    )
```

```python
import jax
import jax.numpy as jnp
from jax import lax
from jax.experimental import pallas as pl
from jax.experimental.pallas import tpu as pltpu
from jax.sharding import Mesh
from jax.sharding import PartitionSpec as P

EPS = 1e-06
BF = jnp.bfloat16
F32 = jnp.float32

ZH, X, ZL, Y, C = 2, 4, 8, 4, 2
SWAP = [(0, 1), (1, 0)]


def exchange(arr, axes):
    return lax.all_to_all(arr, axes, split_axis=0, concat_axis=0, tiled=True)


def to_y(block, k):
    return lax.ppermute(block, "y", [(i, i ^ k) for i in range(Y)])


def call(body, outs, *args, first_in_hbm=False, scratch=()):
    vmem = pl.BlockSpec(memory_space=pltpu.VMEM)
    out_specs = [vmem] * len(outs)
    if first_in_hbm:
        out_specs[0] = pl.BlockSpec(memory_space=pl.ANY)
    return pl.pallas_call(
        body,
        out_shape=[jax.ShapeDtypeStruct(shape, kind) for shape, kind in outs],
        in_specs=[vmem] * len(args),
        out_specs=out_specs,
        scratch_shapes=list(scratch),
        compiler_params=pltpu.CompilerParams(vmem_limit_bytes=40 * 2**20),
    )(*args)


def dot(a, b, ca=1, cb=0):
    return lax.dot_general(a, b, (((ca,), (cb,)), ((), ())), preferred_element_type=F32)


def chooser(rows, cols, source_of):
    row = lax.broadcasted_iota(jnp.int32, (rows, cols), 0)
    col = lax.broadcasted_iota(jnp.int32, (rows, cols), 1)
    return (col == source_of(row)).astype(F32).astype(BF)


def pack_body(
    tok_ref, grad_ref, wq_ref, wo_ref, out_ref, both_vm, wq_vm, wo_vm, sems
):
    copies = [
        pltpu.make_async_copy(src, dst, sems.at[i])
        for i, (src, dst) in enumerate(
            [
                (tok_ref, both_vm.at[0:128]),
                (grad_ref, both_vm.at[128:256]),
                (wq_ref, wq_vm),
                (wo_ref, wo_vm),
            ]
        )
    ]
    for copy in copies:
        copy.start()
    pick = chooser(
        256, 256, lambda i: (i >> 2 & 1) * 128 + (i & 1) * 64 + (i >> 1 & 1) * 32 + (i >> 3)
    )
    for copy in copies:
        copy.wait()
    out_ref[:, :512] = dot(pick, both_vm[...]).astype(BF)
    x = lax.axis_index("x")
    part = wo_vm[...].astype(F32)
    for i in range(3):
        part = jnp.where(x == i, wq_vm[:, i * 512 : i * 512 + 512].astype(F32), part)
    blocks = jnp.concatenate([part[:, y * 128 : y * 128 + 128] for y in range(Y)], axis=0)
    out_ref[:, 512:] = jnp.concatenate([blocks] * ZL, axis=0).astype(BF)


def halves(arr):
    return arr[:, :64], arr[:, 64:]


def weights_body(moved_ref, sent_ref, pair_vm, sems):
    block = moved_ref[:, 512:].astype(F32)
    (low0, low1), (high0, high1) = halves(block[:128]), halves(block[128:])
    planes = block.reshape(4, 2, 32, 128)
    outs = x_is_last()
    for core, cols in ((0, (low0, high0)), (1, (low1, high1))):
        mine = jnp.where(
            outs, planes[:, core].reshape(128, 128), jnp.concatenate(cols, axis=1)
        ).astype(BF)
        pair_vm[core] = mine
    copies = [
        pltpu.make_async_copy(pair_vm, sent_ref.at[2 * xy : 2 * xy + 2], sems.at[xy])
        for xy in range(X * Y)
    ]
    for copy in copies:
        copy.start()
    for copy in copies:
        copy.wait()


def rows_body(moved_ref, own_ref):
    pick = chooser(
        256, 256, lambda i: (i >> 1 & 31) * 8 + (i >> 7) * 4 + (i >> 6 & 1) * 2 + (i & 1)
    )
    own_ref[...] = dot(pick, moved_ref[:, :512]).astype(BF)


def norm_body(own_ref, far_ref, gain_ref, scaled_ref, normed_ref, flipped_ref, grad_ref):
    own, far = own_ref[...], far_ref[...]
    x_in = jnp.concatenate([own[0:64], far[0:64], own[64:128], far[64:128]], axis=0)
    grad_ref[...] = jnp.concatenate([own[128:192], far[128:192], own[192:], far[192:]], axis=0)
    values = x_in.astype(F32)
    inverse = lax.rsqrt(jnp.mean(values * values, axis=-1, keepdims=True) + EPS)
    scaled = values * inverse
    scaled_ref[...] = scaled
    normed = scaled * gain_ref[...]
    normed_ref[...] = normed.astype(BF)
    flipped_ref[...] = normed.T.astype(BF)


def x_is_last():
    return lax.axis_index("x") == 3


def weave(first, second):
    rows, cols = first.shape
    blocks = [arr.reshape(rows // 8, 1, 8, cols) for arr in (first, second)]
    return jnp.concatenate(blocks, axis=1).reshape(2 * rows, cols)


def main_body(
    scaled_ref, normed_ref, flipped_ref, grad_ref, w_ref,
    parts_ref, send_ref, keep_ref, parts_vm, sems,
):
    lanes = []
    for x in range(3):
        for pair in range(2):
            tops, bots = [], []
            for core in range(2):
                at = x * 8 + pair * 4 + core
                (a0, a1), (b0, b1) = (
                    halves(w_ref[at].astype(F32)),
                    halves(w_ref[at + 2].astype(F32)),
                )
                tops.append(jnp.concatenate([a0, b0], axis=1))
                bots.append(jnp.concatenate([a1, b1], axis=1))
            lanes.append(jnp.concatenate([weave(*tops), weave(*bots)], axis=0).astype(BF))
    wh = jnp.concatenate(lanes, axis=1)
    lanes = [
        weave(w_ref[24 + 2 * y].astype(F32), w_ref[25 + 2 * y].astype(F32)).astype(BF)
        for y in range(Y)
    ]
    wo = jnp.concatenate(lanes, axis=1)

    normed, g_in = normed_ref[...], grad_ref[...]
    qkv = dot(normed, wh).astype(BF)
    ups = dot(g_in, wo, 1, 1).astype(BF)

    lane = lax.broadcasted_iota(jnp.int32, (128, 128), 1)
    first = lane < 64
    zero = jnp.zeros((128, 128), BF)

    def stack(arr):
        return jnp.concatenate([jnp.where(first, arr, zero), jnp.where(first, zero, arr)], axis=0)

    def pile(arr):
        return jnp.concatenate([arr[:, :128], arr[:, 128:]], axis=0)

    def frames(items):
        return [
            jnp.concatenate([items[0], items[2]], axis=0),
            jnp.concatenate([items[1], items[3]], axis=0),
        ]

    copies = []

    def leave(part, messages):
        for yc in range(8):
            parts_vm[part * 8 + yc] = messages(yc).astype(BF)
        at = slice(part * 8, part * 8 + 8)
        copy = pltpu.make_async_copy(parts_vm.at[at], parts_ref.at[at], sems.at[part])
        copy.start()
        copies.append(copy)

    def leave_columns(part, columns, tail):
        grads = dot(flipped, columns).reshape(ZL, Y, 2, 8, 256)

        def message(yc):
            block = grads[:, yc // 2, yc % 2].reshape(64, 256)
            return jnp.concatenate([block[:, :128], block[:, 128:], tail], axis=0)

        leave(part, message)

    flipped = flipped_ref[...]
    none = jnp.zeros((8, 128), F32)
    atts, dvs, dscores, sides = [], [], [], []
    for f in range(2):
        rows = slice(f * 128, (f + 1) * 128)
        for pair in range(2):
            at = pair * 128
            q = qkv[rows, at : at + 128]
            k2 = stack(qkv[rows, 256 + at : 256 + at + 128])
            v2 = stack(qkv[rows, 512 + at : 512 + at + 128])
            u = ups[rows, at : at + 128]
            scores = dot(q, k2, 1, 1) * 0.125
            dprob = dot(u, v2, 1, 1)
            weights, scored = [], []
            for head in range(2):
                cols = slice(head * 128, (head + 1) * 128)
                s = scores[:, cols]
                expo = jnp.exp(s - jnp.max(s, axis=-1, keepdims=True))
                probs = expo * (1.0 / jnp.sum(expo, axis=-1, keepdims=True))
                dp = dprob[:, cols]
                weights.append(probs.astype(BF))
                inner = jnp.sum(probs * dp, axis=-1, keepdims=True)
                scored.append((probs * (dp - inner) * 0.125).astype(BF))
            weight = jnp.concatenate(weights, axis=1)
            atts.append(dot(weight, v2).astype(BF))
            dvs.append(dot(pile(weight), stack(u), 0, 0).astype(BF))
            dscores.append(jnp.concatenate(scored, axis=1))
            sides.append((q, k2))

    att = jnp.concatenate(frames(atts), axis=1)
    g_out = dot(att, g_in, 0, 0).reshape(4, Y, 2, 8, 512)

    def out_message(yc):
        block = g_out[:, yc // 2, yc % 2].reshape(32, 512)
        pieces = [block[:, i * 128 : i * 128 + 128] for i in range(4)]
        return jnp.concatenate(pieces + [none], axis=0)

    leave(3, out_message)
    dv = jnp.concatenate(frames(dvs), axis=1)
    leave_columns(2, dv, none)

    dq = [dot(dscore, k2).astype(BF) for dscore, (q, k2) in zip(dscores, sides)]
    dk = [dot(pile(dscore), stack(q), 0, 0).astype(BF) for dscore, (q, k2) in zip(dscores, sides)]
    dq = jnp.concatenate(frames(dq), axis=1)
    dk = jnp.concatenate(frames(dk), axis=1)
    dn = dot(jnp.concatenate([dq, dk, dv], axis=1), wh, 1, 1)
    gg = two_rows(jnp.sum(dn * scaled_ref[...], axis=0, keepdims=True))
    gg = jnp.concatenate([gg[0:2, i * 128 : i * 128 + 128] for i in range(4)], axis=0)
    leave_columns(1, dk, gg)
    leave_columns(0, dq, gg)
    keep_ref[...] = jnp.concatenate([dn[0:64], dn[128:192]], axis=0)
    send_ref[...] = jnp.concatenate([dn[64:128], dn[192:]], axis=0).astype(BF)
    for copy in copies:
        copy.wait()


def finish_body(own_ref, keep_ref, far_ref, gain_ref, out_ref):
    gain = gain_ref[...]
    values = own_ref[0:128, :].astype(F32)
    inverse = lax.rsqrt(jnp.mean(values * values, axis=-1, keepdims=True) + EPS)
    scaled = values * inverse
    ds = (keep_ref[...] + far_ref[...].astype(F32)) * gain
    inner = jnp.mean(ds * scaled, axis=-1, keepdims=True)
    result = (own_ref[128:256, :].astype(F32) + inverse * (ds - scaled * inner)).astype(BF)
    y = lax.axis_index("y")

    def source(i):
        return (i >> 4 & 1) * 64 + (i >> 1 & 7) * 8 + ((i >> 5) ^ y) * 2 + (i & 1)

    result = dot(chooser(128, 128, source), result).astype(BF)
    for k in range(Y):
        out_ref[k] = result[k * 32 : k * 32 + 32]


def two_rows(vec):
    high = vec.astype(BF).astype(F32)
    return jnp.concatenate([high, vec - high, jnp.zeros((6, vec.shape[1]), F32)], axis=0)


def two_blocks(rows):
    high = rows.astype(BF).astype(F32)
    return jnp.concatenate([high, rows - high], axis=0)


def merge_body(got_ref, hop_ref, b1_ref, b3_ref, out_ref):
    total = got_ref[0:2].astype(F32)
    for i in range(1, 16):
        total = total + got_ref[2 * i : 2 * i + 2].astype(F32)
    low, high = total[0, :128], total[1, :128]
    wide_low = jnp.concatenate([low[:64], low[64:]], axis=1)
    wide_high = jnp.concatenate([high[:64], high[64:]], axis=1)
    cols = jnp.concatenate(
        [piece[:, j * 64 : j * 64 + 64] for j in range(4) for piece in (wide_low, wide_high)],
        axis=1,
    )
    rows = weave(
        jnp.concatenate([low[i * 32 : i * 32 + 32] for i in range(4)], axis=1),
        jnp.concatenate([high[i * 32 : i * 32 + 32] for i in range(4)], axis=1),
    )
    out_ref[:, :512] = jnp.where(x_is_last(), rows, cols).astype(BF)
    pick = chooser(64, 64, lambda i: (i >> 1 & 3) * 16 + (i >> 3) * 2 + (i & 1))
    blocks = [hop_ref[0], b1_ref[...], hop_ref[2], b3_ref[...]]
    for f in range(2):
        rows = jnp.concatenate([block[f * 16 : f * 16 + 16] for block in blocks], axis=0)
        out_ref[:, 512 + f * 512 : 1024 + f * 512] = dot(pick, rows).astype(BF)
    gains = total[0, 128:] + total[1, 128:]
    gains = two_blocks(unpair(gains))
    out_ref[:, 1536:] = jnp.concatenate([gains] * ZL, axis=0).astype(BF)


def unpair(rows):
    return jnp.concatenate(
        [rows[2 * i : 2 * i + 1] + rows[2 * i + 1 : 2 * i + 2] for i in range(4)], axis=0
    )


def split_body(back_ref, hop_ref, rest_ref, last_ref):
    pick = chooser(64, 64, lambda i: (i >> 1 & 7) * 8 + (i >> 4) * 2 + (i & 1))
    for f in range(2):
        rows = dot(pick, back_ref[:, 512 + f * 512 : 1024 + f * 512]).astype(BF)
        hop_ref[f * 16 : f * 16 + 16] = rows[32:48]
        for at, k in enumerate((0, 1, 3)):
            row = at * 32 + f * 16
            rest_ref[row : row + 16] = rows[k * 16 : k * 16 + 16]
    sums = jnp.sum(back_ref[:, :512].astype(F32).reshape(ZL, 8, 512), axis=0)
    last_ref[:, :512] = sums.astype(BF)
    gains = jnp.sum(back_ref[:, 1536:].astype(F32).reshape(ZL, 8, 128), axis=0)
    last_ref[:, 512:] = two_blocks(gains[0:4] + gains[4:8]).astype(BF)


def pair_body(last_ref, far_ref, sent_ref):
    total = last_ref[...].astype(F32) + far_ref[...].astype(F32)
    grads = total[:, :512].astype(BF)
    gains = two_blocks(total[0:4, 512:] + total[4:8, 512:]).astype(BF)
    for x in range(X):
        sent_ref[x, :, :512] = grads
        sent_ref[x, :, 512:] = gains


def tokens_body(rest_ref, two_ref, out_ref):
    y = lax.axis_index("y")
    blocks = jnp.concatenate([rest_ref[0:64], two_ref[...], rest_ref[64:96]], axis=0)

    def source(i):
        return ((i & 3) ^ y) * 32 + (i >> 5 & 1) * 16 + (i >> 2 & 7) * 2 + (i >> 6)

    out_ref[...] = dot(chooser(128, 128, source), blocks).astype(BF)


def end_body(got_ref, qkv_ref, out_ref, gain_ref):
    for x in range(3):
        qkv_ref[:, x * 512 : x * 512 + 512] = got_ref[x, :, :512].astype(F32)
    out_ref[...] = got_ref[3, :, :512].astype(F32)
    gain = got_ref[0, :, 512:].astype(F32)
    gain_ref[...] = gain[0:4] + gain[4:8]


def on_device(tokens, grad_out, gain, w_qkv, w_out):
    row = gain.reshape(1, 512)
    plane = ("x", "y", "c")

    hbm = pl.BlockSpec(memory_space=pl.ANY)
    packed = pl.pallas_call(
        pack_body,
        out_shape=jax.ShapeDtypeStruct((256, 640), BF),
        in_specs=[hbm] * 4,
        out_specs=pl.BlockSpec(memory_space=pltpu.VMEM),
        scratch_shapes=[
            pltpu.VMEM((256, 512), BF),
            pltpu.VMEM((8, 1536), BF),
            pltpu.VMEM((8, 512), BF),
            pltpu.SemaphoreType.DMA((4,)),
        ],
        compiler_params=pltpu.CompilerParams(vmem_limit_bytes=60 * 2**20),
    )(tokens.reshape(128, 512), grad_out.reshape(128, 512), w_qkv, w_out)
    moved = exchange(packed.reshape(ZL * Y, 8, 640), ("zl", "y")).reshape(256, 640)
    [sent] = call(
        weights_body,
        [((32, 128, 128), BF)],
        moved,
        first_in_hbm=True,
        scratch=[pltpu.VMEM((2, 128, 128), BF), pltpu.SemaphoreType.DMA((X * Y,))],
    )
    weights = exchange(sent, plane)
    [own] = call(rows_body, [((256, 512), BF)], moved)
    far = lax.ppermute(own, "c", SWAP)
    scaled, normed, flipped, grads = call(
        norm_body,
        [((256, 512), F32), ((256, 512), BF), ((512, 256), BF), ((256, 512), BF)],
        own, far, row,
    )
    parts, send, keep = call(
        main_body,
        [((32, 136, 128), BF), ((128, 512), BF), ((128, 512), F32)],
        scaled, normed, flipped, grads, weights,
        first_in_hbm=True,
        scratch=[pltpu.VMEM((32, 136, 128), BF), pltpu.SemaphoreType.DMA((4,))],
    )
    got = exchange(parts, plane)
    dn_far = lax.ppermute(send, "c", SWAP)
    [hop] = call(finish_body, [((Y, 32, 512), BF)], own, keep, dn_far, row)
    [sent] = call(merge_body, [((64, 1664), BF)], got, hop, to_y(hop[1], 1), to_y(hop[3], 3))
    back = exchange(sent.reshape(ZL, 8, 1664), "zl").reshape(64, 1664)
    hop, rest, last = call(
        split_body, [((32, 512), BF), ((96, 512), BF), ((8, 640), BF)], back
    )
    last_far = lax.ppermute(last, "zh", SWAP)
    [grad_tokens] = call(tokens_body, [((128, 512), BF)], rest, to_y(hop, 2))
    last_far, grad_tokens = lax.optimization_barrier((last_far, grad_tokens))
    [sent] = call(pair_body, [((X, 8, 640), BF)], last, last_far)
    ends = exchange(sent, "x")
    shard_qkv, shard_out, total = call(
        end_body, [((8, 1536), F32), ((8, 512), F32), ((4, 128), F32)], ends
    )
    return grad_tokens.reshape(1, 2, 64, 512), shard_qkv, shard_out, total.reshape(512)


def solution(mesh):
    inner = Mesh(mesh.devices.reshape(ZH, X, ZL, Y, C), ("zh", "x", "zl", "y", "c"))
    grid = ("zl", "y", "c")
    tok = P(("zh", "x"), grid, None, None)
    return jax.shard_map(
        on_device,
        mesh=inner,
        in_specs=(tok, tok, P(), P(grid, None), P(grid, None)),
        out_specs=(tok, P(grid, None), P(grid, None), P()),
        check_vma=False,
    )
```

```python
import jax
import jax.numpy as jnp
from jax import lax
from jax.experimental import pallas as pl
from jax.experimental.pallas import tpu as pltpu
from jax.sharding import Mesh
from jax.sharding import PartitionSpec as P

EPS = 1e-06
BF = jnp.bfloat16
F32 = jnp.float32

ZH, X, ZL, Y, C = 2, 4, 8, 4, 2
SWAP = [(0, 1), (1, 0)]


def exchange(arr, axes):
    return lax.all_to_all(arr, axes, split_axis=0, concat_axis=0, tiled=True)


def to_y(block, k):
    return lax.ppermute(block, "y", [(i, i ^ k) for i in range(Y)])


def call(body, outs, *args, first_in_hbm=False, scratch=()):
    vmem = pl.BlockSpec(memory_space=pltpu.VMEM)
    out_specs = [vmem] * len(outs)
    if first_in_hbm:
        out_specs[0] = pl.BlockSpec(memory_space=pl.ANY)
    return pl.pallas_call(
        body,
        out_shape=[jax.ShapeDtypeStruct(shape, kind) for shape, kind in outs],
        in_specs=[vmem] * len(args),
        out_specs=out_specs,
        scratch_shapes=list(scratch),
        compiler_params=pltpu.CompilerParams(vmem_limit_bytes=40 * 2**20),
    )(*args)


def dot(a, b, ca=1, cb=0):
    return lax.dot_general(a, b, (((ca,), (cb,)), ((), ())), preferred_element_type=F32)


def chooser(rows, cols, source_of):
    row = lax.broadcasted_iota(jnp.int32, (rows, cols), 0)
    col = lax.broadcasted_iota(jnp.int32, (rows, cols), 1)
    return (col == source_of(row)).astype(F32).astype(BF)


def pack_body(
    tok_ref, grad_ref, wq_ref, wo_ref, out_ref, both_vm, wq_vm, wo_vm, sems
):
    copies = [
        pltpu.make_async_copy(src, dst, sems.at[i])
        for i, (src, dst) in enumerate(
            [
                (tok_ref, both_vm.at[0:128]),
                (grad_ref, both_vm.at[128:256]),
                (wq_ref, wq_vm),
                (wo_ref, wo_vm),
            ]
        )
    ]
    for copy in copies:
        copy.start()
    pick = chooser(
        256, 256, lambda i: (i >> 2 & 1) * 128 + (i & 1) * 64 + (i >> 1 & 1) * 32 + (i >> 3)
    )
    for copy in copies:
        copy.wait()
    out_ref[:, :512] = dot(pick, both_vm[...]).astype(BF)
    x = lax.axis_index("x")
    part = wo_vm[...].astype(F32)
    for i in range(3):
        part = jnp.where(x == i, wq_vm[:, i * 512 : i * 512 + 512].astype(F32), part)
    blocks = jnp.concatenate([part[:, y * 128 : y * 128 + 128] for y in range(Y)], axis=0)
    out_ref[:, 512:] = jnp.concatenate([blocks] * ZL, axis=0).astype(BF)


def halves(arr):
    return arr[:, :64], arr[:, 64:]


def weights_body(moved_ref, sent_ref, pair_vm, sems):
    block = moved_ref[:, 512:].astype(F32)
    (low0, low1), (high0, high1) = halves(block[:128]), halves(block[128:])
    planes = block.reshape(4, 2, 32, 128)
    outs = x_is_last()
    for core, cols in ((0, (low0, high0)), (1, (low1, high1))):
        mine = jnp.where(
            outs, planes[:, core].reshape(128, 128), jnp.concatenate(cols, axis=1)
        ).astype(BF)
        pair_vm[core] = mine
    copies = [
        pltpu.make_async_copy(pair_vm, sent_ref.at[2 * xy : 2 * xy + 2], sems.at[xy])
        for xy in range(X * Y)
    ]
    for copy in copies:
        copy.start()
    for copy in copies:
        copy.wait()


def rows_body(moved_ref, own_ref):
    pick = chooser(
        256, 256, lambda i: (i >> 1 & 31) * 8 + (i >> 7) * 4 + (i >> 6 & 1) * 2 + (i & 1)
    )
    own_ref[...] = dot(pick, moved_ref[:, :512]).astype(BF)


def norm_body(own_ref, far_ref, gain_ref, scaled_ref, normed_ref, flipped_ref, grad_ref):
    own, far = own_ref[...], far_ref[...]
    x_in = jnp.concatenate([own[0:64], far[0:64], own[64:128], far[64:128]], axis=0)
    grad_ref[...] = jnp.concatenate([own[128:192], far[128:192], own[192:], far[192:]], axis=0)
    values = x_in.astype(F32)
    inverse = lax.rsqrt(jnp.mean(values * values, axis=-1, keepdims=True) + EPS)
    scaled = values * inverse
    scaled_ref[...] = scaled
    normed = scaled * gain_ref[...]
    normed_ref[...] = normed.astype(BF)
    flipped_ref[...] = normed.T.astype(BF)


def x_is_last():
    return lax.axis_index("x") == 3


def weave(first, second):
    rows, cols = first.shape
    blocks = [arr.reshape(rows // 8, 1, 8, cols) for arr in (first, second)]
    return jnp.concatenate(blocks, axis=1).reshape(2 * rows, cols)


def main_body(
    scaled_ref, normed_ref, flipped_ref, grad_ref, w_ref,
    parts_ref, send_ref, keep_ref, parts_vm, sems,
):
    lanes = []
    for x in range(3):
        for pair in range(2):
            tops, bots = [], []
            for core in range(2):
                at = x * 8 + pair * 4 + core
                (a0, a1), (b0, b1) = (
                    halves(w_ref[at].astype(F32)),
                    halves(w_ref[at + 2].astype(F32)),
                )
                tops.append(jnp.concatenate([a0, b0], axis=1))
                bots.append(jnp.concatenate([a1, b1], axis=1))
            lanes.append(jnp.concatenate([weave(*tops), weave(*bots)], axis=0).astype(BF))
    wh = jnp.concatenate(lanes, axis=1)
    lanes = [
        weave(w_ref[24 + 2 * y].astype(F32), w_ref[25 + 2 * y].astype(F32)).astype(BF)
        for y in range(Y)
    ]
    wo = jnp.concatenate(lanes, axis=1)

    normed, g_in = normed_ref[...], grad_ref[...]
    qkv = dot(normed, wh).astype(BF)
    ups = dot(g_in, wo, 1, 1).astype(BF)

    lane = lax.broadcasted_iota(jnp.int32, (128, 128), 1)
    first = lane < 64
    zero = jnp.zeros((128, 128), BF)

    def stack(arr):
        return jnp.concatenate([jnp.where(first, arr, zero), jnp.where(first, zero, arr)], axis=0)

    def pile(arr):
        return jnp.concatenate([arr[:, :128], arr[:, 128:]], axis=0)

    def frames(items):
        return [
            jnp.concatenate([items[0], items[2]], axis=0),
            jnp.concatenate([items[1], items[3]], axis=0),
        ]

    copies = []

    def leave(part, messages):
        for yc in range(8):
            parts_vm[part * 8 + yc] = messages(yc).astype(BF)
        at = slice(part * 8, part * 8 + 8)
        copy = pltpu.make_async_copy(parts_vm.at[at], parts_ref.at[at], sems.at[part])
        copy.start()
        copies.append(copy)

    def leave_columns(part, columns, tail):
        grads = dot(flipped, columns).reshape(ZL, Y, 2, 8, 256)

        def message(yc):
            block = grads[:, yc // 2, yc % 2].reshape(64, 256)
            return jnp.concatenate([block[:, :128], block[:, 128:], tail], axis=0)

        leave(part, message)

    flipped = flipped_ref[...]
    none = jnp.zeros((8, 128), F32)
    atts, dvs, dscores, sides = [], [], [], []
    for f in range(2):
        rows = slice(f * 128, (f + 1) * 128)
        for pair in range(2):
            at = pair * 128
            q = qkv[rows, at : at + 128]
            k2 = stack(qkv[rows, 256 + at : 256 + at + 128])
            v2 = stack(qkv[rows, 512 + at : 512 + at + 128])
            u = ups[rows, at : at + 128]
            scores = dot(q, k2, 1, 1) * 0.125
            dprob = dot(u, v2, 1, 1)
            weights, scored = [], []
            for head in range(2):
                cols = slice(head * 128, (head + 1) * 128)
                s = scores[:, cols]
                expo = jnp.exp(s - jnp.max(s, axis=-1, keepdims=True))
                probs = expo * (1.0 / jnp.sum(expo, axis=-1, keepdims=True))
                dp = dprob[:, cols]
                weights.append(probs.astype(BF))
                inner = jnp.sum(probs * dp, axis=-1, keepdims=True)
                scored.append((probs * (dp - inner) * 0.125).astype(BF))
            weight = jnp.concatenate(weights, axis=1)
            atts.append(dot(weight, v2).astype(BF))
            dvs.append(dot(pile(weight), stack(u), 0, 0).astype(BF))
            dscores.append(jnp.concatenate(scored, axis=1))
            sides.append((q, k2))

    att = jnp.concatenate(frames(atts), axis=1)
    g_out = dot(att, g_in, 0, 0).reshape(4, Y, 2, 8, 512)

    def out_message(yc):
        block = g_out[:, yc // 2, yc % 2].reshape(32, 512)
        pieces = [block[:, i * 128 : i * 128 + 128] for i in range(4)]
        return jnp.concatenate(pieces + [none], axis=0)

    leave(3, out_message)
    dv = jnp.concatenate(frames(dvs), axis=1)
    leave_columns(2, dv, none)

    dq = [dot(dscore, k2).astype(BF) for dscore, (q, k2) in zip(dscores, sides)]
    dk = [dot(pile(dscore), stack(q), 0, 0).astype(BF) for dscore, (q, k2) in zip(dscores, sides)]
    dq = jnp.concatenate(frames(dq), axis=1)
    dk = jnp.concatenate(frames(dk), axis=1)
    dn = dot(jnp.concatenate([dq, dk, dv], axis=1), wh, 1, 1)
    gg = two_rows(jnp.sum(dn * scaled_ref[...], axis=0, keepdims=True))
    gg = jnp.concatenate([gg[0:2, i * 128 : i * 128 + 128] for i in range(4)], axis=0)
    leave_columns(1, dk, gg)
    leave_columns(0, dq, gg)
    keep_ref[...] = jnp.concatenate([dn[0:64], dn[128:192]], axis=0)
    send_ref[...] = jnp.concatenate([dn[64:128], dn[192:]], axis=0).astype(BF)
    for copy in copies:
        copy.wait()


def finish_body(own_ref, keep_ref, far_ref, gain_ref, out_ref):
    gain = gain_ref[...]
    values = own_ref[0:128, :].astype(F32)
    inverse = lax.rsqrt(jnp.mean(values * values, axis=-1, keepdims=True) + EPS)
    scaled = values * inverse
    ds = (keep_ref[...] + far_ref[...].astype(F32)) * gain
    inner = jnp.mean(ds * scaled, axis=-1, keepdims=True)
    result = (own_ref[128:256, :].astype(F32) + inverse * (ds - scaled * inner)).astype(BF)
    y = lax.axis_index("y")

    def source(i):
        return (i >> 4 & 1) * 64 + (i >> 1 & 7) * 8 + ((i >> 5) ^ y) * 2 + (i & 1)

    result = dot(chooser(128, 128, source), result).astype(BF)
    for k in range(Y):
        out_ref[k] = result[k * 32 : k * 32 + 32]


def two_rows(vec):
    high = vec.astype(BF).astype(F32)
    return jnp.concatenate([high, vec - high, jnp.zeros((6, vec.shape[1]), F32)], axis=0)


def two_blocks(rows):
    high = rows.astype(BF).astype(F32)
    return jnp.concatenate([high, rows - high], axis=0)


def merge_body(got_ref, hop_ref, b1_ref, b3_ref, out_ref):
    total = got_ref[0:2].astype(F32)
    for i in range(1, 16):
        total = total + got_ref[2 * i : 2 * i + 2].astype(F32)
    low, high = total[0, :128], total[1, :128]
    wide_low = jnp.concatenate([low[:64], low[64:]], axis=1)
    wide_high = jnp.concatenate([high[:64], high[64:]], axis=1)
    cols = jnp.concatenate(
        [piece[:, j * 64 : j * 64 + 64] for j in range(4) for piece in (wide_low, wide_high)],
        axis=1,
    )
    rows = weave(
        jnp.concatenate([low[i * 32 : i * 32 + 32] for i in range(4)], axis=1),
        jnp.concatenate([high[i * 32 : i * 32 + 32] for i in range(4)], axis=1),
    )
    out_ref[:, :512] = jnp.where(x_is_last(), rows, cols).astype(BF)
    pick = chooser(64, 64, lambda i: (i >> 1 & 3) * 16 + (i >> 3) * 2 + (i & 1))
    blocks = [hop_ref[0], b1_ref[...], hop_ref[2], b3_ref[...]]
    for f in range(2):
        rows = jnp.concatenate([block[f * 16 : f * 16 + 16] for block in blocks], axis=0)
        out_ref[:, 512 + f * 512 : 1024 + f * 512] = dot(pick, rows).astype(BF)
    gains = total[0, 128:] + total[1, 128:]
    gains = two_blocks(unpair(gains))
    out_ref[:, 1536:] = jnp.concatenate([gains] * ZL, axis=0).astype(BF)


def unpair(rows):
    return jnp.concatenate(
        [rows[2 * i : 2 * i + 1] + rows[2 * i + 1 : 2 * i + 2] for i in range(4)], axis=0
    )


def split_body(back_ref, hop_ref, rest_ref, last_ref):
    pick = chooser(64, 64, lambda i: (i >> 1 & 7) * 8 + (i >> 4) * 2 + (i & 1))
    for f in range(2):
        rows = dot(pick, back_ref[:, 512 + f * 512 : 1024 + f * 512]).astype(BF)
        hop_ref[f * 16 : f * 16 + 16] = rows[32:48]
        for at, k in enumerate((0, 1, 3)):
            row = at * 32 + f * 16
            rest_ref[row : row + 16] = rows[k * 16 : k * 16 + 16]
    sums = jnp.sum(back_ref[:, :512].astype(F32).reshape(ZL, 8, 512), axis=0)
    last_ref[:, :512] = sums.astype(BF)
    gains = jnp.sum(back_ref[:, 1536:].astype(F32).reshape(ZL, 8, 128), axis=0)
    last_ref[:, 512:] = two_blocks(gains[0:4] + gains[4:8]).astype(BF)


def pair_body(last_ref, far_ref, sent_ref):
    total = last_ref[...].astype(F32) + far_ref[...].astype(F32)
    grads = total[:, :512].astype(BF)
    gains = two_blocks(total[0:4, 512:] + total[4:8, 512:]).astype(BF)
    for x in range(X):
        sent_ref[x, :, :512] = grads
        sent_ref[x, :, 512:] = gains


def tokens_body(rest_ref, two_ref, out_ref):
    y = lax.axis_index("y")
    blocks = jnp.concatenate([rest_ref[0:64], two_ref[...], rest_ref[64:96]], axis=0)

    def source(i):
        return ((i & 3) ^ y) * 32 + (i >> 5 & 1) * 16 + (i >> 2 & 7) * 2 + (i >> 6)

    out_ref[...] = dot(chooser(128, 128, source), blocks).astype(BF)


def end_body(got_ref, qkv_ref, out_ref, gain_ref):
    for x in range(3):
        qkv_ref[:, x * 512 : x * 512 + 512] = got_ref[x, :, :512].astype(F32)
    out_ref[...] = got_ref[3, :, :512].astype(F32)
    gain = got_ref[0, :, 512:].astype(F32)
    gain_ref[...] = gain[0:4] + gain[4:8]


def on_device(tokens, grad_out, gain, w_qkv, w_out):
    row = gain.reshape(1, 512)
    plane = ("x", "y", "c")

    hbm = pl.BlockSpec(memory_space=pl.ANY)
    packed = pl.pallas_call(
        pack_body,
        out_shape=jax.ShapeDtypeStruct((256, 640), BF),
        in_specs=[hbm] * 4,
        out_specs=pl.BlockSpec(memory_space=pltpu.VMEM),
        scratch_shapes=[
            pltpu.VMEM((256, 512), BF),
            pltpu.VMEM((8, 1536), BF),
            pltpu.VMEM((8, 512), BF),
            pltpu.SemaphoreType.DMA((4,)),
        ],
        compiler_params=pltpu.CompilerParams(vmem_limit_bytes=60 * 2**20),
    )(tokens.reshape(128, 512), grad_out.reshape(128, 512), w_qkv, w_out)
    moved = exchange(packed.reshape(ZL * Y, 8, 640), ("zl", "y")).reshape(256, 640)
    [sent] = call(
        weights_body,
        [((32, 128, 128), BF)],
        moved,
        first_in_hbm=True,
        scratch=[pltpu.VMEM((2, 128, 128), BF), pltpu.SemaphoreType.DMA((X * Y,))],
    )
    weights = exchange(sent, plane)
    [own] = call(rows_body, [((256, 512), BF)], moved)
    far = lax.ppermute(own, "c", SWAP)
    scaled, normed, flipped, grads = call(
        norm_body,
        [((256, 512), F32), ((256, 512), BF), ((512, 256), BF), ((256, 512), BF)],
        own, far, row,
    )
    parts, send, keep = call(
        main_body,
        [((32, 136, 128), BF), ((128, 512), BF), ((128, 512), F32)],
        scaled, normed, flipped, grads, weights,
        first_in_hbm=True,
        scratch=[pltpu.VMEM((32, 136, 128), BF), pltpu.SemaphoreType.DMA((4,))],
    )
    got = exchange(parts, plane)
    dn_far = lax.ppermute(send, "c", SWAP)
    [hop] = call(finish_body, [((Y, 32, 512), BF)], own, keep, dn_far, row)
    [sent] = call(merge_body, [((64, 1664), BF)], got, hop, to_y(hop[1], 1), to_y(hop[3], 3))
    back = exchange(sent.reshape(ZL, 8, 1664), "zl").reshape(64, 1664)
    hop, rest, last = call(
        split_body, [((32, 512), BF), ((96, 512), BF), ((8, 640), BF)], back
    )
    last_far = lax.ppermute(last, "zh", SWAP)
    [grad_tokens] = call(tokens_body, [((128, 512), BF)], rest, to_y(hop, 2))
    [sent] = call(pair_body, [((X, 8, 640), BF)], last, last_far)
    ends = exchange(sent, "x")
    shard_qkv, shard_out, total = call(
        end_body, [((8, 1536), F32), ((8, 512), F32), ((4, 128), F32)], ends
    )
    return grad_tokens.reshape(1, 2, 64, 512), shard_qkv, shard_out, total.reshape(512)


def solution(mesh):
    inner = Mesh(mesh.devices.reshape(ZH, X, ZL, Y, C), ("zh", "x", "zl", "y", "c"))
    grid = ("zl", "y", "c")
    tok = P(("zh", "x"), grid, None, None)
    return jax.shard_map(
        on_device,
        mesh=inner,
        in_specs=(tok, tok, P(), P(grid, None), P(grid, None)),
        out_specs=(tok, P(grid, None), P(grid, None), P()),
        check_vma=False,
    )
```

```python
import jax
import jax.numpy as jnp
from jax import lax
from jax.experimental import pallas as pl
from jax.experimental.pallas import tpu as pltpu
from jax.sharding import Mesh
from jax.sharding import PartitionSpec as P

EPS = 1e-06
BF = jnp.bfloat16
F32 = jnp.float32

ZH, X, ZL, Y, C = 2, 4, 8, 4, 2
SWAP = [(0, 1), (1, 0)]


def exchange(arr, axes):
    return lax.all_to_all(arr, axes, split_axis=0, concat_axis=0, tiled=True)


def to_y(block, k):
    return lax.ppermute(block, "y", [(i, i ^ k) for i in range(Y)])


def call(body, outs, *args, first_in_hbm=False, scratch=()):
    vmem = pl.BlockSpec(memory_space=pltpu.VMEM)
    out_specs = [vmem] * len(outs)
    if first_in_hbm:
        out_specs[0] = pl.BlockSpec(memory_space=pl.ANY)
    return pl.pallas_call(
        body,
        out_shape=[jax.ShapeDtypeStruct(shape, kind) for shape, kind in outs],
        in_specs=[vmem] * len(args),
        out_specs=out_specs,
        scratch_shapes=list(scratch),
        compiler_params=pltpu.CompilerParams(vmem_limit_bytes=40 * 2**20),
    )(*args)


def dot(a, b, ca=1, cb=0):
    return lax.dot_general(a, b, (((ca,), (cb,)), ((), ())), preferred_element_type=F32)


def chooser(rows, cols, source_of):
    row = lax.broadcasted_iota(jnp.int32, (rows, cols), 0)
    col = lax.broadcasted_iota(jnp.int32, (rows, cols), 1)
    return (col == source_of(row)).astype(F32).astype(BF)


def pack_body(
    tok_ref, grad_ref, wq_ref, wo_ref, out_ref, both_vm, wq_vm, wo_vm, sems
):
    copies = [
        pltpu.make_async_copy(src, dst, sems.at[i])
        for i, (src, dst) in enumerate(
            [
                (tok_ref, both_vm.at[0:128]),
                (grad_ref, both_vm.at[128:256]),
                (wq_ref, wq_vm),
                (wo_ref, wo_vm),
            ]
        )
    ]
    for copy in copies:
        copy.start()
    pick = chooser(
        256, 256, lambda i: (i >> 2 & 1) * 128 + (i & 1) * 64 + (i >> 1 & 1) * 32 + (i >> 3)
    )
    copies[2].wait()
    copies[3].wait()
    x = lax.axis_index("x")
    part = wo_vm[...].astype(F32)
    for i in range(3):
        part = jnp.where(x == i, wq_vm[:, i * 512 : i * 512 + 512].astype(F32), part)
    blocks = jnp.concatenate([part[:, y * 128 : y * 128 + 128] for y in range(Y)], axis=0)
    out_ref[:, 512:] = jnp.concatenate([blocks] * ZL, axis=0).astype(BF)
    copies[0].wait()
    copies[1].wait()
    out_ref[:, :512] = dot(pick, both_vm[...]).astype(BF)


def halves(arr):
    return arr[:, :64], arr[:, 64:]


def weights_body(moved_ref, sent_ref, pair_vm, sems):
    block = moved_ref[:, 512:].astype(F32)
    (low0, low1), (high0, high1) = halves(block[:128]), halves(block[128:])
    planes = block.reshape(4, 2, 32, 128)
    outs = x_is_last()
    for core, cols in ((0, (low0, high0)), (1, (low1, high1))):
        mine = jnp.where(
            outs, planes[:, core].reshape(128, 128), jnp.concatenate(cols, axis=1)
        ).astype(BF)
        pair_vm[core] = mine
    copies = [
        pltpu.make_async_copy(pair_vm, sent_ref.at[2 * xy : 2 * xy + 2], sems.at[xy])
        for xy in range(X * Y)
    ]
    for copy in copies:
        copy.start()
    for copy in copies:
        copy.wait()


def rows_body(moved_ref, own_ref):
    pick = chooser(
        256, 256, lambda i: (i >> 1 & 31) * 8 + (i >> 7) * 4 + (i >> 6 & 1) * 2 + (i & 1)
    )
    own_ref[...] = dot(pick, moved_ref[:, :512]).astype(BF)


def norm_body(own_ref, far_ref, gain_ref, scaled_ref, normed_ref, flipped_ref, grad_ref):
    own, far = own_ref[...], far_ref[...]
    x_in = jnp.concatenate([own[0:64], far[0:64], own[64:128], far[64:128]], axis=0)
    grad_ref[...] = jnp.concatenate([own[128:192], far[128:192], own[192:], far[192:]], axis=0)
    values = x_in.astype(F32)
    inverse = lax.rsqrt(jnp.mean(values * values, axis=-1, keepdims=True) + EPS)
    scaled = values * inverse
    scaled_ref[...] = scaled
    normed = scaled * gain_ref[...]
    normed_ref[...] = normed.astype(BF)
    flipped_ref[...] = normed.T.astype(BF)


def x_is_last():
    return lax.axis_index("x") == 3


def weave(first, second):
    rows, cols = first.shape
    blocks = [arr.reshape(rows // 8, 1, 8, cols) for arr in (first, second)]
    return jnp.concatenate(blocks, axis=1).reshape(2 * rows, cols)


def main_body(
    scaled_ref, normed_ref, flipped_ref, grad_ref, w_ref,
    parts_ref, send_ref, keep_ref, parts_vm, sems,
):
    lanes = []
    for x in range(3):
        for pair in range(2):
            tops, bots = [], []
            for core in range(2):
                at = x * 8 + pair * 4 + core
                (a0, a1), (b0, b1) = (
                    halves(w_ref[at].astype(F32)),
                    halves(w_ref[at + 2].astype(F32)),
                )
                tops.append(jnp.concatenate([a0, b0], axis=1))
                bots.append(jnp.concatenate([a1, b1], axis=1))
            lanes.append(jnp.concatenate([weave(*tops), weave(*bots)], axis=0).astype(BF))
    wh = jnp.concatenate(lanes, axis=1)
    lanes = [
        weave(w_ref[24 + 2 * y].astype(F32), w_ref[25 + 2 * y].astype(F32)).astype(BF)
        for y in range(Y)
    ]
    wo = jnp.concatenate(lanes, axis=1)

    normed, g_in = normed_ref[...], grad_ref[...]
    qkv = dot(normed, wh).astype(BF)
    ups = dot(g_in, wo, 1, 1).astype(BF)

    lane = lax.broadcasted_iota(jnp.int32, (128, 128), 1)
    first = lane < 64
    zero = jnp.zeros((128, 128), BF)

    def stack(arr):
        return jnp.concatenate([jnp.where(first, arr, zero), jnp.where(first, zero, arr)], axis=0)

    def pile(arr):
        return jnp.concatenate([arr[:, :128], arr[:, 128:]], axis=0)

    def frames(items):
        return [
            jnp.concatenate([items[0], items[2]], axis=0),
            jnp.concatenate([items[1], items[3]], axis=0),
        ]

    copies = []

    def leave(part, messages):
        for yc in range(8):
            parts_vm[part * 8 + yc] = messages(yc).astype(BF)
        at = slice(part * 8, part * 8 + 8)
        copy = pltpu.make_async_copy(parts_vm.at[at], parts_ref.at[at], sems.at[part])
        copy.start()
        copies.append(copy)

    def leave_columns(part, columns, tail):
        grads = dot(flipped, columns).reshape(ZL, Y, 2, 8, 256)

        def message(yc):
            block = grads[:, yc // 2, yc % 2].reshape(64, 256)
            return jnp.concatenate([block[:, :128], block[:, 128:], tail], axis=0)

        leave(part, message)

    flipped = flipped_ref[...]
    none = jnp.zeros((8, 128), F32)
    atts, dvs, dscores, sides = [], [], [], []
    for f in range(2):
        rows = slice(f * 128, (f + 1) * 128)
        for pair in range(2):
            at = pair * 128
            q = qkv[rows, at : at + 128]
            k2 = stack(qkv[rows, 256 + at : 256 + at + 128])
            v2 = stack(qkv[rows, 512 + at : 512 + at + 128])
            u = ups[rows, at : at + 128]
            scores = dot(q, k2, 1, 1) * 0.125
            dprob = dot(u, v2, 1, 1)
            weights, scored = [], []
            for head in range(2):
                cols = slice(head * 128, (head + 1) * 128)
                s = scores[:, cols]
                expo = jnp.exp(s - jnp.max(s, axis=-1, keepdims=True))
                probs = expo * (1.0 / jnp.sum(expo, axis=-1, keepdims=True))
                dp = dprob[:, cols]
                weights.append(probs.astype(BF))
                inner = jnp.sum(probs * dp, axis=-1, keepdims=True)
                scored.append((probs * (dp - inner) * 0.125).astype(BF))
            weight = jnp.concatenate(weights, axis=1)
            atts.append(dot(weight, v2).astype(BF))
            dvs.append(dot(pile(weight), stack(u), 0, 0).astype(BF))
            dscores.append(jnp.concatenate(scored, axis=1))
            sides.append((q, k2))

    att = jnp.concatenate(frames(atts), axis=1)
    g_out = dot(att, g_in, 0, 0).reshape(4, Y, 2, 8, 512)

    def out_message(yc):
        block = g_out[:, yc // 2, yc % 2].reshape(32, 512)
        pieces = [block[:, i * 128 : i * 128 + 128] for i in range(4)]
        return jnp.concatenate(pieces + [none], axis=0)

    leave(3, out_message)
    dv = jnp.concatenate(frames(dvs), axis=1)
    leave_columns(2, dv, none)

    dq = [dot(dscore, k2).astype(BF) for dscore, (q, k2) in zip(dscores, sides)]
    dk = [dot(pile(dscore), stack(q), 0, 0).astype(BF) for dscore, (q, k2) in zip(dscores, sides)]
    dq = jnp.concatenate(frames(dq), axis=1)
    dk = jnp.concatenate(frames(dk), axis=1)
    leave_columns(1, dk, none)
    dn = dot(jnp.concatenate([dq, dk, dv], axis=1), wh, 1, 1)
    gg = two_rows(jnp.sum(dn * scaled_ref[...], axis=0, keepdims=True))
    gg = jnp.concatenate([gg[0:2, i * 128 : i * 128 + 128] for i in range(4)], axis=0)
    leave_columns(0, dq, gg)
    keep_ref[...] = jnp.concatenate([dn[0:64], dn[128:192]], axis=0)
    send_ref[...] = jnp.concatenate([dn[64:128], dn[192:]], axis=0).astype(BF)
    for copy in copies:
        copy.wait()


def finish_body(own_ref, keep_ref, far_ref, gain_ref, out_ref):
    gain = gain_ref[...]
    values = own_ref[0:128, :].astype(F32)
    inverse = lax.rsqrt(jnp.mean(values * values, axis=-1, keepdims=True) + EPS)
    scaled = values * inverse
    ds = (keep_ref[...] + far_ref[...].astype(F32)) * gain
    inner = jnp.mean(ds * scaled, axis=-1, keepdims=True)
    result = (own_ref[128:256, :].astype(F32) + inverse * (ds - scaled * inner)).astype(BF)
    y = lax.axis_index("y")

    def source(i):
        return (i >> 4 & 1) * 64 + (i >> 1 & 7) * 8 + ((i >> 5) ^ y) * 2 + (i & 1)

    result = dot(chooser(128, 128, source), result).astype(BF)
    for k in range(Y):
        out_ref[k] = result[k * 32 : k * 32 + 32]


def two_rows(vec):
    high = vec.astype(BF).astype(F32)
    return jnp.concatenate([high, vec - high, jnp.zeros((6, vec.shape[1]), F32)], axis=0)


def two_blocks(rows):
    high = rows.astype(BF).astype(F32)
    return jnp.concatenate([high, rows - high], axis=0)


def merge_body(got_ref, hop_ref, b1_ref, b3_ref, out_ref):
    total = got_ref[0:2].astype(F32)
    for i in range(1, 16):
        total = total + got_ref[2 * i : 2 * i + 2].astype(F32)
    low, high = total[0, :128], total[1, :128]
    wide_low = jnp.concatenate([low[:64], low[64:]], axis=1)
    wide_high = jnp.concatenate([high[:64], high[64:]], axis=1)
    cols = jnp.concatenate(
        [piece[:, j * 64 : j * 64 + 64] for j in range(4) for piece in (wide_low, wide_high)],
        axis=1,
    )
    rows = weave(
        jnp.concatenate([low[i * 32 : i * 32 + 32] for i in range(4)], axis=1),
        jnp.concatenate([high[i * 32 : i * 32 + 32] for i in range(4)], axis=1),
    )
    out_ref[:, :512] = jnp.where(x_is_last(), rows, cols).astype(BF)
    pick = chooser(64, 64, lambda i: (i >> 1 & 3) * 16 + (i >> 3) * 2 + (i & 1))
    blocks = [hop_ref[0], b1_ref[...], hop_ref[2], b3_ref[...]]
    for f in range(2):
        rows = jnp.concatenate([block[f * 16 : f * 16 + 16] for block in blocks], axis=0)
        out_ref[:, 512 + f * 512 : 1024 + f * 512] = dot(pick, rows).astype(BF)
    gains = total[0, 128:] + total[1, 128:]
    gains = two_blocks(unpair(gains))
    out_ref[:, 1536:] = jnp.concatenate([gains] * ZL, axis=0).astype(BF)


def unpair(rows):
    return jnp.concatenate(
        [rows[2 * i : 2 * i + 1] + rows[2 * i + 1 : 2 * i + 2] for i in range(4)], axis=0
    )


def split_body(back_ref, hop_ref, rest_ref, last_ref):
    pick = chooser(64, 64, lambda i: (i >> 1 & 7) * 8 + (i >> 4) * 2 + (i & 1))
    for f in range(2):
        rows = dot(pick, back_ref[:, 512 + f * 512 : 1024 + f * 512]).astype(BF)
        hop_ref[f * 16 : f * 16 + 16] = rows[32:48]
        for at, k in enumerate((0, 1, 3)):
            row = at * 32 + f * 16
            rest_ref[row : row + 16] = rows[k * 16 : k * 16 + 16]
    sums = jnp.sum(back_ref[:, :512].astype(F32).reshape(ZL, 8, 512), axis=0)
    last_ref[:, :512] = sums.astype(BF)
    gains = jnp.sum(back_ref[:, 1536:].astype(F32).reshape(ZL, 8, 128), axis=0)
    last_ref[:, 512:] = two_blocks(gains[0:4] + gains[4:8]).astype(BF)


def pair_body(last_ref, far_ref, sent_ref):
    total = last_ref[...].astype(F32) + far_ref[...].astype(F32)
    grads = total[:, :512].astype(BF)
    gains = two_blocks(total[0:4, 512:] + total[4:8, 512:]).astype(BF)
    for x in range(X):
        sent_ref[x, :, :512] = grads
        sent_ref[x, :, 512:] = gains


def tokens_body(rest_ref, two_ref, out_ref):
    y = lax.axis_index("y")
    blocks = jnp.concatenate([rest_ref[0:64], two_ref[...], rest_ref[64:96]], axis=0)

    def source(i):
        return ((i & 3) ^ y) * 32 + (i >> 5 & 1) * 16 + (i >> 2 & 7) * 2 + (i >> 6)

    out_ref[...] = dot(chooser(128, 128, source), blocks).astype(BF)


def end_body(got_ref, qkv_ref, out_ref, gain_ref):
    for x in range(3):
        qkv_ref[:, x * 512 : x * 512 + 512] = got_ref[x, :, :512].astype(F32)
    out_ref[...] = got_ref[3, :, :512].astype(F32)
    gain = got_ref[0, :, 512:].astype(F32)
    gain_ref[...] = gain[0:4] + gain[4:8]


def on_device(tokens, grad_out, gain, w_qkv, w_out):
    row = gain.reshape(1, 512)
    plane = ("x", "y", "c")

    hbm = pl.BlockSpec(memory_space=pl.ANY)
    packed = pl.pallas_call(
        pack_body,
        out_shape=jax.ShapeDtypeStruct((256, 640), BF),
        in_specs=[hbm] * 4,
        out_specs=pl.BlockSpec(memory_space=pltpu.VMEM),
        scratch_shapes=[
            pltpu.VMEM((256, 512), BF),
            pltpu.VMEM((8, 1536), BF),
            pltpu.VMEM((8, 512), BF),
            pltpu.SemaphoreType.DMA((4,)),
        ],
        compiler_params=pltpu.CompilerParams(vmem_limit_bytes=60 * 2**20),
    )(tokens.reshape(128, 512), grad_out.reshape(128, 512), w_qkv, w_out)
    moved = exchange(packed.reshape(ZL * Y, 8, 640), ("zl", "y")).reshape(256, 640)
    [sent] = call(
        weights_body,
        [((32, 128, 128), BF)],
        moved,
        first_in_hbm=True,
        scratch=[pltpu.VMEM((2, 128, 128), BF), pltpu.SemaphoreType.DMA((X * Y,))],
    )
    weights = exchange(sent, plane)
    [own] = call(rows_body, [((256, 512), BF)], moved)
    far = lax.ppermute(own, "c", SWAP)
    scaled, normed, flipped, grads = call(
        norm_body,
        [((256, 512), F32), ((256, 512), BF), ((512, 256), BF), ((256, 512), BF)],
        own, far, row,
    )
    parts, send, keep = call(
        main_body,
        [((32, 136, 128), BF), ((128, 512), BF), ((128, 512), F32)],
        scaled, normed, flipped, grads, weights,
        first_in_hbm=True,
        scratch=[pltpu.VMEM((32, 136, 128), BF), pltpu.SemaphoreType.DMA((4,))],
    )
    got = exchange(parts, plane)
    dn_far = lax.ppermute(send, "c", SWAP)
    [hop] = call(finish_body, [((Y, 32, 512), BF)], own, keep, dn_far, row)
    [sent] = call(merge_body, [((64, 1664), BF)], got, hop, to_y(hop[1], 1), to_y(hop[3], 3))
    back = exchange(sent.reshape(ZL, 8, 1664), "zl").reshape(64, 1664)
    hop, rest, last = call(
        split_body, [((32, 512), BF), ((96, 512), BF), ((8, 640), BF)], back
    )
    last_far = lax.ppermute(last, "zh", SWAP)
    [grad_tokens] = call(tokens_body, [((128, 512), BF)], rest, to_y(hop, 2))
    [sent] = call(pair_body, [((X, 8, 640), BF)], last, last_far)
    ends = exchange(sent, "x")
    shard_qkv, shard_out, total = call(
        end_body, [((8, 1536), F32), ((8, 512), F32), ((4, 128), F32)], ends
    )
    return grad_tokens.reshape(1, 2, 64, 512), shard_qkv, shard_out, total.reshape(512)


def solution(mesh):
    inner = Mesh(mesh.devices.reshape(ZH, X, ZL, Y, C), ("zh", "x", "zl", "y", "c"))
    grid = ("zl", "y", "c")
    tok = P(("zh", "x"), grid, None, None)
    return jax.shard_map(
        on_device,
        mesh=inner,
        in_specs=(tok, tok, P(), P(grid, None), P(grid, None)),
        out_specs=(tok, P(grid, None), P(grid, None), P()),
        check_vma=False,
    )
```

```python
import jax
import jax.numpy as jnp
from jax import lax
from jax.experimental import pallas as pl
from jax.experimental.pallas import tpu as pltpu
from jax.sharding import Mesh
from jax.sharding import PartitionSpec as P

EPS = 1e-06
BF = jnp.bfloat16
F32 = jnp.float32

ZH, X, ZL, Y, C = 2, 4, 8, 4, 2
SWAP = [(0, 1), (1, 0)]


def exchange(arr, axes):
    return lax.all_to_all(arr, axes, split_axis=0, concat_axis=0, tiled=True)


def to_y(block, k):
    return lax.ppermute(block, "y", [(i, i ^ k) for i in range(Y)])


def call(body, outs, *args, first_in_hbm=False, scratch=()):
    vmem = pl.BlockSpec(memory_space=pltpu.VMEM)
    out_specs = [vmem] * len(outs)
    if first_in_hbm:
        out_specs[0] = pl.BlockSpec(memory_space=pl.ANY)
    return pl.pallas_call(
        body,
        out_shape=[jax.ShapeDtypeStruct(shape, kind) for shape, kind in outs],
        in_specs=[vmem] * len(args),
        out_specs=out_specs,
        scratch_shapes=list(scratch),
        compiler_params=pltpu.CompilerParams(vmem_limit_bytes=40 * 2**20),
    )(*args)


def dot(a, b, ca=1, cb=0):
    return lax.dot_general(a, b, (((ca,), (cb,)), ((), ())), preferred_element_type=F32)


def chooser(rows, cols, source_of):
    row = lax.broadcasted_iota(jnp.int32, (rows, cols), 0)
    col = lax.broadcasted_iota(jnp.int32, (rows, cols), 1)
    return (col == source_of(row)).astype(F32).astype(BF)


def pack_body(
    tok_ref, grad_ref, wq_ref, wo_ref, out_ref, both_vm, wq_vm, wo_vm, sems
):
    copies = [
        pltpu.make_async_copy(src, dst, sems.at[i])
        for i, (src, dst) in enumerate(
            [
                (tok_ref, both_vm.at[0:128]),
                (grad_ref, both_vm.at[128:256]),
                (wq_ref, wq_vm),
                (wo_ref, wo_vm),
            ]
        )
    ]
    for copy in copies:
        copy.start()
    pick = chooser(
        256, 256, lambda i: (i >> 2 & 1) * 128 + (i & 1) * 64 + (i >> 1 & 1) * 32 + (i >> 3)
    )
    copies[2].wait()
    copies[3].wait()
    x = lax.axis_index("x")
    part = wo_vm[...].astype(F32)
    for i in range(3):
        part = jnp.where(x == i, wq_vm[:, i * 512 : i * 512 + 512].astype(F32), part)
    blocks = jnp.concatenate([part[:, y * 128 : y * 128 + 128] for y in range(Y)], axis=0)
    out_ref[:, 512:] = jnp.concatenate([blocks] * ZL, axis=0).astype(BF)
    copies[0].wait()
    copies[1].wait()
    out_ref[:, :512] = dot(pick, both_vm[...]).astype(BF)


def halves(arr):
    return arr[:, :64], arr[:, 64:]


def weights_body(moved_ref, sent_ref, pair_vm, sems):
    block = moved_ref[:, 512:].astype(F32)
    (low0, low1), (high0, high1) = halves(block[:128]), halves(block[128:])
    planes = block.reshape(4, 2, 32, 128)
    outs = x_is_last()
    copies = []
    for core, cols in ((0, (low0, high0)), (1, (low1, high1))):
        mine = jnp.where(
            outs, planes[:, core].reshape(128, 128), jnp.concatenate(cols, axis=1)
        ).astype(BF)
        pair_vm[core] = mine
        for xy in range(X * Y):
            at = 2 * xy + core
            copy = pltpu.make_async_copy(pair_vm.at[core], sent_ref.at[at], sems.at[at])
            copy.start()
            copies.append(copy)
    for copy in copies:
        copy.wait()


def rows_body(moved_ref, own_ref):
    pick = chooser(
        256, 256, lambda i: (i >> 1 & 31) * 8 + (i >> 7) * 4 + (i >> 6 & 1) * 2 + (i & 1)
    )
    own_ref[...] = dot(pick, moved_ref[:, :512]).astype(BF)


def norm_body(own_ref, far_ref, gain_ref, scaled_ref, normed_ref, flipped_ref, grad_ref):
    own, far = own_ref[...], far_ref[...]
    x_in = jnp.concatenate([own[0:64], far[0:64], own[64:128], far[64:128]], axis=0)
    grad_ref[...] = jnp.concatenate([own[128:192], far[128:192], own[192:], far[192:]], axis=0)
    values = x_in.astype(F32)
    inverse = lax.rsqrt(jnp.mean(values * values, axis=-1, keepdims=True) + EPS)
    scaled = values * inverse
    scaled_ref[...] = scaled
    normed = scaled * gain_ref[...]
    normed_ref[...] = normed.astype(BF)
    flipped_ref[...] = normed.T.astype(BF)


def x_is_last():
    return lax.axis_index("x") == 3


def weave(first, second):
    rows, cols = first.shape
    blocks = [arr.reshape(rows // 8, 1, 8, cols) for arr in (first, second)]
    return jnp.concatenate(blocks, axis=1).reshape(2 * rows, cols)


def main_body(
    scaled_ref, normed_ref, flipped_ref, grad_ref, w_ref,
    parts_ref, send_ref, keep_ref, parts_vm, sems,
):
    lanes = []
    for x in range(3):
        for pair in range(2):
            tops, bots = [], []
            for core in range(2):
                at = x * 8 + pair * 4 + core
                (a0, a1), (b0, b1) = (
                    halves(w_ref[at].astype(F32)),
                    halves(w_ref[at + 2].astype(F32)),
                )
                tops.append(jnp.concatenate([a0, b0], axis=1))
                bots.append(jnp.concatenate([a1, b1], axis=1))
            lanes.append(jnp.concatenate([weave(*tops), weave(*bots)], axis=0).astype(BF))
    wh = jnp.concatenate(lanes, axis=1)
    lanes = [
        weave(w_ref[24 + 2 * y].astype(F32), w_ref[25 + 2 * y].astype(F32)).astype(BF)
        for y in range(Y)
    ]
    wo = jnp.concatenate(lanes, axis=1)

    normed, g_in = normed_ref[...], grad_ref[...]
    qkv = dot(normed, wh).astype(BF)
    ups = dot(g_in, wo, 1, 1).astype(BF)

    lane = lax.broadcasted_iota(jnp.int32, (128, 128), 1)
    first = lane < 64
    zero = jnp.zeros((128, 128), BF)

    def stack(arr):
        return jnp.concatenate([jnp.where(first, arr, zero), jnp.where(first, zero, arr)], axis=0)

    def pile(arr):
        return jnp.concatenate([arr[:, :128], arr[:, 128:]], axis=0)

    def frames(items):
        return [
            jnp.concatenate([items[0], items[2]], axis=0),
            jnp.concatenate([items[1], items[3]], axis=0),
        ]

    copies = []

    def leave(part, messages):
        for yc in range(8):
            parts_vm[part * 8 + yc] = messages(yc).astype(BF)
        at = slice(part * 8, part * 8 + 8)
        copy = pltpu.make_async_copy(parts_vm.at[at], parts_ref.at[at], sems.at[part])
        copy.start()
        copies.append(copy)

    def leave_columns(part, columns, tail):
        grads = dot(flipped, columns).reshape(ZL, Y, 2, 8, 256)

        def message(yc):
            block = grads[:, yc // 2, yc % 2].reshape(64, 256)
            return jnp.concatenate([block[:, :128], block[:, 128:], tail], axis=0)

        leave(part, message)

    flipped = flipped_ref[...]
    none = jnp.zeros((8, 128), F32)
    atts, dvs, dscores, sides = [], [], [], []
    for f in range(2):
        rows = slice(f * 128, (f + 1) * 128)
        for pair in range(2):
            at = pair * 128
            q = qkv[rows, at : at + 128]
            k2 = stack(qkv[rows, 256 + at : 256 + at + 128])
            v2 = stack(qkv[rows, 512 + at : 512 + at + 128])
            u = ups[rows, at : at + 128]
            scores = dot(q, k2, 1, 1) * 0.125
            dprob = dot(u, v2, 1, 1)
            weights, scored = [], []
            for head in range(2):
                cols = slice(head * 128, (head + 1) * 128)
                s = scores[:, cols]
                expo = jnp.exp(s - jnp.max(s, axis=-1, keepdims=True))
                probs = expo * (1.0 / jnp.sum(expo, axis=-1, keepdims=True))
                dp = dprob[:, cols]
                weights.append(probs.astype(BF))
                inner = jnp.sum(probs * dp, axis=-1, keepdims=True)
                scored.append((probs * (dp - inner) * 0.125).astype(BF))
            weight = jnp.concatenate(weights, axis=1)
            atts.append(dot(weight, v2).astype(BF))
            dvs.append(dot(pile(weight), stack(u), 0, 0).astype(BF))
            dscores.append(jnp.concatenate(scored, axis=1))
            sides.append((q, k2))

    att = jnp.concatenate(frames(atts), axis=1)
    g_out = dot(att, g_in, 0, 0).reshape(4, Y, 2, 8, 512)

    def out_message(yc):
        block = g_out[:, yc // 2, yc % 2].reshape(32, 512)
        pieces = [block[:, i * 128 : i * 128 + 128] for i in range(4)]
        return jnp.concatenate(pieces + [none], axis=0)

    leave(3, out_message)
    dv = jnp.concatenate(frames(dvs), axis=1)
    leave_columns(2, dv, none)

    dq = [dot(dscore, k2).astype(BF) for dscore, (q, k2) in zip(dscores, sides)]
    dk = [dot(pile(dscore), stack(q), 0, 0).astype(BF) for dscore, (q, k2) in zip(dscores, sides)]
    dq = jnp.concatenate(frames(dq), axis=1)
    dk = jnp.concatenate(frames(dk), axis=1)
    leave_columns(1, dk, none)
    dn = dot(jnp.concatenate([dq, dk, dv], axis=1), wh, 1, 1)
    gg = two_rows(jnp.sum(dn * scaled_ref[...], axis=0, keepdims=True))
    gg = jnp.concatenate([gg[0:2, i * 128 : i * 128 + 128] for i in range(4)], axis=0)
    leave_columns(0, dq, gg)
    keep_ref[...] = jnp.concatenate([dn[0:64], dn[128:192]], axis=0)
    send_ref[...] = jnp.concatenate([dn[64:128], dn[192:]], axis=0).astype(BF)
    for copy in copies:
        copy.wait()


def finish_body(own_ref, keep_ref, far_ref, gain_ref, out_ref):
    gain = gain_ref[...]
    values = own_ref[0:128, :].astype(F32)
    inverse = lax.rsqrt(jnp.mean(values * values, axis=-1, keepdims=True) + EPS)
    scaled = values * inverse
    ds = (keep_ref[...] + far_ref[...].astype(F32)) * gain
    inner = jnp.mean(ds * scaled, axis=-1, keepdims=True)
    result = (own_ref[128:256, :].astype(F32) + inverse * (ds - scaled * inner)).astype(BF)
    y = lax.axis_index("y")

    def source(i):
        return (i >> 4 & 1) * 64 + (i >> 1 & 7) * 8 + ((i >> 5) ^ y) * 2 + (i & 1)

    result = dot(chooser(128, 128, source), result).astype(BF)
    for k in range(Y):
        out_ref[k] = result[k * 32 : k * 32 + 32]


def two_rows(vec):
    high = vec.astype(BF).astype(F32)
    return jnp.concatenate([high, vec - high, jnp.zeros((6, vec.shape[1]), F32)], axis=0)


def two_blocks(rows):
    high = rows.astype(BF).astype(F32)
    return jnp.concatenate([high, rows - high], axis=0)


def merge_body(got_ref, hop_ref, b1_ref, b3_ref, out_ref):
    total = got_ref[0:2].astype(F32)
    for i in range(1, 16):
        total = total + got_ref[2 * i : 2 * i + 2].astype(F32)
    low, high = total[0, :128], total[1, :128]
    wide_low = jnp.concatenate([low[:64], low[64:]], axis=1)
    wide_high = jnp.concatenate([high[:64], high[64:]], axis=1)
    cols = jnp.concatenate(
        [piece[:, j * 64 : j * 64 + 64] for j in range(4) for piece in (wide_low, wide_high)],
        axis=1,
    )
    rows = weave(
        jnp.concatenate([low[i * 32 : i * 32 + 32] for i in range(4)], axis=1),
        jnp.concatenate([high[i * 32 : i * 32 + 32] for i in range(4)], axis=1),
    )
    out_ref[:, :512] = jnp.where(x_is_last(), rows, cols).astype(BF)
    pick = chooser(64, 64, lambda i: (i >> 1 & 3) * 16 + (i >> 3) * 2 + (i & 1))
    blocks = [hop_ref[0], b1_ref[...], hop_ref[2], b3_ref[...]]
    for f in range(2):
        rows = jnp.concatenate([block[f * 16 : f * 16 + 16] for block in blocks], axis=0)
        out_ref[:, 512 + f * 512 : 1024 + f * 512] = dot(pick, rows).astype(BF)
    gains = total[0, 128:] + total[1, 128:]
    gains = two_blocks(unpair(gains))
    out_ref[:, 1536:] = jnp.concatenate([gains] * ZL, axis=0).astype(BF)


def unpair(rows):
    return jnp.concatenate(
        [rows[2 * i : 2 * i + 1] + rows[2 * i + 1 : 2 * i + 2] for i in range(4)], axis=0
    )


def split_body(back_ref, hop_ref, rest_ref, last_ref):
    pick = chooser(64, 64, lambda i: (i >> 1 & 7) * 8 + (i >> 4) * 2 + (i & 1))
    for f in range(2):
        rows = dot(pick, back_ref[:, 512 + f * 512 : 1024 + f * 512]).astype(BF)
        hop_ref[f * 16 : f * 16 + 16] = rows[32:48]
        for at, k in enumerate((0, 1, 3)):
            row = at * 32 + f * 16
            rest_ref[row : row + 16] = rows[k * 16 : k * 16 + 16]
    sums = jnp.sum(back_ref[:, :512].astype(F32).reshape(ZL, 8, 512), axis=0)
    last_ref[:, :512] = sums.astype(BF)
    gains = jnp.sum(back_ref[:, 1536:].astype(F32).reshape(ZL, 8, 128), axis=0)
    last_ref[:, 512:] = two_blocks(gains[0:4] + gains[4:8]).astype(BF)


def pair_body(last_ref, far_ref, sent_ref):
    total = last_ref[...].astype(F32) + far_ref[...].astype(F32)
    grads = total[:, :512].astype(BF)
    gains = two_blocks(total[0:4, 512:] + total[4:8, 512:]).astype(BF)
    for x in range(X):
        sent_ref[x, :, :512] = grads
        sent_ref[x, :, 512:] = gains


def tokens_body(rest_ref, two_ref, out_ref):
    y = lax.axis_index("y")
    blocks = jnp.concatenate([rest_ref[0:64], two_ref[...], rest_ref[64:96]], axis=0)

    def source(i):
        return ((i & 3) ^ y) * 32 + (i >> 5 & 1) * 16 + (i >> 2 & 7) * 2 + (i >> 6)

    out_ref[...] = dot(chooser(128, 128, source), blocks).astype(BF)


def end_body(got_ref, qkv_ref, out_ref, gain_ref):
    for x in range(3):
        qkv_ref[:, x * 512 : x * 512 + 512] = got_ref[x, :, :512].astype(F32)
    out_ref[...] = got_ref[3, :, :512].astype(F32)
    gain = got_ref[0, :, 512:].astype(F32)
    gain_ref[...] = gain[0:4] + gain[4:8]


def on_device(tokens, grad_out, gain, w_qkv, w_out):
    row = gain.reshape(1, 512)
    plane = ("x", "y", "c")

    hbm = pl.BlockSpec(memory_space=pl.ANY)
    packed = pl.pallas_call(
        pack_body,
        out_shape=jax.ShapeDtypeStruct((256, 640), BF),
        in_specs=[hbm] * 4,
        out_specs=pl.BlockSpec(memory_space=pltpu.VMEM),
        scratch_shapes=[
            pltpu.VMEM((256, 512), BF),
            pltpu.VMEM((8, 1536), BF),
            pltpu.VMEM((8, 512), BF),
            pltpu.SemaphoreType.DMA((4,)),
        ],
        compiler_params=pltpu.CompilerParams(vmem_limit_bytes=60 * 2**20),
    )(tokens.reshape(128, 512), grad_out.reshape(128, 512), w_qkv, w_out)
    moved = exchange(packed.reshape(ZL * Y, 8, 640), ("zl", "y")).reshape(256, 640)
    [sent] = call(
        weights_body,
        [((32, 128, 128), BF)],
        moved,
        first_in_hbm=True,
        scratch=[pltpu.VMEM((2, 128, 128), BF), pltpu.SemaphoreType.DMA((2 * X * Y,))],
    )
    weights = exchange(sent, plane)
    [own] = call(rows_body, [((256, 512), BF)], moved)
    far = lax.ppermute(own, "c", SWAP)
    scaled, normed, flipped, grads = call(
        norm_body,
        [((256, 512), F32), ((256, 512), BF), ((512, 256), BF), ((256, 512), BF)],
        own, far, row,
    )
    parts, send, keep = call(
        main_body,
        [((32, 136, 128), BF), ((128, 512), BF), ((128, 512), F32)],
        scaled, normed, flipped, grads, weights,
        first_in_hbm=True,
        scratch=[pltpu.VMEM((32, 136, 128), BF), pltpu.SemaphoreType.DMA((4,))],
    )
    got = exchange(parts, plane)
    dn_far = lax.ppermute(send, "c", SWAP)
    [hop] = call(finish_body, [((Y, 32, 512), BF)], own, keep, dn_far, row)
    [sent] = call(merge_body, [((64, 1664), BF)], got, hop, to_y(hop[1], 1), to_y(hop[3], 3))
    back = exchange(sent.reshape(ZL, 8, 1664), "zl").reshape(64, 1664)
    hop, rest, last = call(
        split_body, [((32, 512), BF), ((96, 512), BF), ((8, 640), BF)], back
    )
    last_far = lax.ppermute(last, "zh", SWAP)
    [grad_tokens] = call(tokens_body, [((128, 512), BF)], rest, to_y(hop, 2))
    [sent] = call(pair_body, [((X, 8, 640), BF)], last, last_far)
    ends = exchange(sent, "x")
    shard_qkv, shard_out, total = call(
        end_body, [((8, 1536), F32), ((8, 512), F32), ((4, 128), F32)], ends
    )
    return grad_tokens.reshape(1, 2, 64, 512), shard_qkv, shard_out, total.reshape(512)


def solution(mesh):
    inner = Mesh(mesh.devices.reshape(ZH, X, ZL, Y, C), ("zh", "x", "zl", "y", "c"))
    grid = ("zl", "y", "c")
    tok = P(("zh", "x"), grid, None, None)
    return jax.shard_map(
        on_device,
        mesh=inner,
        in_specs=(tok, tok, P(), P(grid, None), P(grid, None)),
        out_specs=(tok, P(grid, None), P(grid, None), P()),
        check_vma=False,
    )
```
